128 devices in a mesh: dp: 8 (over y, core), cent: 16 (over x, z).
Axes of the slice: x: 4, y: 4, z: 4, core: 2. Of those that a mesh axis runs over, the one named last changes fastest.
Arguments:
- points: bfloat16 [32768, 1024], P(('dp', 'cent')), may hold values from -8 to 8
- assign: int32 [32768], P(('dp', 'cent')), may hold values from 0 to 65535, as said below
- parent_one: int32 [65536], P('cent'), may hold values from 0 to 4095, as said below
- parent_two: int32 [4096], replicated, may hold values from 0 to 255, as said below
- old_level_one: bfloat16 [65536, 1024], P('cent', 'dp'), may hold values from -6 to 6
Outputs:
- level_one: float32 [65536, 1024], P('cent', 'dp')
- level_two: float32 [4096, 1024], P('cent', 'dp')
- level_three: float32 [256, 1024], replicated
- residual: bfloat16 [32768, 1024], P(('dp', 'cent'))
The draws below stay inside these ranges and needn't reach their ends.
Inputs may be any that keep to these rules, and one draw needn't show every extreme that they name: With 32 = 32: the 256 points of one device name at most 32 centroids of one block of 4096 level-1 centroids (block = assign // 4096); for every dp index one block is named by exactly 32 points of every device of that dp index. `parent_one`: every level-2 centroid is the parent of exactly 16 level-1 centroids. `parent_two`: every level-3 centroid is the parent of exactly 16 level-2 centroids.
All inputs are finite; a program needn't handle non-finite values.
Results may differ from the reference program's by a relative error of at most 0.013.
Values may be sent and summed in bfloat16 or wider, within the bound.
No kernel may reach another device: no remote copies, remote signals or barrier semaphores. Data moves between devices by JAX's collectives and lax.ppermute only.
A program may use at most 64 MiB of HBM per device.

```python
import jax
import jax.numpy as jnp

D = 1024
K1_DEV = 4096
K1 = 65536
K2 = 4096
K3 = 256
PTS_DEV = 256
CAP = 32
PTS = 32768


def hierarchy(key):
    owners = K1 // K1_DEV
    blocks = PTS // PTS_DEV
    rows = jnp.arange(PTS_DEV, dtype=jnp.int32)[None, :]
    hot_rows = jax.random.randint(jax.random.fold_in(key, 101), (blocks // owners,), 0, owners)
    hot = jnp.repeat(hot_rows, owners)[:, None]
    others = (rows - CAP) % (owners - 1)
    others = jnp.where(others >= hot, others + 1, others)
    owner = jnp.where(rows < CAP, hot, others)
    first = jax.random.randint(jax.random.fold_in(key, 102), (blocks, PTS_DEV), 0, K1_DEV)
    second = jax.random.randint(jax.random.fold_in(key, 103), (blocks, PTS_DEV), 0, K1_DEV)
    local = first * second // K1_DEV
    top_rows = (rows == 0) | (rows == CAP + owners - 2)
    low_rows = (rows == 1) | (rows == CAP)
    local = jnp.where(top_rows, K1_DEV - 1, local)
    local = jnp.where(low_rows, 0, local)
    labels = owner * K1_DEV + local
    shuffles = jax.vmap(lambda sub_key: jax.random.permutation(sub_key, PTS_DEV))(jax.random.split(jax.random.fold_in(key, 104), blocks))
    labels = jnp.take_along_axis(labels, shuffles.astype(jnp.int32), axis=1).reshape(PTS).astype(jnp.int32)
    parents_one = (jax.random.permutation(jax.random.fold_in(key, 105), K1) % K2).astype(jnp.int32)
    parents_two = (jax.random.permutation(jax.random.fold_in(key, 106), K2) % K3).astype(jnp.int32)
    return (labels, parents_one, parents_two)


def draw_assign(key, part):
    labels, parents_one, parents_two = hierarchy(key)
    return labels


def draw_parent_one(key, part):
    labels, parents_one, parents_two = hierarchy(key)
    return parents_one


def draw_parent_two(key, part):
    labels, parents_one, parents_two = hierarchy(key)
    return parents_two


def draw_points(key, part):
    labels, parents_one, parents_two = hierarchy(key)
    middle = parents_one[labels]
    coarse = parents_two[middle]
    key = jax.random.fold_in(key, 7)
    coarse_centers = jax.random.normal(jax.random.fold_in(key, 1), (K3, D), jnp.float32)
    middle_centers = jax.random.normal(jax.random.fold_in(key, 2), (K2, D), jnp.float32)
    noise = jax.random.normal(jax.random.fold_in(key, 3), (PTS, D), jnp.float32)
    values = 1.2 * coarse_centers[coarse] + 0.8 * middle_centers[middle] + 0.7 * noise
    return jnp.clip(values, -8.0, 8.0).astype(jnp.bfloat16)


def levels(rng, dims, pieces, smallest, largest):
    loudness, own = 1.0, jax.random.fold_in(rng, 6)
    for axis_at, shards_of in pieces:
        heights = jnp.exp(jax.random.uniform(jax.random.fold_in(own, axis_at), (shards_of,), jnp.float32, smallest / len(pieces), largest / len(pieces)))
        loudness = loudness * jnp.repeat(heights, dims[axis_at] // shards_of).reshape([-1 if axis == axis_at else 1 for axis in range(len(dims))])
    return loudness


def scatter_about(rng, dims, deviation, bound, cuts=(), kind=jnp.bfloat16):
    result = jax.random.normal(rng, dims, jnp.float32) * deviation
    if len(cuts) > 0:
        result = levels(rng, dims, cuts, -0.22, 0.18) * result
    return jnp.clip(result, min=-bound, max=bound).astype(kind)


def setup_inputs(seed: int = 0) -> dict:
    key_list = jax.random.split(jax.random.key(seed), 6)
    return {
        "points": draw_points(jax.random.fold_in(key_list[5], 71), 0),
        "assign": draw_assign(jax.random.fold_in(key_list[5], 71), 0),
        "parent_one": draw_parent_one(jax.random.fold_in(key_list[5], 71), 0),
        "parent_two": draw_parent_two(jax.random.fold_in(key_list[5], 71), 0),
        "old_level_one": scatter_about(key_list[4], (K1, D), 1.0, 6.0, ((0, 16), (1, 8))),
    }


def reference(points, assign, parent_one, parent_two, old_level_one):
    values = points.astype(jnp.float32)
    sums_one = jax.ops.segment_sum(values, assign, num_segments=K1)
    counts_one = jax.ops.segment_sum(jnp.ones((PTS,), jnp.float32), assign, num_segments=K1)
    mass_one = sums_one + old_level_one.astype(jnp.float32)
    weight_one = counts_one + 1.0
    level_one = mass_one / weight_one[:, None]
    residual = (values - level_one[assign]).astype(jnp.bfloat16)
    mass_two = jax.ops.segment_sum(mass_one, parent_one, num_segments=K2)
    weight_two = jax.ops.segment_sum(weight_one, parent_one, num_segments=K2)
    level_two = mass_two / weight_two[:, None]
    mass_three = jax.ops.segment_sum(mass_two, parent_two, num_segments=K3)
    weight_three = jax.ops.segment_sum(weight_two, parent_two, num_segments=K3)
    level_three = mass_three / weight_three[:, None]
    return level_one, level_two, level_three, residual
```

```python
import jax
import jax.numpy as jnp
from jax import lax
from jax.experimental import pallas as pl
from jax.experimental.pallas import tpu as pltpu
from jax.sharding import PartitionSpec as P

F32 = jnp.float32
BF16 = jnp.bfloat16
I32 = jnp.int32
LANES = 128
CHUNK = 512
LOW = 512
HIGHS = 8
CAP = 32
EXTRA = 8
BOTH = ("dp", "cent")


def iota(shape, axis):
    return lax.broadcasted_iota(I32, shape, axis)


def dot(left, right):
    return jnp.dot(left, right, preferred_element_type=F32)


def dot_nt(left, right):
    return lax.dot_general(left, right, (((1,), (1,)), ((), ())), preferred_element_type=F32)


def call(body, out_shape, scratch=(), flops=0, size=4 << 20, vmem=24 << 20):
    return pl.pallas_call(
        body,
        out_shape=out_shape,
        scratch_shapes=list(scratch),
        compiler_params=pltpu.CompilerParams(vmem_limit_bytes=vmem),
        cost_estimate=pl.CostEstimate(flops=flops, bytes_accessed=size, transcendentals=0),
    )


def pack_kernel(assign_ref, points_ref, send_ref, back_ref):
    count = assign_ref.shape[1]
    owners = send_ref.shape[1]
    label = assign_ref[...]
    owner = lax.shift_right_logical(label, 12)
    local = label & 4095
    mine = iota((owners, count), 0) == owner
    mine_f = jnp.where(mine, 1.0, 0.0)
    before = jnp.where(iota((count, count), 0) <= iota((count, count), 1), 1.0, 0.0).astype(BF16)
    running = dot(mine_f.astype(BF16), before)
    place = jnp.sum(running * mine_f, axis=0, keepdims=True).astype(I32) - 1
    slot = owner * CAP + place
    table = jnp.where(iota((owners * CAP, count), 0) == slot, 1.0, 0.0).astype(BF16)
    same = jnp.where(iota((count, count), 0) == iota((count, count), 1), 1.0, 0.0).astype(BF16)
    back_ref[...] = dot_nt(same, table).astype(BF16)
    shift = (lax.axis_index("cent") % 4) * CAP
    lane_table = jnp.where(iota((LANES, count), 0) == place + shift, 1.0, 0.0).astype(BF16)
    high = (lax.shift_right_logical(local, 6) + 1).astype(F32)
    low = ((local & 63) + 1).astype(F32)
    high_rows = dot_nt((mine_f * high).astype(BF16), lane_table)
    low_rows = dot_nt((mine_f * low).astype(BF16), lane_table)
    row = iota((owners, EXTRA, LANES), 1)
    extra = jnp.where(row == 0, high_rows[:, None, :], jnp.where(row == 1, low_rows[:, None, :], 0.0))
    extra = extra.astype(BF16)
    for part in range(send_ref.shape[0]):
        rows = dot(table, points_ref[:, part * LANES : (part + 1) * LANES]).astype(BF16)
        send_ref[part, :, 0:CAP, :] = rows.reshape(owners, CAP, LANES)
        send_ref[part, :, CAP : CAP + EXTRA, :] = extra


def slot_digits(slab_ref, digits_ref):
    rows = slab_ref[:, CAP : CAP + EXTRA, :].astype(F32).reshape(-1, LANES).astype(BF16)
    shape = (64, rows.shape[0])
    column, line = iota(shape, 1), iota(shape, 0)
    pick = (lax.shift_right_logical(column, 5) == (line & 31)) & (
        (column & 7) == lax.shift_right_logical(line, 5)
    )
    digits_ref[...] = dot(jnp.where(pick, 1.0, 0.0).astype(BF16), rows)


def digit_rows(digits_ref, at):
    return digits_ref[pl.ds(at, 1), :], digits_ref[pl.ds(at + 32, 1), :]


def across_lanes(digits_ref, step):
    found = []
    for part in range(CHUNK // LANES):
        high, low = digit_rows(digits_ref, step * (CHUNK // LANES) + part)
        found.append((high * 64.0 + low).astype(I32) - 65)
    return found


def down_rows(digits_ref, step):
    same = iota((LANES, LANES), 0) == iota((LANES, LANES), 1)
    parts = []
    for part in range(CHUNK // LANES):
        high, low = digit_rows(digits_ref, step * (CHUNK // LANES) + part)
        parts.append(
            jnp.concatenate([jnp.where(same, high, 0.0), jnp.where(same, low, 0.0)], axis=1)
        )
    left = jnp.concatenate(parts, axis=0).astype(BF16)
    right = jnp.where(iota((2 * LANES, LANES), 0) < LANES, 64.0, 1.0).astype(BF16)
    return dot(left, right).astype(I32) - 65


def add_segments(total_ref, digits_ref, step, rows):
    line = iota((LOW, LANES), 0)
    left = jnp.concatenate(
        [
            jnp.where(line == (label & (LOW - 1)), 1.0, 0.0).astype(BF16)
            for label in across_lanes(digits_ref, step)
        ],
        axis=1,
    )
    high = lax.shift_right_arithmetic(down_rows(digits_ref, step), 9)
    wide = rows.astype(F32)
    for pair in range(HIGHS // 2):
        right = jnp.concatenate(
            [jnp.where(high == 2 * pair + side, wide, 0.0).astype(BF16) for side in range(2)], axis=1
        )
        at = slice(2 * pair * LANES, (2 * pair + 2) * LANES)
        total_ref[:, at] += dot(left, right)
    lane = iota((CHUNK, LANES), 1)
    ones = jnp.where((high == (lane & 7)) & (lane < 16), 1.0, 0.0).astype(BF16)
    total_ref[:, HIGHS * LANES :] += dot(left, ones)


def parent_kernel(parent_ref, old_ref, total_ref, digits_ref):
    parent = parent_ref[...]
    digits_ref[0:32, :] = (lax.shift_right_logical(parent, 6) + 1).astype(F32)
    digits_ref[32:64, :] = ((parent & 63) + 1).astype(F32)
    total_ref[...] = jnp.zeros_like(total_ref)

    def step(at, carry):
        rows = old_ref[pl.ds(pl.multiple_of(at * CHUNK, CHUNK), CHUNK), :]
        add_segments(total_ref, digits_ref, at, rows)
        return carry

    lax.fori_loop(0, old_ref.shape[0] // CHUNK, step, 0)


def slab_rows(slab_ref, at):
    sources = CHUNK // CAP
    return slab_ref[pl.ds(at * sources, sources), 0:CAP, :].reshape(CHUNK, LANES)


def upper_kernel(slab_ref, table_ref, top_ref, start_ref, send_ref, digits_ref, parents_ref, total_ref):
    slot_digits(slab_ref, digits_ref)
    total_ref[...] = start_ref[...]
    steps = slab_ref.shape[0] * CAP // CHUNK
    line = iota((LANES, LANES), 0)

    def step(at, carry):
        for part in range(CHUNK // LANES):
            row = at * (CHUNK // LANES) + part
            high, low = digit_rows(digits_ref, row)
            left = jnp.where(line == high.astype(I32) - 1, 1.0, 0.0).astype(BF16)
            found = dot(table_ref[...], left)
            found = jnp.where((line & 63) == low.astype(I32) - 1, found, 0.0)
            parents_ref[pl.ds(row, 1), :] = jnp.sum(found[0:64], axis=0, keepdims=True)
            parents_ref[pl.ds(row + 32, 1), :] = jnp.sum(found[64:128], axis=0, keepdims=True)
        add_segments(total_ref, parents_ref, at, slab_rows(slab_ref, at))
        return carry

    lax.fori_loop(0, steps, step, 0)
    weights = total_ref[:, HIGHS * LANES :]
    coarse = weights.astype(BF16).astype(F32)
    fine = weights - coarse
    lane = iota((LOW, LANES), 1)
    tops = jnp.zeros((256, 2 * LANES), F32)
    for high in range(HIGHS):
        mass = total_ref[:, high * LANES : (high + 1) * LANES].astype(BF16)
        for half in range(2):
            send_ref[2 * high + half, 0:256, :] = mass[half * 256 : (half + 1) * 256]
        heavy = jnp.where(lane == high, coarse, jnp.where(lane == high + 8, fine, 0.0)).astype(BF16)
        left = jnp.concatenate(
            [
                jnp.where(
                    iota((256, LANES), 0) == top_ref[high * 4 + part : high * 4 + part + 1, :], 1.0, 0.0
                ).astype(BF16)
                for part in range(4)
            ],
            axis=1,
        )
        tops += dot(left, jnp.concatenate([mass, heavy], axis=1))
    top_mass = tops[:, :LANES].astype(BF16)
    top_weight = jnp.sum(tops[:, LANES:].T[0:16], axis=0, keepdims=True)
    top_coarse = top_weight.astype(BF16).astype(F32)
    top_fine = top_weight - top_coarse
    coarse_t, fine_t = coarse.T, fine.T
    for owner in range(send_ref.shape[0]):
        send_ref[owner, 256:272, :] = top_mass[owner * 16 : (owner + 1) * 16]
        high, from_lane = owner // 2, (owner % 2) * 256
        rows = []
        for source, line_at, lane_at in (
            (coarse_t, high, from_lane),
            (fine_t, high, from_lane),
            (top_coarse, 0, 0),
            (top_fine, 0, 0),
        ):
            for half in range(2):
                first = lane_at + half * LANES
                rows.append(source[line_at : line_at + 1, first : first + LANES])
        send_ref[owner, 272:280, :] = jnp.concatenate(rows, axis=0).astype(BF16)


def level_kernel(slab_ref, old_ref, level_ref, residual_ref, digits_ref, total_ref, table_ref):
    slot_digits(slab_ref, digits_ref)
    total_ref[...] = jnp.zeros_like(total_ref)
    steps = slab_ref.shape[0] * CAP // CHUNK

    def gather(at, carry):
        add_segments(total_ref, digits_ref, at, slab_rows(slab_ref, at))
        return carry

    lax.fori_loop(0, steps, gather, 0)
    inverse = 1.0 / (total_ref[:, HIGHS * LANES :] + 1.0)
    for high in range(HIGHS):
        lines = slice(high * LOW, (high + 1) * LOW)
        lanes = slice(high * LANES, (high + 1) * LANES)
        mass = total_ref[:, lanes] + old_ref[lines, :].astype(F32)
        level = mass * jnp.broadcast_to(inverse[:, high : high + 1], mass.shape)
        level_ref[lines, :] = level
        table_ref[:, lanes] = level.astype(BF16)

    def subtract(at, carry):
        label = down_rows(digits_ref, at)
        low = label & (LOW - 1)
        high = lax.shift_right_arithmetic(label, 9)
        lane = iota((CHUNK, LANES), 1)
        left = jnp.concatenate(
            [
                jnp.where(low == lane + part * LANES, 1.0, 0.0).astype(BF16)
                for part in range(LOW // LANES)
            ],
            axis=1,
        )
        rows = slab_rows(slab_ref, at).astype(F32)
        for pair in range(HIGHS // 2):
            found = dot(left, table_ref[:, 2 * pair * LANES : (2 * pair + 2) * LANES])
            for side in range(2):
                chosen = found[:, side * LANES : (side + 1) * LANES]
                rows -= jnp.where(high == 2 * pair + side, chosen, 0.0)
        sources = CHUNK // CAP
        residual_ref[pl.ds(at * sources, sources), :, :] = rows.astype(BF16).reshape(
            sources, CAP, LANES
        )
        return carry

    lax.fori_loop(0, steps, subtract, 0)


def finish_kernel(parts_ref, level_ref, send_ref, column_ref):
    total = parts_ref[0].astype(F32)
    for source in range(1, parts_ref.shape[0]):
        total += parts_ref[source].astype(F32)
    tail = total[272:280].T
    for half in range(2):
        weight = tail[:, half : half + 1] + tail[:, half + 2 : half + 3]
        lines = slice(half * LANES, (half + 1) * LANES)
        level_ref[lines, :] = total[lines] / jnp.broadcast_to(weight, (LANES, LANES))
    me = lax.axis_index("cent")
    first = tail[:, 4:5] + tail[:, 6:7]
    second = tail[:, 5:6] + tail[:, 7:8]
    chosen = jnp.where(me < 8, first, second)
    column_ref[...] = jnp.broadcast_to(chosen, (LANES, LANES))
    weight = column_ref[pl.ds(pl.multiple_of((me % 8) * 16, 16), 16), :]
    top = (total[256:272] / weight).astype(BF16)
    send_ref[...] = jnp.broadcast_to(top[None], send_ref.shape)


def unpack_kernel(back_ref, returned_ref, residual_ref):
    owners, cap, lanes = returned_ref.shape[1:]
    for pair in range(returned_ref.shape[0] // 2):
        right = jnp.concatenate(
            [returned_ref[2 * pair + side].reshape(owners * cap, lanes) for side in range(2)], axis=1
        )
        residual_ref[:, 2 * pair * lanes : (2 * pair + 2) * lanes] = dot(back_ref[...], right).astype(BF16)


def top_kernel(parts_ref, level_ref):
    for part in range(parts_ref.shape[0]):
        rows = parts_ref[part].reshape(level_ref.shape[0], LANES)
        level_ref[:, part * LANES : (part + 1) * LANES] = rows.astype(F32)


def shape(dims, kind):
    return jax.ShapeDtypeStruct(dims, kind)


def swap(value, axes):
    return lax.all_to_all(value, axes, split_axis=0, concat_axis=0, tiled=True)


def on_device(points, assign, parent_one, parent_two, old_level_one):
    count, width = points.shape
    owners = lax.axis_size("cent")
    groups = lax.axis_size("dp")
    devices = owners * groups
    block, lanes = old_level_one.shape
    slots = owners * CAP
    rows = CAP + EXTRA
    total_shape = shape((LOW, (HIGHS + 1) * LANES), F32)
    work = 2 * LOW * block * (HIGHS + 1) * LANES

    send, back = call(
        pack_kernel,
        (shape((groups, owners, rows, lanes), BF16), shape((count, slots), BF16)),
        flops=2 * slots * count * width,
    )(assign.reshape(1, count), points)
    slab = swap(send.reshape(devices, rows, lanes), BOTH)

    start = call(
        parent_kernel, total_shape, [pltpu.VMEM((64, LANES), F32)], flops=work
    )(parent_one.reshape(block // LANES, LANES), old_level_one)
    grid = parent_one.reshape(64, 64).T
    table = jnp.concatenate([lax.shift_right_logical(grid, 6), grid & 63], axis=0) + 1
    table = jnp.pad(table, ((0, 0), (0, 64))).astype(BF16)

    share = call(
        upper_kernel,
        shape((owners, 280, lanes), BF16),
        [
            pltpu.VMEM((64, LANES), F32),
            pltpu.VMEM((64, LANES), F32),
            pltpu.VMEM(total_shape.shape, F32),
        ],
        flops=work,
    )(slab, table, parent_two.reshape(-1, LANES), start)
    shares = swap(share, "cent")

    level_one, slab_residual = call(
        level_kernel,
        (shape((block, lanes), F32), shape((devices, CAP, lanes), BF16)),
        [
            pltpu.VMEM((64, LANES), F32),
            pltpu.VMEM(total_shape.shape, F32),
            pltpu.VMEM((LOW, HIGHS * LANES), BF16),
        ],
        flops=2 * work,
    )(slab, old_level_one)
    returned = swap(slab_residual, BOTH)

    level_two, top = call(
        finish_kernel,
        (shape((256, lanes), F32), shape((devices, 16, lanes), BF16)),
        [pltpu.VMEM((LANES, LANES), F32)],
    )(shares)
    tops = swap(top, BOTH)
    residual = call(unpack_kernel, shape((count, width), BF16), flops=2 * slots * count * width)(
        back, returned.reshape(groups, owners, CAP, lanes)
    )
    level_three = call(top_kernel, shape((owners * 16, width), F32))(
        tops.reshape(groups, owners, 16, lanes)
    )
    return (level_one, level_two, level_three, residual)


def solution(mesh):
    in_specs = (P(("dp", "cent"), None), P(("dp", "cent")), P("cent"), P(), P("cent", "dp"))
    out_specs = (P("cent", "dp"), P("cent", "dp"), P(), P(("dp", "cent"), None))
    return jax.shard_map(
        on_device, mesh=mesh, in_specs=in_specs, out_specs=out_specs, check_vma=False
    )
```

```python
import jax
import jax.numpy as jnp
from jax import lax
from jax.experimental import pallas as pl
from jax.experimental.pallas import tpu as pltpu
from jax.sharding import PartitionSpec as P

F32 = jnp.float32
BF16 = jnp.bfloat16
I32 = jnp.int32
LANES = 128
LOW = 512
HIGHS = 8
CAP = 32
HALF = 16
EXTRA = 8
TOP = 16
BOTH = ("dp", "cent")


def iota(shape, axis):
    return lax.broadcasted_iota(I32, shape, axis)


def dot(left, right):
    return jnp.dot(left, right, preferred_element_type=F32)


def dot_nt(left, right):
    return lax.dot_general(left, right, (((1,), (1,)), ((), ())), preferred_element_type=F32)


def lane_slice(at, width=LANES):
    return slice(at * width, (at + 1) * width)


HBM = pl.BlockSpec(memory_space=pltpu.HBM)
VMEM = pl.BlockSpec(memory_space=pltpu.VMEM)


def call(body, out_shape, ins, outs, scratch=(), flops=0, size=4 << 20, vmem=32 << 20, alias=None):
    return pl.pallas_call(
        body,
        out_shape=out_shape,
        in_specs=ins,
        out_specs=outs,
        scratch_shapes=list(scratch),
        input_output_aliases=alias or {},
        compiler_params=pltpu.CompilerParams(vmem_limit_bytes=vmem),
        cost_estimate=pl.CostEstimate(flops=flops, bytes_accessed=size, transcendentals=0),
    )


def pack_kernel(assign_hbm, points_hbm, send_hbm, back_ref, assign_ref, points_ref, send_ref, sems):
    owners = send_ref.shape[1]
    parts = send_ref.shape[0]
    count = points_ref.shape[0]
    load = pltpu.make_async_copy(assign_hbm, assign_ref, sems.at[0])
    load.start()
    loads = []
    for pair in range(parts // 2):
        at = lane_slice(pair, 2 * LANES)
        loads.append(
            pltpu.make_async_copy(points_hbm.at[:, at], points_ref.at[:, at], sems.at[1 + pair])
        )
        loads[-1].start()
    before = jnp.where(iota((count, count), 0) <= iota((count, count), 1), 1.0, 0.0).astype(BF16)
    same = jnp.where(iota((count, count), 0) == iota((count, count), 1), 1.0, 0.0).astype(BF16)
    load.wait()
    label = assign_ref[...]
    owner = lax.shift_right_logical(label, 12)
    local = label & 4095
    mine = iota((owners, count), 0) == owner
    mine_f = jnp.where(mine, 1.0, 0.0)
    running = dot(mine_f.astype(BF16), before)
    place = jnp.sum(running * mine_f, axis=0, keepdims=True).astype(I32) - 1
    slot = owner * CAP + place
    table = jnp.where(iota((owners * CAP, count), 0) == slot, 1.0, 0.0).astype(BF16)
    shift = (lax.axis_index("cent") % 8) * HALF
    line = iota((LANES, count), 0)
    row = iota((owners, EXTRA, LANES), 1)
    digits = [(lax.shift_right_logical(local, 6) + 1).astype(F32), ((local & 63) + 1).astype(F32)]
    digits = [(mine_f * digit).astype(BF16) for digit in digits]
    extra = jnp.zeros((owners, EXTRA, LANES), F32)
    for half in range(2):
        first = half * HALF
        inside = (place >= first) & (place < first + HALF)
        lane = jnp.where(inside, place - first + shift, -1)
        lane_table = jnp.where(line == lane, 1.0, 0.0).astype(BF16)
        for kind in range(2):
            found = dot_nt(digits[kind], lane_table)
            extra = jnp.where(row == 2 * kind + half, found[:, None, :], extra)
    extra = extra.astype(BF16)
    stores = []
    for part in range(parts):
        if part % 2 == 0:
            loads[part // 2].wait()
            both = dot(table, points_ref[:, lane_slice(part // 2, 2 * LANES)]).astype(BF16)
        rows = both[:, lane_slice(part % 2)]
        send_ref[part, :, 0:CAP, :] = rows.reshape(owners, CAP, LANES)
        send_ref[part, :, CAP : CAP + EXTRA, :] = extra
        stores.append(
            pltpu.make_async_copy(send_ref.at[part], send_hbm.at[part], sems.at[1 + parts // 2 + part])
        )
        stores[-1].start()
    back_ref[...] = dot_nt(same, table).astype(BF16)
    for store in stores:
        store.wait()


def slot_digits(slab_ref, digits_ref):
    rows = slab_ref[:, CAP : CAP + EXTRA, :].astype(F32).reshape(-1, LANES).astype(BF16)
    shape = (64, rows.shape[0])
    column, line = iota(shape, 1), iota(shape, 0)
    pick = (lax.shift_right_logical(column, 6) == (line & 15)) & (
        (column & 7) == lax.shift_right_logical(line, 4)
    )
    digits_ref[...] = dot(jnp.where(pick, 1.0, 0.0).astype(BF16), rows)


def across_lanes(digits_ref, at, count):
    found = []
    for part in range(count):
        high, low = digits_ref[pl.ds(at + part, 1), :], digits_ref[pl.ds(at + part + 32, 1), :]
        found.append((high * 64.0 + low).astype(I32) - 65)
    return found


def down_rows(digits_ref, at, count):
    same = iota((LANES, LANES), 0) == iota((LANES, LANES), 1)
    parts = []
    for part in range(count):
        high, low = digits_ref[pl.ds(at + part, 1), :], digits_ref[pl.ds(at + part + 32, 1), :]
        parts.append(
            jnp.concatenate([jnp.where(same, high, 0.0), jnp.where(same, low, 0.0)], axis=1)
        )
    left = jnp.concatenate(parts, axis=0).astype(BF16)
    right = jnp.where(iota((2 * LANES, LANES), 0) < LANES, 64.0, 1.0).astype(BF16)
    return dot(left, right).astype(I32) - 65


def low_table(labels):
    line = iota((LOW, LANES), 0)
    return jnp.concatenate(
        [jnp.where(line == (label & (LOW - 1)), 1.0, 0.0).astype(BF16) for label in labels], axis=1
    )


def masked(rows, high, which):
    return jnp.where(high == which, rows, 0.0).astype(BF16)


def counting(high):
    lane = iota(high.shape, 1)
    return jnp.where((high == (lane & 7)) & (lane < 16), 1.0, 0.0).astype(BF16)


def segments(total_ref, left_ref, high_ref, rows_of, digits_ref, steps):
    for step in range(steps):
        left_ref[:, lane_slice(step, 512)] = low_table(across_lanes(digits_ref, 4 * step, 4))
        high_ref[lane_slice(step, 512), :] = lax.shift_right_arithmetic(
            down_rows(digits_ref, 4 * step, 4), 9
        )
    left = left_ref[:, 0 : steps * 512]
    for pair in range(HIGHS // 2):
        right = []
        for step in range(steps):
            high, rows = high_ref[lane_slice(step, 512), :], rows_of(step)
            right.append(
                jnp.concatenate([masked(rows, high, 2 * pair + side) for side in range(2)], axis=1)
            )
        total_ref[:, lane_slice(pair, 2 * LANES)] = dot(left, jnp.concatenate(right, axis=0))
    total_ref[:, HIGHS * LANES :] = dot(left, counting(high_ref[0 : steps * 512, :]))


def add_segments(total_ref, digits_ref, at, rows):
    left = low_table(across_lanes(digits_ref, at, 2))
    high = lax.shift_right_arithmetic(down_rows(digits_ref, at, 2), 9)
    for pair in range(HIGHS // 2):
        right = jnp.concatenate([masked(rows, high, 2 * pair + side) for side in range(2)], axis=1)
        total_ref[:, lane_slice(pair, 2 * LANES)] += dot(left, right)
    total_ref[:, HIGHS * LANES :] += dot(left, counting(high))


def lower_rows(slab_ref, step):
    return slab_ref[lane_slice(step, 32), 0:HALF, :].reshape(512, LANES).astype(F32)


def upper_rows(slab_ref, group):
    return slab_ref[pl.ds(group * 16, 16), HALF:CAP, :].reshape(256, LANES).astype(F32)


def any_label(digits_ref, group):
    return jnp.max(digits_ref[pl.ds(16 + 2 * group, 2), :]) > 0.0


def parent_kernel(parent_ref, old_ref, total_ref, digits_ref):
    parent = parent_ref[...]
    digits_ref[0:32, :] = (lax.shift_right_logical(parent, 6) + 1).astype(F32)
    digits_ref[32:64, :] = ((parent & 63) + 1).astype(F32)
    total_ref[...] = jnp.zeros_like(total_ref)

    def step(at, carry):
        rows = old_ref[pl.ds(pl.multiple_of(at * 256, 256), 256), :].astype(F32)
        add_segments(total_ref, digits_ref, 2 * at, rows)
        return carry

    lax.fori_loop(0, old_ref.shape[0] // 256, step, 0)


def find_parents(digits_ref, parents_ref, table_ref, at, count):
    line = iota((LANES, LANES), 0)
    rows = [(digits_ref[pl.ds(at + n, 1), :], digits_ref[pl.ds(at + n + 32, 1), :]) for n in range(count)]
    left = [jnp.where(line == high.astype(I32) - 1, 1.0, 0.0).astype(BF16) for high, _ in rows]
    found = dot(table_ref[...], jnp.concatenate(left, axis=1))
    for n in range(count):
        chosen = jnp.where((line & 63) == rows[n][1].astype(I32) - 1, found[:, lane_slice(n)], 0.0)
        parents_ref[pl.ds(at + n, 1), :] = jnp.sum(chosen[0:64], axis=0, keepdims=True)
        parents_ref[pl.ds(at + n + 32, 1), :] = jnp.sum(chosen[64:128], axis=0, keepdims=True)


def upper_kernel(
    slab_ref, table_ref, top_ref, start_hbm, send_hbm,
    digits_ref, parents_ref, total_ref, left_ref, high_ref, start_ref, send_ref, right_ref, sems,
):
    load = pltpu.make_async_copy(start_hbm, start_ref, sems.at[0])
    load.start()
    slot_digits(slab_ref, digits_ref)
    for step in range(4):
        find_parents(digits_ref, parents_ref, table_ref, 4 * step, 4)
    segments(total_ref, left_ref, high_ref, lambda step: lower_rows(slab_ref, step), parents_ref, 4)

    def more(group, carry):
        @pl.when(any_label(digits_ref, group))
        def _():
            find_parents(digits_ref, parents_ref, table_ref, 16 + 2 * group, 2)
            add_segments(total_ref, parents_ref, 16 + 2 * group, upper_rows(slab_ref, group))

        return carry

    lax.fori_loop(0, slab_ref.shape[0] // 16, more, 0)
    load.wait()
    at = slice(HIGHS * LANES, (HIGHS + 1) * LANES)
    weights = total_ref[:, at] + start_ref[:, at]
    coarse = weights.astype(BF16).astype(F32)
    fine = weights - coarse
    lane = iota((LOW, LANES), 1)
    tops = []
    for high in range(HIGHS):
        mass = (total_ref[:, lane_slice(high)] + start_ref[:, lane_slice(high)]).astype(BF16)
        for half in range(2):
            send_ref[2 * high + half, 0:256, :] = mass[half * 256 : (half + 1) * 256]
        right_ref[lane_slice(high, LOW), 0:LANES] = mass
        right_ref[lane_slice(high, LOW), LANES:] = jnp.where(
            lane == high, coarse, jnp.where(lane == high + 8, fine, 0.0)
        ).astype(BF16)
        for part in range(4):
            hit = iota((256, LANES), 0) == top_ref[high * 4 + part : high * 4 + part + 1, :]
            tops.append(jnp.where(hit, 1.0, 0.0).astype(BF16))
    tops = dot(jnp.concatenate(tops, axis=1), right_ref[...])
    top_mass = tops[:, :LANES].astype(BF16)
    top_weight = jnp.sum(tops[:, LANES:].T[0:16], axis=0, keepdims=True)
    top_coarse = top_weight.astype(BF16).astype(F32)
    top_fine = top_weight - top_coarse
    coarse_t, fine_t = coarse.T, fine.T
    stores = []
    for owner in range(send_ref.shape[0]):
        send_ref[owner, 256:272, :] = top_mass[owner * TOP : (owner + 1) * TOP]
        high, from_lane = owner // 2, (owner % 2) * 256
        rows = []
        for source, line_at, lane_at in (
            (coarse_t, high, from_lane),
            (fine_t, high, from_lane),
            (top_coarse, 0, 0),
            (top_fine, 0, 0),
        ):
            for half in range(2):
                first = lane_at + half * LANES
                rows.append(source[line_at : line_at + 1, first : first + LANES])
        send_ref[owner, 272:280, :] = jnp.concatenate(rows, axis=0).astype(BF16)
        if owner % 4 == 3:
            part = pl.ds(owner - 3, 4)
            stores.append(
                pltpu.make_async_copy(send_ref.at[part], send_hbm.at[part], sems.at[1 + owner // 4])
            )
            stores[-1].start()
    for store in stores:
        store.wait()


def level_kernel(
    slab_ref, old_hbm, level_hbm, residual_hbm,
    digits_ref, total_ref, table_ref, left_ref, high_ref, old_ref, level_ref, residual_ref,
    load_sem, level_sems, low_sems, up_sems,
):
    load = pltpu.make_async_copy(old_hbm, old_ref, load_sem)
    load.start()
    slot_digits(slab_ref, digits_ref)
    segments(total_ref, left_ref, high_ref, lambda step: lower_rows(slab_ref, step), digits_ref, 4)
    groups = slab_ref.shape[0] // 16

    def more(group, carry):
        @pl.when(any_label(digits_ref, group))
        def _():
            add_segments(total_ref, digits_ref, 16 + 2 * group, upper_rows(slab_ref, group))

        return carry

    lax.fori_loop(0, groups, more, 0)
    load.wait()
    inverse = 1.0 / (total_ref[:, HIGHS * LANES :] + 1.0)
    stores = []
    for high in range(HIGHS):
        lines = lane_slice(high, LOW)
        mass = total_ref[:, lane_slice(high)] + old_ref[lines, :].astype(F32)
        level = mass * jnp.broadcast_to(inverse[:, high : high + 1], mass.shape)
        level_ref[lines, :] = level
        table_ref[:, lane_slice(high)] = level.astype(BF16)
        stores.append(
            pltpu.make_async_copy(level_ref.at[lines], level_hbm.at[lines], level_sems.at[high])
        )
        stores[-1].start()

    def subtract(at, count, rows):
        label = down_rows(digits_ref, at, count)
        low = label & (LOW - 1)
        high = lax.shift_right_arithmetic(label, 9)
        lane = iota(label.shape, 1)
        left = jnp.concatenate(
            [
                jnp.where(low == lane + part * LANES, 1.0, 0.0).astype(BF16)
                for part in range(LOW // LANES)
            ],
            axis=1,
        )
        for pair in range(HIGHS // 2):
            found = dot(left, table_ref[:, lane_slice(pair, 2 * LANES)])
            for side in range(2):
                rows -= jnp.where(high == 2 * pair + side, found[:, lane_slice(side)], 0.0)
        return rows.astype(BF16)

    for step in range(4):
        sources = lane_slice(step, 32)
        residual_ref[sources, 0:HALF, :] = subtract(
            4 * step, 4, lower_rows(slab_ref, step)
        ).reshape(32, HALF, LANES)
        part = (sources, slice(0, HALF))
        stores.append(
            pltpu.make_async_copy(residual_ref.at[part], residual_hbm.at[part], low_sems.at[step])
        )
        stores[-1].start()

    def upper_copy(group):
        part = (pl.ds(group * 16, 16), pl.ds(HALF, HALF))
        return pltpu.make_async_copy(residual_ref.at[part], residual_hbm.at[part], up_sems.at[group])

    def finish(group, carry):
        sources = pl.ds(group * 16, 16)
        live = any_label(digits_ref, group)

        @pl.when(live)
        def _():
            residual_ref[sources, HALF:CAP, :] = subtract(
                16 + 2 * group, 2, upper_rows(slab_ref, group)
            ).reshape(16, HALF, LANES)

        @pl.when(jnp.logical_not(live))
        def _():
            residual_ref[sources, HALF:CAP, :] = slab_ref[sources, HALF:CAP, :]

        upper_copy(group).start()
        return carry

    lax.fori_loop(0, groups, finish, 0)
    for store in stores:
        store.wait()

    def settle(group, carry):
        upper_copy(group).wait()
        return carry

    lax.fori_loop(0, groups, settle, 0)


def finish_kernel(parts_ref, send_in, level_ref, send_hbm, column_ref, top_ref, sem):
    total = parts_ref[0].astype(F32)
    for source in range(1, parts_ref.shape[0]):
        total += parts_ref[source].astype(F32)
    tail = total[272:280].T
    me = lax.axis_index("cent")
    chosen = jnp.where(me < 8, tail[:, 4:5] + tail[:, 6:7], tail[:, 5:6] + tail[:, 7:8])
    column_ref[...] = jnp.broadcast_to(chosen, (LANES, LANES))
    weight = column_ref[pl.ds(pl.multiple_of((me % 8) * TOP, TOP), TOP), :]
    top = (total[256:272] / weight).astype(BF16)
    top_ref[...] = jnp.broadcast_to(top[None], top_ref.shape)
    store = pltpu.make_async_copy(top_ref, send_hbm.at[:, pl.ds(CAP, TOP), :], sem)
    store.start()
    for half in range(2):
        weight = tail[:, half : half + 1] + tail[:, half + 2 : half + 3]
        lines = slice(half * LANES, (half + 1) * LANES)
        level_ref[lines, :] = total[lines] / jnp.broadcast_to(weight, (LANES, LANES))
    store.wait()


def unpack_kernel(back_ref, returned_ref, residual_ref, level_ref):
    groups, owners, rows, lanes = returned_ref.shape
    for pair in range(groups // 2):
        right = jnp.concatenate(
            [
                returned_ref[2 * pair + side, :, 0:CAP, :].reshape(owners * CAP, lanes)
                for side in range(2)
            ],
            axis=1,
        )
        residual_ref[:, lane_slice(pair, 2 * lanes)] = dot(back_ref[...], right).astype(BF16)
    for group in range(groups):
        top = returned_ref[group, :, CAP:rows, :].astype(F32)
        level_ref[:, lane_slice(group)] = top.reshape(owners * TOP, lanes)


def shape(dims, kind):
    return jax.ShapeDtypeStruct(dims, kind)


def swap(value, axes):
    return lax.all_to_all(value, axes, split_axis=0, concat_axis=0, tiled=True)


def on_device(points, assign, parent_one, parent_two, old_level_one):
    count, width = points.shape
    owners = lax.axis_size("cent")
    groups = lax.axis_size("dp")
    devices = owners * groups
    block, lanes = old_level_one.shape
    slots = owners * CAP
    rows = CAP + EXTRA
    total_dims = (LOW, (HIGHS + 1) * LANES)
    work = 2 * LOW * block * (HIGHS + 1) * LANES

    send, back = call(
        pack_kernel,
        (shape((groups, owners, rows, lanes), BF16), shape((count, slots), BF16)),
        [HBM, HBM],
        (HBM, VMEM),
        [
            pltpu.VMEM((1, count), I32),
            pltpu.VMEM((count, width), BF16),
            pltpu.VMEM((groups, owners, rows, lanes), BF16),
            pltpu.SemaphoreType.DMA((1 + groups // 2 + groups,)),
        ],
        flops=2 * slots * count * width,
    )(assign.reshape(1, count), points)
    slab = swap(send.reshape(devices, rows, lanes), BOTH)

    start = call(
        parent_kernel,
        shape(total_dims, F32),
        [VMEM, VMEM],
        VMEM,
        [pltpu.VMEM((64, LANES), F32)],
        flops=work,
    )(parent_one.reshape(block // LANES, LANES), old_level_one)
    grid = parent_one.reshape(64, 64).T
    table = jnp.concatenate([lax.shift_right_logical(grid, 6), grid & 63], axis=0) + 1
    table = jnp.pad(table, ((0, 0), (0, 64))).astype(BF16)

    share = call(
        upper_kernel,
        shape((owners, 280, lanes), BF16),
        [VMEM, VMEM, VMEM, HBM],
        HBM,
        [
            pltpu.VMEM((64, LANES), F32),
            pltpu.VMEM((64, LANES), F32),
            pltpu.VMEM(total_dims, F32),
            pltpu.VMEM((LOW, 2048), BF16),
            pltpu.VMEM((2048, LANES), I32),
            pltpu.VMEM(total_dims, F32),
            pltpu.VMEM((owners, 280, lanes), BF16),
            pltpu.VMEM((HIGHS * LOW, 2 * LANES), BF16),
            pltpu.SemaphoreType.DMA((5,)),
        ],
        flops=work,
    )(slab, table, parent_two.reshape(-1, LANES), start)
    shares = swap(share, "cent")

    level_one, answer = call(
        level_kernel,
        (shape((block, lanes), F32), shape((devices, CAP + TOP, lanes), BF16)),
        [VMEM, HBM],
        (HBM, HBM),
        [
            pltpu.VMEM((64, LANES), F32),
            pltpu.VMEM(total_dims, F32),
            pltpu.VMEM((LOW, HIGHS * LANES), BF16),
            pltpu.VMEM((LOW, 2048), BF16),
            pltpu.VMEM((2048, LANES), I32),
            pltpu.VMEM((block, lanes), BF16),
            pltpu.VMEM((block, lanes), F32),
            pltpu.VMEM((devices, CAP, lanes), BF16),
            pltpu.SemaphoreType.DMA(()),
            pltpu.SemaphoreType.DMA((HIGHS,)),
            pltpu.SemaphoreType.DMA((4,)),
            pltpu.SemaphoreType.DMA((groups,)),
        ],
        flops=2 * work,
    )(slab, old_level_one)

    level_two, answer = call(
        finish_kernel,
        (shape((256, lanes), F32), shape((devices, CAP + TOP, lanes), BF16)),
        [VMEM, HBM],
        (VMEM, HBM),
        [
            pltpu.VMEM((LANES, LANES), F32),
            pltpu.VMEM((devices, TOP, lanes), BF16),
            pltpu.SemaphoreType.DMA(()),
        ],
        alias={1: 1},
    )(shares, answer)
    returned = swap(answer, BOTH)
    residual, level_three = call(
        unpack_kernel,
        (shape((count, width), BF16), shape((owners * TOP, width), F32)),
        [VMEM, VMEM],
        (VMEM, VMEM),
        flops=2 * slots * count * width,
    )(back, returned.reshape(groups, owners, CAP + TOP, lanes))
    return (level_one, level_two, level_three, residual)


def solution(mesh):
    in_specs = (P(("dp", "cent"), None), P(("dp", "cent")), P("cent"), P(), P("cent", "dp"))
    out_specs = (P("cent", "dp"), P("cent", "dp"), P(), P(("dp", "cent"), None))
    return jax.shard_map(
        on_device, mesh=mesh, in_specs=in_specs, out_specs=out_specs, check_vma=False
    )
```

```python
import jax
import jax.numpy as jnp
from jax import lax
from jax.experimental import pallas as pl
from jax.experimental.pallas import tpu as pltpu
from jax.sharding import PartitionSpec as P

F32 = jnp.float32
BF16 = jnp.bfloat16
I32 = jnp.int32
LANES = 128
LOW = 512
HIGHS = 8
CAP = 32
HALF = 16
EXTRA = 8
TOP = 16
BOTH = ("dp", "cent")


def iota(shape, axis):
    return lax.broadcasted_iota(I32, shape, axis)


def dot(left, right):
    return jnp.dot(left, right, preferred_element_type=F32)


def dot_nt(left, right):
    return lax.dot_general(left, right, (((1,), (1,)), ((), ())), preferred_element_type=F32)


def lane_slice(at, width=LANES):
    return slice(at * width, (at + 1) * width)


HBM = pl.BlockSpec(memory_space=pltpu.HBM)
VMEM = pl.BlockSpec(memory_space=pltpu.VMEM)


def call(body, out_shape, ins, outs, scratch=(), flops=0, size=4 << 20, vmem=60 << 20, alias=None):
    return pl.pallas_call(
        body,
        out_shape=out_shape,
        in_specs=ins,
        out_specs=outs,
        scratch_shapes=list(scratch),
        input_output_aliases=alias or {},
        compiler_params=pltpu.CompilerParams(vmem_limit_bytes=vmem),
        cost_estimate=pl.CostEstimate(flops=flops, bytes_accessed=size, transcendentals=0),
    )


def pack_kernel(assign_hbm, points_hbm, send_hbm, back_ref, assign_ref, points_ref, send_ref, sems):
    owners = send_ref.shape[1]
    parts = send_ref.shape[0]
    count = points_ref.shape[0]
    load = pltpu.make_async_copy(assign_hbm, assign_ref, sems.at[0])
    load.start()
    loads = []
    for pair in range(parts // 2):
        at = lane_slice(pair, 2 * LANES)
        loads.append(
            pltpu.make_async_copy(points_hbm.at[:, at], points_ref.at[:, at], sems.at[1 + pair])
        )
        loads[-1].start()
    before = jnp.where(iota((count, count), 0) <= iota((count, count), 1), 1.0, 0.0).astype(BF16)
    same = jnp.where(iota((count, count), 0) == iota((count, count), 1), 1.0, 0.0).astype(BF16)
    load.wait()
    label = assign_ref[...]
    owner = lax.shift_right_logical(label, 12)
    local = label & 4095
    mine = iota((owners, count), 0) == owner
    mine_f = jnp.where(mine, 1.0, 0.0)
    running = dot(mine_f.astype(BF16), before)
    place = jnp.sum(running * mine_f, axis=0, keepdims=True).astype(I32) - 1
    slot = owner * CAP + place
    table = jnp.where(iota((owners * CAP, count), 0) == slot, 1.0, 0.0).astype(BF16)
    shift = (lax.axis_index("cent") % 8) * HALF
    line = iota((LANES, count), 0)
    row = iota((owners, EXTRA, LANES), 1)
    digits = [(lax.shift_right_logical(local, 6) + 1).astype(F32), ((local & 63) + 1).astype(F32)]
    digits = [(mine_f * digit).astype(BF16) for digit in digits]
    extra = jnp.zeros((owners, EXTRA, LANES), F32)
    for half in range(2):
        first = half * HALF
        inside = (place >= first) & (place < first + HALF)
        lane = jnp.where(inside, place - first + shift, -1)
        lane_table = jnp.where(line == lane, 1.0, 0.0).astype(BF16)
        for kind in range(2):
            found = dot_nt(digits[kind], lane_table)
            extra = jnp.where(row == 2 * kind + half, found[:, None, :], extra)
    extra = extra.astype(BF16)
    stores = []
    for part in range(parts):
        if part % 2 == 0:
            loads[part // 2].wait()
            both = dot(table, points_ref[:, lane_slice(part // 2, 2 * LANES)]).astype(BF16)
        rows = both[:, lane_slice(part % 2)]
        send_ref[part, :, 0:CAP, :] = rows.reshape(owners, CAP, LANES)
        send_ref[part, :, CAP : CAP + EXTRA, :] = extra
        stores.append(
            pltpu.make_async_copy(send_ref.at[part], send_hbm.at[part], sems.at[1 + parts // 2 + part])
        )
        stores[-1].start()
    back_ref[...] = dot_nt(same, table).astype(BF16)
    for store in stores:
        store.wait()


def slot_digits(slab_ref, digits_ref):
    rows = slab_ref[:, CAP : CAP + EXTRA, :].astype(F32).reshape(-1, LANES).astype(BF16)
    shape = (64, rows.shape[0])
    column, line = iota(shape, 1), iota(shape, 0)
    pick = (lax.shift_right_logical(column, 6) == (line & 15)) & (
        (column & 7) == lax.shift_right_logical(line, 4)
    )
    digits_ref[...] = dot(jnp.where(pick, 1.0, 0.0).astype(BF16), rows)


def across_lanes(digits_ref, at, count):
    found = []
    for part in range(count):
        high, low = digits_ref[pl.ds(at + part, 1), :], digits_ref[pl.ds(at + part + 32, 1), :]
        found.append((high * 64.0 + low).astype(I32) - 65)
    return found


def down_rows(digits_ref, at, count):
    same = iota((LANES, LANES), 0) == iota((LANES, LANES), 1)
    parts = []
    for part in range(count):
        high, low = digits_ref[pl.ds(at + part, 1), :], digits_ref[pl.ds(at + part + 32, 1), :]
        parts.append(
            jnp.concatenate([jnp.where(same, high, 0.0), jnp.where(same, low, 0.0)], axis=1)
        )
    left = jnp.concatenate(parts, axis=0).astype(BF16)
    right = jnp.where(iota((2 * LANES, LANES), 0) < LANES, 64.0, 1.0).astype(BF16)
    return dot(left, right).astype(I32) - 65


def low_table(labels):
    line = iota((LOW, LANES), 0)
    return jnp.concatenate(
        [jnp.where(line == (label & (LOW - 1)), 1.0, 0.0).astype(BF16) for label in labels], axis=1
    )


def masked(rows, high, which):
    return jnp.where(high == which, rows, 0.0).astype(BF16)


def counting(high):
    lane = iota(high.shape, 1)
    return jnp.where((high == (lane & 7)) & (lane < 16), 1.0, 0.0).astype(BF16)


def segments(total_ref, left_ref, high_ref, rows_of, digits_ref, steps):
    for step in range(steps):
        left_ref[:, lane_slice(step, 512)] = low_table(across_lanes(digits_ref, 4 * step, 4))
        high_ref[lane_slice(step, 512), :] = lax.shift_right_arithmetic(
            down_rows(digits_ref, 4 * step, 4), 9
        )
    left = left_ref[:, 0 : steps * 512]
    for pair in range(HIGHS // 2):
        right = []
        for step in range(steps):
            high, rows = high_ref[lane_slice(step, 512), :], rows_of(step)
            right.append(
                jnp.concatenate([masked(rows, high, 2 * pair + side) for side in range(2)], axis=1)
            )
        total_ref[:, lane_slice(pair, 2 * LANES)] = dot(left, jnp.concatenate(right, axis=0))
    total_ref[:, HIGHS * LANES :] = dot(left, counting(high_ref[0 : steps * 512, :]))


def add_segments(total_ref, digits_ref, at, rows):
    left = low_table(across_lanes(digits_ref, at, 2))
    high = lax.shift_right_arithmetic(down_rows(digits_ref, at, 2), 9)
    for pair in range(HIGHS // 2):
        right = jnp.concatenate([masked(rows, high, 2 * pair + side) for side in range(2)], axis=1)
        total_ref[:, lane_slice(pair, 2 * LANES)] += dot(left, right)
    total_ref[:, HIGHS * LANES :] += dot(left, counting(high))


def lower_rows(slab_ref, step):
    return slab_ref[lane_slice(step, 32), 0:HALF, :].reshape(512, LANES).astype(F32)


def upper_rows(slab_ref, group):
    return slab_ref[pl.ds(group * 16, 16), HALF:CAP, :].reshape(256, LANES).astype(F32)


def any_label(digits_ref, group):
    return jnp.max(digits_ref[pl.ds(16 + 2 * group, 2), :]) > 0.0


def parent_kernel(parent_ref, old_ref, total_ref, digits_ref):
    parent = parent_ref[...]
    digits_ref[0:32, :] = (lax.shift_right_logical(parent, 6) + 1).astype(F32)
    digits_ref[32:64, :] = ((parent & 63) + 1).astype(F32)
    total_ref[...] = jnp.zeros_like(total_ref)

    def step(at, carry):
        rows = old_ref[pl.ds(pl.multiple_of(at * 256, 256), 256), :].astype(F32)
        add_segments(total_ref, digits_ref, 2 * at, rows)
        return carry

    lax.fori_loop(0, old_ref.shape[0] // 256, step, 0)


def find_parents(digits_ref, parents_ref, table_ref, at, count):
    line = iota((LANES, LANES), 0)
    rows = [(digits_ref[pl.ds(at + n, 1), :], digits_ref[pl.ds(at + n + 32, 1), :]) for n in range(count)]
    left = [jnp.where(line == high.astype(I32) - 1, 1.0, 0.0).astype(BF16) for high, _ in rows]
    found = dot(table_ref[...], jnp.concatenate(left, axis=1))
    for n in range(count):
        chosen = jnp.where((line & 63) == rows[n][1].astype(I32) - 1, found[:, lane_slice(n)], 0.0)
        parents_ref[pl.ds(at + n, 1), :] = jnp.sum(chosen[0:64], axis=0, keepdims=True)
        parents_ref[pl.ds(at + n + 32, 1), :] = jnp.sum(chosen[64:128], axis=0, keepdims=True)


def upper_kernel(
    slab_ref, table_ref, top_ref, start_hbm, send_hbm,
    digits_ref, parents_ref, total_ref, left_ref, high_ref, start_ref, send_ref, right_ref, sems,
):
    load = pltpu.make_async_copy(start_hbm, start_ref, sems.at[0])
    load.start()
    slot_digits(slab_ref, digits_ref)
    for step in range(4):
        find_parents(digits_ref, parents_ref, table_ref, 4 * step, 4)
    segments(total_ref, left_ref, high_ref, lambda step: lower_rows(slab_ref, step), parents_ref, 4)

    def more(group, carry):
        @pl.when(any_label(digits_ref, group))
        def _():
            find_parents(digits_ref, parents_ref, table_ref, 16 + 2 * group, 2)
            add_segments(total_ref, parents_ref, 16 + 2 * group, upper_rows(slab_ref, group))

        return carry

    lax.fori_loop(0, slab_ref.shape[0] // 16, more, 0)
    load.wait()
    at = slice(HIGHS * LANES, (HIGHS + 1) * LANES)
    weights = total_ref[:, at] + start_ref[:, at]
    coarse = weights.astype(BF16).astype(F32)
    fine = weights - coarse
    lane = iota((LOW, LANES), 1)
    tops = []
    for high in range(HIGHS):
        mass = (total_ref[:, lane_slice(high)] + start_ref[:, lane_slice(high)]).astype(BF16)
        for half in range(2):
            send_ref[2 * high + half, 0:256, :] = mass[half * 256 : (half + 1) * 256]
        right_ref[lane_slice(high, LOW), 0:LANES] = mass
        right_ref[lane_slice(high, LOW), LANES:] = jnp.where(
            lane == high, coarse, jnp.where(lane == high + 8, fine, 0.0)
        ).astype(BF16)
        for part in range(4):
            hit = iota((256, LANES), 0) == top_ref[high * 4 + part : high * 4 + part + 1, :]
            tops.append(jnp.where(hit, 1.0, 0.0).astype(BF16))
    tops = dot(jnp.concatenate(tops, axis=1), right_ref[...])
    top_mass = tops[:, :LANES].astype(BF16)
    top_weight = jnp.sum(tops[:, LANES:].T[0:16], axis=0, keepdims=True)
    top_coarse = top_weight.astype(BF16).astype(F32)
    top_fine = top_weight - top_coarse
    coarse_t, fine_t = coarse.T, fine.T
    stores = []
    for owner in range(send_ref.shape[0]):
        send_ref[owner, 256:272, :] = top_mass[owner * TOP : (owner + 1) * TOP]
        high, from_lane = owner // 2, (owner % 2) * 256
        rows = []
        for source, line_at, lane_at in (
            (coarse_t, high, from_lane),
            (fine_t, high, from_lane),
            (top_coarse, 0, 0),
            (top_fine, 0, 0),
        ):
            for half in range(2):
                first = lane_at + half * LANES
                rows.append(source[line_at : line_at + 1, first : first + LANES])
        send_ref[owner, 272:280, :] = jnp.concatenate(rows, axis=0).astype(BF16)
        if owner % 4 == 3:
            part = pl.ds(owner - 3, 4)
            stores.append(
                pltpu.make_async_copy(send_ref.at[part], send_hbm.at[part], sems.at[1 + owner // 4])
            )
            stores[-1].start()
    for store in stores:
        store.wait()


def level_kernel(
    slab_ref, old_hbm, level_hbm, residual_hbm,
    digits_ref, total_ref, table_ref, left_ref, high_ref, old_ref, level_ref, residual_ref,
    load_sem, level_sems, low_sems, up_sems,
):
    load = pltpu.make_async_copy(old_hbm, old_ref, load_sem)
    load.start()
    slot_digits(slab_ref, digits_ref)
    segments(total_ref, left_ref, high_ref, lambda step: lower_rows(slab_ref, step), digits_ref, 4)
    groups = slab_ref.shape[0] // 16

    def more(group, carry):
        @pl.when(any_label(digits_ref, group))
        def _():
            add_segments(total_ref, digits_ref, 16 + 2 * group, upper_rows(slab_ref, group))

        return carry

    lax.fori_loop(0, groups, more, 0)
    load.wait()
    inverse = 1.0 / (total_ref[:, HIGHS * LANES :] + 1.0)
    stores = []
    for high in range(HIGHS):
        lines = lane_slice(high, LOW)
        mass = total_ref[:, lane_slice(high)] + old_ref[lines, :].astype(F32)
        level = mass * jnp.broadcast_to(inverse[:, high : high + 1], mass.shape)
        level_ref[lines, :] = level
        table_ref[:, lane_slice(high)] = level.astype(BF16)
        stores.append(
            pltpu.make_async_copy(level_ref.at[lines], level_hbm.at[lines], level_sems.at[high])
        )
        stores[-1].start()

    def subtract(at, count, rows):
        label = down_rows(digits_ref, at, count)
        low = label & (LOW - 1)
        high = lax.shift_right_arithmetic(label, 9)
        lane = iota(label.shape, 1)
        left = jnp.concatenate(
            [
                jnp.where(low == lane + part * LANES, 1.0, 0.0).astype(BF16)
                for part in range(LOW // LANES)
            ],
            axis=1,
        )
        for pair in range(HIGHS // 2):
            found = dot(left, table_ref[:, lane_slice(pair, 2 * LANES)])
            for side in range(2):
                rows -= jnp.where(high == 2 * pair + side, found[:, lane_slice(side)], 0.0)
        return rows.astype(BF16)

    for step in range(4):
        sources = lane_slice(step, 32)
        residual_ref[sources, 0:HALF, :] = subtract(
            4 * step, 4, lower_rows(slab_ref, step)
        ).reshape(32, HALF, LANES)
        part = (sources, slice(0, HALF))
        stores.append(
            pltpu.make_async_copy(residual_ref.at[part], residual_hbm.at[part], low_sems.at[step])
        )
        stores[-1].start()

    def upper_copy(group):
        part = (pl.ds(group * 16, 16), pl.ds(HALF, HALF))
        return pltpu.make_async_copy(residual_ref.at[part], residual_hbm.at[part], up_sems.at[group])

    def finish(group, carry):
        sources = pl.ds(group * 16, 16)
        live = any_label(digits_ref, group)

        @pl.when(live)
        def _():
            residual_ref[sources, HALF:CAP, :] = subtract(
                16 + 2 * group, 2, upper_rows(slab_ref, group)
            ).reshape(16, HALF, LANES)

        @pl.when(jnp.logical_not(live))
        def _():
            residual_ref[sources, HALF:CAP, :] = slab_ref[sources, HALF:CAP, :]

        upper_copy(group).start()
        return carry

    lax.fori_loop(0, groups, finish, 0)
    for store in stores:
        store.wait()

    def settle(group, carry):
        upper_copy(group).wait()
        return carry

    lax.fori_loop(0, groups, settle, 0)


def finish_kernel(parts_ref, send_in, level_ref, send_hbm, column_ref, top_ref, sem):
    total = parts_ref[0].astype(F32)
    for source in range(1, parts_ref.shape[0]):
        total += parts_ref[source].astype(F32)
    tail = total[272:280].T
    me = lax.axis_index("cent")
    chosen = jnp.where(me < 8, tail[:, 4:5] + tail[:, 6:7], tail[:, 5:6] + tail[:, 7:8])
    column_ref[...] = jnp.broadcast_to(chosen, (LANES, LANES))
    weight = column_ref[pl.ds(pl.multiple_of((me % 8) * TOP, TOP), TOP), :]
    top = (total[256:272] / weight).astype(BF16)
    top_ref[...] = jnp.broadcast_to(top[None], top_ref.shape)
    store = pltpu.make_async_copy(top_ref, send_hbm.at[:, pl.ds(CAP, TOP), :], sem)
    store.start()
    for half in range(2):
        weight = tail[:, half : half + 1] + tail[:, half + 2 : half + 3]
        lines = slice(half * LANES, (half + 1) * LANES)
        level_ref[lines, :] = total[lines] / jnp.broadcast_to(weight, (LANES, LANES))
    store.wait()


def unpack_kernel(back_ref, returned_ref, residual_ref, level_ref):
    groups, owners, rows, lanes = returned_ref.shape
    for pair in range(groups // 2):
        right = jnp.concatenate(
            [
                returned_ref[2 * pair + side, :, 0:CAP, :].reshape(owners * CAP, lanes)
                for side in range(2)
            ],
            axis=1,
        )
        residual_ref[:, lane_slice(pair, 2 * lanes)] = dot(back_ref[...], right).astype(BF16)
    for group in range(groups):
        top = returned_ref[group, :, CAP:rows, :].astype(F32)
        level_ref[:, lane_slice(group)] = top.reshape(owners * TOP, lanes)


def shape(dims, kind):
    return jax.ShapeDtypeStruct(dims, kind)


def swap(value, axes):
    return lax.all_to_all(value, axes, split_axis=0, concat_axis=0, tiled=True)


def on_device(points, assign, parent_one, parent_two, old_level_one):
    count, width = points.shape
    owners = lax.axis_size("cent")
    groups = lax.axis_size("dp")
    devices = owners * groups
    block, lanes = old_level_one.shape
    slots = owners * CAP
    rows = CAP + EXTRA
    total_dims = (LOW, (HIGHS + 1) * LANES)
    work = 2 * LOW * block * (HIGHS + 1) * LANES

    send, back = call(
        pack_kernel,
        (shape((groups, owners, rows, lanes), BF16), shape((count, slots), BF16)),
        [HBM, HBM],
        (HBM, VMEM),
        [
            pltpu.VMEM((1, count), I32),
            pltpu.VMEM((count, width), BF16),
            pltpu.VMEM((groups, owners, rows, lanes), BF16),
            pltpu.SemaphoreType.DMA((1 + groups // 2 + groups,)),
        ],
        flops=2 * slots * count * width,
    )(assign.reshape(1, count), points)
    slab = swap(send.reshape(devices, rows, lanes), BOTH)

    start = call(
        parent_kernel,
        shape(total_dims, F32),
        [VMEM, VMEM],
        VMEM,
        [pltpu.VMEM((64, LANES), F32)],
        flops=work,
    )(parent_one.reshape(block // LANES, LANES), old_level_one)
    grid = parent_one.reshape(64, 64).T
    table = jnp.concatenate([lax.shift_right_logical(grid, 6), grid & 63], axis=0) + 1
    table = jnp.pad(table, ((0, 0), (0, 64))).astype(BF16)

    share = call(
        upper_kernel,
        shape((owners, 280, lanes), BF16),
        [VMEM, VMEM, VMEM, HBM],
        HBM,
        [
            pltpu.VMEM((64, LANES), F32),
            pltpu.VMEM((64, LANES), F32),
            pltpu.VMEM(total_dims, F32),
            pltpu.VMEM((LOW, 2048), BF16),
            pltpu.VMEM((2048, LANES), I32),
            pltpu.VMEM(total_dims, F32),
            pltpu.VMEM((owners, 280, lanes), BF16),
            pltpu.VMEM((HIGHS * LOW, 2 * LANES), BF16),
            pltpu.SemaphoreType.DMA((5,)),
        ],
        flops=work,
    )(slab, table, parent_two.reshape(-1, LANES), start)
    shares = swap(share, "cent")

    level_one, answer = call(
        level_kernel,
        (shape((block, lanes), F32), shape((devices, CAP + TOP, lanes), BF16)),
        [VMEM, HBM],
        (HBM, HBM),
        [
            pltpu.VMEM((64, LANES), F32),
            pltpu.VMEM(total_dims, F32),
            pltpu.VMEM((LOW, HIGHS * LANES), BF16),
            pltpu.VMEM((LOW, 2048), BF16),
            pltpu.VMEM((2048, LANES), I32),
            pltpu.VMEM((block, lanes), BF16),
            pltpu.VMEM((block, lanes), F32),
            pltpu.VMEM((devices, CAP, lanes), BF16),
            pltpu.SemaphoreType.DMA(()),
            pltpu.SemaphoreType.DMA((HIGHS,)),
            pltpu.SemaphoreType.DMA((4,)),
            pltpu.SemaphoreType.DMA((groups,)),
        ],
        flops=2 * work,
    )(slab, old_level_one)

    level_two, answer = call(
        finish_kernel,
        (shape((256, lanes), F32), shape((devices, CAP + TOP, lanes), BF16)),
        [VMEM, HBM],
        (VMEM, HBM),
        [
            pltpu.VMEM((LANES, LANES), F32),
            pltpu.VMEM((devices, TOP, lanes), BF16),
            pltpu.SemaphoreType.DMA(()),
        ],
        alias={1: 1},
    )(shares, answer)
    returned = swap(answer, BOTH)
    residual, level_three = call(
        unpack_kernel,
        (shape((count, width), BF16), shape((owners * TOP, width), F32)),
        [VMEM, VMEM],
        (VMEM, VMEM),
        flops=2 * slots * count * width,
    )(back, returned.reshape(groups, owners, CAP + TOP, lanes))
    return (level_one, level_two, level_three, residual)


def solution(mesh):
    in_specs = (P(("dp", "cent"), None), P(("dp", "cent")), P("cent"), P(), P("cent", "dp"))
    out_specs = (P("cent", "dp"), P("cent", "dp"), P(), P(("dp", "cent"), None))
    return jax.shard_map(
        on_device, mesh=mesh, in_specs=in_specs, out_specs=out_specs, check_vma=False
    )
```

```python
import jax
import jax.numpy as jnp
from jax import lax
from jax.experimental import pallas as pl
from jax.experimental.pallas import tpu as pltpu
from jax.sharding import PartitionSpec as P

F32 = jnp.float32
BF16 = jnp.bfloat16
I32 = jnp.int32
LANES = 128
LOW = 512
HIGHS = 8
CAP = 32
HALF = 16
EXTRA = 8
TOP = 16
BOTH = ("dp", "cent")


def iota(shape, axis):
    return lax.broadcasted_iota(I32, shape, axis)


def dot(left, right):
    return jnp.dot(left, right, preferred_element_type=F32)


def dot_nt(left, right):
    return lax.dot_general(left, right, (((1,), (1,)), ((), ())), preferred_element_type=F32)


def lane_slice(at, width=LANES):
    return slice(at * width, (at + 1) * width)


HBM = pl.BlockSpec(memory_space=pltpu.HBM)
VMEM = pl.BlockSpec(memory_space=pltpu.VMEM)


FULL = 62_900_000
LESS = 62_100_000
LEAST = 61_100_000


def call(body, out_shape, ins, outs, vmem, scratch=(), flops=0, size=4 << 20, alias=None):
    return pl.pallas_call(
        body,
        out_shape=out_shape,
        in_specs=ins,
        out_specs=outs,
        scratch_shapes=list(scratch),
        input_output_aliases=alias or {},
        compiler_params=pltpu.CompilerParams(vmem_limit_bytes=vmem),
        cost_estimate=pl.CostEstimate(flops=flops, bytes_accessed=size, transcendentals=0),
    )


def pack_kernel(
    assign_hbm, points_hbm, send_hbm, back_hbm, assign_ref, points_ref, send_ref, back_ref, sems
):
    owners = send_ref.shape[1]
    parts = send_ref.shape[0]
    count = points_ref.shape[0]
    load = pltpu.make_async_copy(assign_hbm, assign_ref, sems.at[0])
    load.start()
    loads = []
    for pair in range(parts // 2):
        at = lane_slice(pair, 2 * LANES)
        loads.append(
            pltpu.make_async_copy(points_hbm.at[:, at], points_ref.at[:, at], sems.at[1 + pair])
        )
        loads[-1].start()
    before = jnp.where(iota((count, count), 0) <= iota((count, count), 1), 1.0, 0.0).astype(BF16)
    same = jnp.where(iota((count, count), 0) == iota((count, count), 1), 1.0, 0.0).astype(BF16)
    load.wait()
    label = assign_ref[...]
    owner = lax.shift_right_logical(label, 12)
    local = label & 4095
    mine = iota((owners, count), 0) == owner
    mine_f = jnp.where(mine, 1.0, 0.0)
    running = dot(mine_f.astype(BF16), before)
    place = jnp.sum(running * mine_f, axis=0, keepdims=True).astype(I32) - 1
    slot = owner * CAP + place
    table = jnp.where(iota((owners * CAP, count), 0) == slot, 1.0, 0.0).astype(BF16)
    shift = (lax.axis_index("cent") % 8) * HALF
    line = iota((LANES, count), 0)
    row = iota((owners, EXTRA, LANES), 1)
    digits = [(lax.shift_right_logical(local, 6) + 1).astype(F32), ((local & 63) + 1).astype(F32)]
    digits = [(mine_f * digit).astype(BF16) for digit in digits]
    extra = jnp.zeros((owners, EXTRA, LANES), F32)
    for half in range(2):
        first = half * HALF
        inside = (place >= first) & (place < first + HALF)
        lane = jnp.where(inside, place - first + shift, -1)
        lane_table = jnp.where(line == lane, 1.0, 0.0).astype(BF16)
        for kind in range(2):
            found = dot_nt(digits[kind], lane_table)
            extra = jnp.where(row == 2 * kind + half, found[:, None, :], extra)
    extra = extra.astype(BF16)
    stores = []
    for part in range(parts):
        if part % 2 == 0:
            loads[part // 2].wait()
            both = dot(table, points_ref[:, lane_slice(part // 2, 2 * LANES)]).astype(BF16)
        rows = both[:, lane_slice(part % 2)]
        send_ref[part, :, 0:CAP, :] = rows.reshape(owners, CAP, LANES)
        send_ref[part, :, CAP : CAP + EXTRA, :] = extra
        stores.append(
            pltpu.make_async_copy(send_ref.at[part], send_hbm.at[part], sems.at[1 + parts // 2 + part])
        )
        stores[-1].start()
        if part == 0:
            back_ref[...] = dot_nt(same, table).astype(BF16)
            stores.append(pltpu.make_async_copy(back_ref, back_hbm, sems.at[1 + parts // 2 + parts]))
            stores[-1].start()
    for store in stores:
        store.wait()


def slot_digits(slab_ref, digits_ref):
    rows = slab_ref[:, CAP : CAP + EXTRA, :].astype(F32).reshape(-1, LANES).astype(BF16)
    shape = (64, rows.shape[0])
    column, line = iota(shape, 1), iota(shape, 0)
    pick = (lax.shift_right_logical(column, 6) == (line & 15)) & (
        (column & 7) == lax.shift_right_logical(line, 4)
    )
    digits_ref[...] = dot(jnp.where(pick, 1.0, 0.0).astype(BF16), rows)


def across_lanes(digits_ref, at, count):
    found = []
    for part in range(count):
        high, low = digits_ref[pl.ds(at + part, 1), :], digits_ref[pl.ds(at + part + 32, 1), :]
        found.append((high * 64.0 + low).astype(I32) - 65)
    return found


def down_rows(digits_ref, at, count):
    same = iota((LANES, LANES), 0) == iota((LANES, LANES), 1)
    parts = []
    for part in range(count):
        high, low = digits_ref[pl.ds(at + part, 1), :], digits_ref[pl.ds(at + part + 32, 1), :]
        parts.append(
            jnp.concatenate([jnp.where(same, high, 0.0), jnp.where(same, low, 0.0)], axis=1)
        )
    left = jnp.concatenate(parts, axis=0).astype(BF16)
    right = jnp.where(iota((2 * LANES, LANES), 0) < LANES, 64.0, 1.0).astype(BF16)
    return dot(left, right).astype(I32) - 65


def low_table(labels):
    line = iota((LOW, LANES), 0)
    return jnp.concatenate(
        [jnp.where(line == (label & (LOW - 1)), 1.0, 0.0).astype(BF16) for label in labels], axis=1
    )


def masked(rows, high, which):
    return jnp.where(high == which, rows, 0.0).astype(BF16)


def counting(high):
    lane = iota(high.shape, 1)
    return jnp.where((high == (lane & 7)) & (lane < 16), 1.0, 0.0).astype(BF16)


def segments(total_ref, left_ref, high_ref, rows_of, digits_ref, steps):
    for step in range(steps):
        left_ref[:, lane_slice(step, 512)] = low_table(across_lanes(digits_ref, 4 * step, 4))
        high_ref[lane_slice(step, 512), :] = lax.shift_right_arithmetic(
            down_rows(digits_ref, 4 * step, 4), 9
        )
    left = left_ref[:, 0 : steps * 512]
    for pair in range(HIGHS // 2):
        right = []
        for step in range(steps):
            high, rows = high_ref[lane_slice(step, 512), :], rows_of(step)
            right.append(
                jnp.concatenate([masked(rows, high, 2 * pair + side) for side in range(2)], axis=1)
            )
        total_ref[:, lane_slice(pair, 2 * LANES)] = dot(left, jnp.concatenate(right, axis=0))
    total_ref[:, HIGHS * LANES :] = dot(left, counting(high_ref[0 : steps * 512, :]))


def add_segments(total_ref, digits_ref, at, rows):
    left = low_table(across_lanes(digits_ref, at, 2))
    high = lax.shift_right_arithmetic(down_rows(digits_ref, at, 2), 9)
    for pair in range(HIGHS // 2):
        right = jnp.concatenate([masked(rows, high, 2 * pair + side) for side in range(2)], axis=1)
        total_ref[:, lane_slice(pair, 2 * LANES)] += dot(left, right)
    total_ref[:, HIGHS * LANES :] += dot(left, counting(high))


def lower_rows(slab_ref, step):
    return slab_ref[lane_slice(step, 32), 0:HALF, :].reshape(512, LANES).astype(F32)


def upper_rows(slab_ref, group):
    return slab_ref[pl.ds(group * 16, 16), HALF:CAP, :].reshape(256, LANES).astype(F32)


def mark_live(digits_ref, live_ref):
    for group in range(live_ref.shape[0]):
        most = jnp.max(digits_ref[16 + 2 * group : 18 + 2 * group, :])
        live_ref[group] = jnp.where(most > 0.0, 1, 0)


def parent_kernel(parent_ref, old_ref, total_ref, digits_ref, left_ref, high_ref):
    parent = parent_ref[...]
    digits_ref[0:32, :] = (lax.shift_right_logical(parent, 6) + 1).astype(F32)
    digits_ref[32:64, :] = ((parent & 63) + 1).astype(F32)
    segments(
        total_ref,
        left_ref,
        high_ref,
        lambda step: old_ref[lane_slice(step, 512), :].astype(F32),
        digits_ref,
        old_ref.shape[0] // 512,
    )


def find_parents(digits_ref, parents_ref, table_ref, at, count):
    line = iota((LANES, LANES), 0)
    rows = [(digits_ref[pl.ds(at + n, 1), :], digits_ref[pl.ds(at + n + 32, 1), :]) for n in range(count)]
    left = [jnp.where(line == high.astype(I32) - 1, 1.0, 0.0).astype(BF16) for high, _ in rows]
    found = dot(table_ref[...], jnp.concatenate(left, axis=1))
    for n in range(count):
        chosen = jnp.where((line & 63) == rows[n][1].astype(I32) - 1, found[:, lane_slice(n)], 0.0)
        parents_ref[pl.ds(at + n, 1), :] = jnp.sum(chosen[0:64], axis=0, keepdims=True)
        parents_ref[pl.ds(at + n + 32, 1), :] = jnp.sum(chosen[64:128], axis=0, keepdims=True)


def upper_kernel(
    slab_ref, table_ref, top_ref, start_hbm, send_hbm,
    digits_ref, parents_ref, total_ref, left_ref, high_ref, start_ref, send_ref, right_ref, live_ref, sems,
):
    load = pltpu.make_async_copy(start_hbm, start_ref, sems.at[0])
    load.start()
    slot_digits(slab_ref, digits_ref)
    mark_live(digits_ref, live_ref)
    for step in range(4):
        find_parents(digits_ref, parents_ref, table_ref, 4 * step, 4)
    segments(total_ref, left_ref, high_ref, lambda step: lower_rows(slab_ref, step), parents_ref, 4)

    def more(group, carry):
        @pl.when(live_ref[group] > 0)
        def _():
            find_parents(digits_ref, parents_ref, table_ref, 16 + 2 * group, 2)
            add_segments(total_ref, parents_ref, 16 + 2 * group, upper_rows(slab_ref, group))

        return carry

    lax.fori_loop(0, slab_ref.shape[0] // 16, more, 0)
    load.wait()
    at = slice(HIGHS * LANES, (HIGHS + 1) * LANES)
    weights = total_ref[:, at] + start_ref[:, at]
    coarse = weights.astype(BF16).astype(F32)
    fine = weights - coarse
    lane = iota((LOW, LANES), 1)
    tops = []
    for high in range(HIGHS):
        mass = (total_ref[:, lane_slice(high)] + start_ref[:, lane_slice(high)]).astype(BF16)
        for half in range(2):
            send_ref[2 * high + half, 0:256, :] = mass[half * 256 : (half + 1) * 256]
        right_ref[lane_slice(high, LOW), 0:LANES] = mass
        right_ref[lane_slice(high, LOW), LANES:] = jnp.where(
            lane == high, coarse, jnp.where(lane == high + 8, fine, 0.0)
        ).astype(BF16)
        for part in range(4):
            hit = iota((256, LANES), 0) == top_ref[high * 4 + part : high * 4 + part + 1, :]
            tops.append(jnp.where(hit, 1.0, 0.0).astype(BF16))
    tops = dot(jnp.concatenate(tops, axis=1), right_ref[...])
    top_mass = tops[:, :LANES].astype(BF16)
    top_weight = jnp.sum(tops[:, LANES:].T[0:16], axis=0, keepdims=True)
    top_coarse = top_weight.astype(BF16).astype(F32)
    top_fine = top_weight - top_coarse
    coarse_t, fine_t = coarse.T, fine.T
    stores = []
    for owner in range(send_ref.shape[0]):
        send_ref[owner, 256:272, :] = top_mass[owner * TOP : (owner + 1) * TOP]
        high, from_lane = owner // 2, (owner % 2) * 256
        rows = []
        for source, line_at, lane_at in (
            (coarse_t, high, from_lane),
            (fine_t, high, from_lane),
            (top_coarse, 0, 0),
            (top_fine, 0, 0),
        ):
            for half in range(2):
                first = lane_at + half * LANES
                rows.append(source[line_at : line_at + 1, first : first + LANES])
        send_ref[owner, 272:280, :] = jnp.concatenate(rows, axis=0).astype(BF16)
        if owner % 4 == 3:
            part = pl.ds(owner - 3, 4)
            stores.append(
                pltpu.make_async_copy(send_ref.at[part], send_hbm.at[part], sems.at[1 + owner // 4])
            )
            stores[-1].start()
    for store in stores:
        store.wait()


def level_kernel(
    slab_ref, old_hbm, level_hbm, residual_hbm,
    digits_ref, total_ref, table_ref, left_ref, high_ref, old_ref, level_ref, residual_ref, live_ref,
    load_sem, level_sems, low_sems, up_sems,
):
    load = pltpu.make_async_copy(old_hbm, old_ref, load_sem)
    load.start()
    slot_digits(slab_ref, digits_ref)
    mark_live(digits_ref, live_ref)
    segments(total_ref, left_ref, high_ref, lambda step: lower_rows(slab_ref, step), digits_ref, 4)
    groups = slab_ref.shape[0] // 16

    def more(group, carry):
        @pl.when(live_ref[group] > 0)
        def _():
            add_segments(total_ref, digits_ref, 16 + 2 * group, upper_rows(slab_ref, group))

        return carry

    lax.fori_loop(0, groups, more, 0)
    load.wait()
    inverse = 1.0 / (total_ref[:, HIGHS * LANES :] + 1.0)
    stores = []
    for high in range(HIGHS):
        lines = lane_slice(high, LOW)
        mass = total_ref[:, lane_slice(high)] + old_ref[lines, :].astype(F32)
        level = mass * jnp.broadcast_to(inverse[:, high : high + 1], mass.shape)
        level_ref[lines, :] = level
        table_ref[:, lane_slice(high)] = level.astype(BF16)
        stores.append(
            pltpu.make_async_copy(level_ref.at[lines], level_hbm.at[lines], level_sems.at[high])
        )
        stores[-1].start()

    def subtract(at, count, rows):
        label = down_rows(digits_ref, at, count)
        low = label & (LOW - 1)
        high = lax.shift_right_arithmetic(label, 9)
        lane = iota(label.shape, 1)
        left = jnp.concatenate(
            [
                jnp.where(low == lane + part * LANES, 1.0, 0.0).astype(BF16)
                for part in range(LOW // LANES)
            ],
            axis=1,
        )
        for pair in range(HIGHS // 2):
            found = dot(left, table_ref[:, lane_slice(pair, 2 * LANES)])
            for side in range(2):
                rows -= jnp.where(high == 2 * pair + side, found[:, lane_slice(side)], 0.0)
        return rows.astype(BF16)

    for step in range(4):
        sources = lane_slice(step, 32)
        residual_ref[sources, 0:HALF, :] = subtract(
            4 * step, 4, lower_rows(slab_ref, step)
        ).reshape(32, HALF, LANES)
        part = (sources, slice(0, HALF))
        stores.append(
            pltpu.make_async_copy(residual_ref.at[part], residual_hbm.at[part], low_sems.at[step])
        )
        stores[-1].start()

    def upper_copy(group):
        part = (pl.ds(group * 16, 16), pl.ds(HALF, HALF))
        return pltpu.make_async_copy(residual_ref.at[part], residual_hbm.at[part], up_sems.at[group])

    def finish(group, carry):
        sources = pl.ds(group * 16, 16)
        @pl.when(live_ref[group] > 0)
        def _():
            residual_ref[sources, HALF:CAP, :] = subtract(
                16 + 2 * group, 2, upper_rows(slab_ref, group)
            ).reshape(16, HALF, LANES)

        @pl.when(live_ref[group] == 0)
        def _():
            residual_ref[sources, HALF:CAP, :] = slab_ref[sources, HALF:CAP, :]

        upper_copy(group).start()
        return carry

    lax.fori_loop(0, groups, finish, 0)
    for store in stores:
        store.wait()

    def settle(group, carry):
        upper_copy(group).wait()
        return carry

    lax.fori_loop(0, groups, settle, 0)


def finish_kernel(parts_ref, send_in, level_ref, send_hbm, column_ref, top_ref, sem):
    total = parts_ref[0].astype(F32)
    for source in range(1, parts_ref.shape[0]):
        total += parts_ref[source].astype(F32)
    tail = total[272:280].T
    me = lax.axis_index("cent")
    chosen = jnp.where(me < 8, tail[:, 4:5] + tail[:, 6:7], tail[:, 5:6] + tail[:, 7:8])
    column_ref[...] = jnp.broadcast_to(chosen, (LANES, LANES))
    weight = column_ref[pl.ds(pl.multiple_of((me % 8) * TOP, TOP), TOP), :]
    top = (total[256:272] / weight).astype(BF16)
    top_ref[...] = jnp.broadcast_to(top[None], top_ref.shape)
    store = pltpu.make_async_copy(top_ref, send_hbm.at[:, pl.ds(CAP, TOP), :], sem)
    store.start()
    for half in range(2):
        weight = tail[:, half : half + 1] + tail[:, half + 2 : half + 3]
        lines = slice(half * LANES, (half + 1) * LANES)
        level_ref[lines, :] = total[lines] / jnp.broadcast_to(weight, (LANES, LANES))
    store.wait()


def unpack_kernel(back_ref, returned_ref, residual_ref, level_ref):
    groups, owners, rows, lanes = returned_ref.shape
    for pair in range(groups // 2):
        right = jnp.concatenate(
            [
                returned_ref[2 * pair + side, :, 0:CAP, :].reshape(owners * CAP, lanes)
                for side in range(2)
            ],
            axis=1,
        )
        residual_ref[:, lane_slice(pair, 2 * lanes)] = dot(back_ref[...], right).astype(BF16)
    for group in range(groups):
        top = returned_ref[group, :, CAP:rows, :].astype(F32)
        level_ref[:, lane_slice(group)] = top.reshape(owners * TOP, lanes)


def shape(dims, kind):
    return jax.ShapeDtypeStruct(dims, kind)


def swap(value, axes):
    return lax.all_to_all(value, axes, split_axis=0, concat_axis=0, tiled=True)


def on_device(points, assign, parent_one, parent_two, old_level_one):
    count, width = points.shape
    owners = lax.axis_size("cent")
    groups = lax.axis_size("dp")
    devices = owners * groups
    block, lanes = old_level_one.shape
    slots = owners * CAP
    rows = CAP + EXTRA
    total_dims = (LOW, (HIGHS + 1) * LANES)
    work = 2 * LOW * block * (HIGHS + 1) * LANES

    send, back = call(
        pack_kernel,
        (shape((groups, owners, rows, lanes), BF16), shape((count, slots), BF16)),
        [HBM, HBM],
        (HBM, HBM),
        FULL,
        [
            pltpu.VMEM((1, count), I32),
            pltpu.VMEM((count, width), BF16),
            pltpu.VMEM((groups, owners, rows, lanes), BF16),
            pltpu.VMEM((count, slots), BF16),
            pltpu.SemaphoreType.DMA((2 + groups // 2 + groups,)),
        ],
        flops=2 * slots * count * width,
    )(assign.reshape(1, count), points)
    slab = swap(send.reshape(devices, rows, lanes), BOTH)

    start = call(
        parent_kernel,
        shape(total_dims, F32),
        [VMEM, VMEM],
        VMEM,
        FULL,
        [
            pltpu.VMEM((64, LANES), F32),
            pltpu.VMEM((LOW, block), BF16),
            pltpu.VMEM((block, LANES), I32),
        ],
        flops=work,
    )(parent_one.reshape(block // LANES, LANES), old_level_one)
    grid = parent_one.reshape(64, 64).T
    table = jnp.concatenate([lax.shift_right_logical(grid, 6), grid & 63], axis=0) + 1
    table = jnp.pad(table, ((0, 0), (0, 64))).astype(BF16)

    share = call(
        upper_kernel,
        shape((owners, 280, lanes), BF16),
        [VMEM, VMEM, VMEM, HBM],
        HBM,
        LESS,
        [
            pltpu.VMEM((64, LANES), F32),
            pltpu.VMEM((64, LANES), F32),
            pltpu.VMEM(total_dims, F32),
            pltpu.VMEM((LOW, 2048), BF16),
            pltpu.VMEM((2048, LANES), I32),
            pltpu.VMEM(total_dims, F32),
            pltpu.VMEM((owners, 280, lanes), BF16),
            pltpu.VMEM((HIGHS * LOW, 2 * LANES), BF16),
            pltpu.SMEM((groups,), I32),
            pltpu.SemaphoreType.DMA((5,)),
        ],
        flops=work,
    )(slab, table, parent_two.reshape(-1, LANES), start)
    shares = swap(share, "cent")

    level_one, answer = call(
        level_kernel,
        (shape((block, lanes), F32), shape((devices, CAP + TOP, lanes), BF16)),
        [VMEM, HBM],
        (HBM, HBM),
        LEAST,
        [
            pltpu.VMEM((64, LANES), F32),
            pltpu.VMEM(total_dims, F32),
            pltpu.VMEM((LOW, HIGHS * LANES), BF16),
            pltpu.VMEM((LOW, 2048), BF16),
            pltpu.VMEM((2048, LANES), I32),
            pltpu.VMEM((block, lanes), BF16),
            pltpu.VMEM((block, lanes), F32),
            pltpu.VMEM((devices, CAP, lanes), BF16),
            pltpu.SMEM((groups,), I32),
            pltpu.SemaphoreType.DMA(()),
            pltpu.SemaphoreType.DMA((HIGHS,)),
            pltpu.SemaphoreType.DMA((4,)),
            pltpu.SemaphoreType.DMA((groups,)),
        ],
        flops=2 * work,
    )(slab, old_level_one)

    level_two, answer = call(
        finish_kernel,
        (shape((256, lanes), F32), shape((devices, CAP + TOP, lanes), BF16)),
        [VMEM, HBM],
        (VMEM, HBM),
        LESS,
        [
            pltpu.VMEM((LANES, LANES), F32),
            pltpu.VMEM((devices, TOP, lanes), BF16),
            pltpu.SemaphoreType.DMA(()),
        ],
        alias={1: 1},
    )(shares, answer)
    returned = swap(answer, BOTH)
    residual, level_three = call(
        unpack_kernel,
        (shape((count, width), BF16), shape((owners * TOP, width), F32)),
        [VMEM, VMEM],
        (VMEM, VMEM),
        LESS,
        flops=2 * slots * count * width,
    )(back, returned.reshape(groups, owners, CAP + TOP, lanes))
    return (level_one, level_two, level_three, residual)


def solution(mesh):
    in_specs = (P(("dp", "cent"), None), P(("dp", "cent")), P("cent"), P(), P("cent", "dp"))
    out_specs = (P("cent", "dp"), P("cent", "dp"), P(), P(("dp", "cent"), None))
    return jax.shard_map(
        on_device, mesh=mesh, in_specs=in_specs, out_specs=out_specs, check_vma=False
    )
```

```python
import jax
import jax.numpy as jnp
from jax import lax
from jax.experimental import pallas as pl
from jax.experimental.pallas import tpu as pltpu
from jax.sharding import PartitionSpec as P

F32 = jnp.float32
BF16 = jnp.bfloat16
I32 = jnp.int32
LANES = 128
LOW = 512
HIGHS = 8
CAP = 32
HALF = 16
EXTRA = 8
TOP = 16
BOTH = ("dp", "cent")


def iota(shape, axis):
    return lax.broadcasted_iota(I32, shape, axis)


def dot(left, right):
    return jnp.dot(left, right, preferred_element_type=F32)


def dot_nt(left, right):
    return lax.dot_general(left, right, (((1,), (1,)), ((), ())), preferred_element_type=F32)


def lane_slice(at, width=LANES):
    return slice(at * width, (at + 1) * width)


HBM = pl.BlockSpec(memory_space=pltpu.HBM)
VMEM = pl.BlockSpec(memory_space=pltpu.VMEM)


FULL = 62_900_000
UPPER = 61_000_000
LEVEL = 58_600_000
SMALL = 16_000_000


def call(body, out_shape, ins, outs, vmem, scratch=(), flops=0, size=4 << 20, alias=None):
    return pl.pallas_call(
        body,
        out_shape=out_shape,
        in_specs=ins,
        out_specs=outs,
        scratch_shapes=list(scratch),
        input_output_aliases=alias or {},
        compiler_params=pltpu.CompilerParams(vmem_limit_bytes=vmem),
        cost_estimate=pl.CostEstimate(flops=flops, bytes_accessed=size, transcendentals=0),
    )


def pack_kernel(
    assign_hbm, points_hbm, send_hbm, back_hbm, assign_ref, points_ref, send_ref, back_ref, sems
):
    owners = send_ref.shape[1]
    parts = send_ref.shape[0]
    count = points_ref.shape[0]
    load = pltpu.make_async_copy(assign_hbm, assign_ref, sems.at[0])
    load.start()
    loads = []
    for pair in range(parts // 2):
        at = lane_slice(pair, 2 * LANES)
        loads.append(
            pltpu.make_async_copy(points_hbm.at[:, at], points_ref.at[:, at], sems.at[1 + pair])
        )
        loads[-1].start()
    before = jnp.where(iota((count, count), 0) <= iota((count, count), 1), 1.0, 0.0).astype(BF16)
    same = jnp.where(iota((count, count), 0) == iota((count, count), 1), 1.0, 0.0).astype(BF16)
    load.wait()
    label = assign_ref[...]
    owner = lax.shift_right_logical(label, 12)
    local = label & 4095
    mine = iota((owners, count), 0) == owner
    mine_f = jnp.where(mine, 1.0, 0.0)
    running = dot(mine_f.astype(BF16), before)
    place = jnp.sum(running * mine_f, axis=0, keepdims=True).astype(I32) - 1
    slot = owner * CAP + place
    table = jnp.where(iota((owners * CAP, count), 0) == slot, 1.0, 0.0).astype(BF16)
    shift = (lax.axis_index("cent") % 8) * HALF
    line = iota((LANES, count), 0)
    row = iota((owners, EXTRA, LANES), 1)
    digits = [(lax.shift_right_logical(local, 6) + 1).astype(F32), ((local & 63) + 1).astype(F32)]
    digits = [(mine_f * digit).astype(BF16) for digit in digits]
    extra = jnp.zeros((owners, EXTRA, LANES), F32)
    for half in range(2):
        first = half * HALF
        inside = (place >= first) & (place < first + HALF)
        lane = jnp.where(inside, place - first + shift, -1)
        lane_table = jnp.where(line == lane, 1.0, 0.0).astype(BF16)
        for kind in range(2):
            found = dot_nt(digits[kind], lane_table)
            extra = jnp.where(row == 2 * kind + half, found[:, None, :], extra)
    extra = extra.astype(BF16)
    stores = []
    for part in range(parts):
        if part % 2 == 0:
            loads[part // 2].wait()
            both = dot(table, points_ref[:, lane_slice(part // 2, 2 * LANES)]).astype(BF16)
        rows = both[:, lane_slice(part % 2)]
        send_ref[part, :, 0:CAP, :] = rows.reshape(owners, CAP, LANES)
        send_ref[part, :, CAP : CAP + EXTRA, :] = extra
        stores.append(
            pltpu.make_async_copy(send_ref.at[part], send_hbm.at[part], sems.at[1 + parts // 2 + part])
        )
        stores[-1].start()
        if part == 0:
            back_ref[...] = dot_nt(same, table).astype(BF16)
            stores.append(pltpu.make_async_copy(back_ref, back_hbm, sems.at[1 + parts // 2 + parts]))
            stores[-1].start()
    for store in stores:
        store.wait()


def slot_digits(slab_ref, digits_ref):
    rows = slab_ref[:, CAP : CAP + EXTRA, :].astype(F32).reshape(-1, LANES).astype(BF16)
    shape = (64, rows.shape[0])
    column, line = iota(shape, 1), iota(shape, 0)
    pick = (lax.shift_right_logical(column, 6) == (line & 15)) & (
        (column & 7) == lax.shift_right_logical(line, 4)
    )
    digits_ref[...] = dot(jnp.where(pick, 1.0, 0.0).astype(BF16), rows)


def across_lanes(digits_ref, at, count):
    found = []
    for part in range(count):
        high, low = digits_ref[pl.ds(at + part, 1), :], digits_ref[pl.ds(at + part + 32, 1), :]
        found.append((high * 64.0 + low).astype(I32) - 65)
    return found


def down_rows(digits_ref, at, count):
    same = iota((LANES, LANES), 0) == iota((LANES, LANES), 1)
    parts = []
    for part in range(count):
        high, low = digits_ref[pl.ds(at + part, 1), :], digits_ref[pl.ds(at + part + 32, 1), :]
        parts.append(
            jnp.concatenate([jnp.where(same, high, 0.0), jnp.where(same, low, 0.0)], axis=1)
        )
    left = jnp.concatenate(parts, axis=0).astype(BF16)
    right = jnp.where(iota((2 * LANES, LANES), 0) < LANES, 64.0, 1.0).astype(BF16)
    return dot(left, right).astype(I32) - 65


def low_table(labels):
    line = iota((LOW, LANES), 0)
    return jnp.concatenate(
        [jnp.where(line == (label & (LOW - 1)), 1.0, 0.0).astype(BF16) for label in labels], axis=1
    )


def masked(rows, high, which):
    return jnp.where(high == which, rows, 0.0).astype(BF16)


def counting(high):
    lane = iota(high.shape, 1)
    return jnp.where((high == (lane & 7)) & (lane < 16), 1.0, 0.0).astype(BF16)


def segments(total_ref, left_ref, high_ref, rows_of, digits_ref, steps):
    for step in range(steps):
        left_ref[:, lane_slice(step, 512)] = low_table(across_lanes(digits_ref, 4 * step, 4))
        high_ref[lane_slice(step, 512), :] = lax.shift_right_arithmetic(
            down_rows(digits_ref, 4 * step, 4), 9
        )
    left = left_ref[:, 0 : steps * 512]
    for pair in range(HIGHS // 2):
        right = []
        for step in range(steps):
            high, rows = high_ref[lane_slice(step, 512), :], rows_of(step)
            right.append(
                jnp.concatenate([masked(rows, high, 2 * pair + side) for side in range(2)], axis=1)
            )
        total_ref[:, lane_slice(pair, 2 * LANES)] = dot(left, jnp.concatenate(right, axis=0))
    total_ref[:, HIGHS * LANES :] = dot(left, counting(high_ref[0 : steps * 512, :]))


def add_segments(total_ref, digits_ref, at, rows):
    left = low_table(across_lanes(digits_ref, at, 2))
    high = lax.shift_right_arithmetic(down_rows(digits_ref, at, 2), 9)
    for pair in range(HIGHS // 2):
        right = jnp.concatenate([masked(rows, high, 2 * pair + side) for side in range(2)], axis=1)
        total_ref[:, lane_slice(pair, 2 * LANES)] += dot(left, right)
    total_ref[:, HIGHS * LANES :] += dot(left, counting(high))


def lower_rows(slab_ref, step):
    return slab_ref[lane_slice(step, 32), 0:HALF, :].reshape(512, LANES).astype(F32)


def upper_rows(slab_ref, group):
    return slab_ref[pl.ds(group * 16, 16), HALF:CAP, :].reshape(256, LANES).astype(F32)


def mark_live(digits_ref, live_ref):
    for group in range(live_ref.shape[0]):
        most = jnp.max(digits_ref[16 + 2 * group : 18 + 2 * group, :])
        live_ref[group] = jnp.where(most > 0.0, 1, 0)


def parent_kernel(parent_ref, old_ref, total_ref, digits_ref, left_ref, high_ref):
    parent = parent_ref[...]
    digits_ref[0:32, :] = (lax.shift_right_logical(parent, 6) + 1).astype(F32)
    digits_ref[32:64, :] = ((parent & 63) + 1).astype(F32)
    segments(
        total_ref,
        left_ref,
        high_ref,
        lambda step: old_ref[lane_slice(step, 512), :].astype(F32),
        digits_ref,
        old_ref.shape[0] // 512,
    )


def find_parents(digits_ref, parents_ref, table_ref, at, count):
    line = iota((LANES, LANES), 0)
    rows = [(digits_ref[pl.ds(at + n, 1), :], digits_ref[pl.ds(at + n + 32, 1), :]) for n in range(count)]
    left = [jnp.where(line == high.astype(I32) - 1, 1.0, 0.0).astype(BF16) for high, _ in rows]
    found = dot(table_ref[...], jnp.concatenate(left, axis=1))
    for n in range(count):
        chosen = jnp.where((line & 63) == rows[n][1].astype(I32) - 1, found[:, lane_slice(n)], 0.0)
        parents_ref[pl.ds(at + n, 1), :] = jnp.sum(chosen[0:64], axis=0, keepdims=True)
        parents_ref[pl.ds(at + n + 32, 1), :] = jnp.sum(chosen[64:128], axis=0, keepdims=True)


def upper_kernel(
    slab_ref, table_ref, top_ref, start_hbm, send_hbm,
    digits_ref, parents_ref, total_ref, left_ref, high_ref, start_ref, send_ref, right_ref, live_ref, sems,
):
    load = pltpu.make_async_copy(start_hbm, start_ref, sems.at[0])
    load.start()
    slot_digits(slab_ref, digits_ref)
    mark_live(digits_ref, live_ref)
    for step in range(4):
        find_parents(digits_ref, parents_ref, table_ref, 4 * step, 4)
    segments(total_ref, left_ref, high_ref, lambda step: lower_rows(slab_ref, step), parents_ref, 4)

    def more(group, carry):
        @pl.when(live_ref[group] > 0)
        def _():
            find_parents(digits_ref, parents_ref, table_ref, 16 + 2 * group, 2)
            add_segments(total_ref, parents_ref, 16 + 2 * group, upper_rows(slab_ref, group))

        return carry

    lax.fori_loop(0, slab_ref.shape[0] // 16, more, 0)
    load.wait()
    at = slice(HIGHS * LANES, (HIGHS + 1) * LANES)
    weights = total_ref[:, at] + start_ref[:, at]
    coarse = weights.astype(BF16).astype(F32)
    fine = weights - coarse
    lane = iota((LOW, LANES), 1)
    tops = []
    for high in range(HIGHS):
        mass = (total_ref[:, lane_slice(high)] + start_ref[:, lane_slice(high)]).astype(BF16)
        for half in range(2):
            send_ref[2 * high + half, 0:256, :] = mass[half * 256 : (half + 1) * 256]
        right_ref[lane_slice(high, LOW), 0:LANES] = mass
        right_ref[lane_slice(high, LOW), LANES:] = jnp.where(
            lane == high, coarse, jnp.where(lane == high + 8, fine, 0.0)
        ).astype(BF16)
        for part in range(4):
            hit = iota((256, LANES), 0) == top_ref[high * 4 + part : high * 4 + part + 1, :]
            tops.append(jnp.where(hit, 1.0, 0.0).astype(BF16))
    tops = dot(jnp.concatenate(tops, axis=1), right_ref[...])
    top_mass = tops[:, :LANES].astype(BF16)
    top_weight = jnp.sum(tops[:, LANES:].T[0:16], axis=0, keepdims=True)
    top_coarse = top_weight.astype(BF16).astype(F32)
    top_fine = top_weight - top_coarse
    coarse_t, fine_t = coarse.T, fine.T
    stores = []
    for owner in range(send_ref.shape[0]):
        send_ref[owner, 256:272, :] = top_mass[owner * TOP : (owner + 1) * TOP]
        high, from_lane = owner // 2, (owner % 2) * 256
        rows = []
        for source, line_at, lane_at in (
            (coarse_t, high, from_lane),
            (fine_t, high, from_lane),
            (top_coarse, 0, 0),
            (top_fine, 0, 0),
        ):
            for half in range(2):
                first = lane_at + half * LANES
                rows.append(source[line_at : line_at + 1, first : first + LANES])
        send_ref[owner, 272:280, :] = jnp.concatenate(rows, axis=0).astype(BF16)
        if owner % 4 == 3:
            part = pl.ds(owner - 3, 4)
            stores.append(
                pltpu.make_async_copy(send_ref.at[part], send_hbm.at[part], sems.at[1 + owner // 4])
            )
            stores[-1].start()
    for store in stores:
        store.wait()


def level_kernel(
    slab_ref, old_hbm, level_hbm, residual_hbm,
    digits_ref, total_ref, table_ref, left_ref, high_ref, old_ref, level_ref, residual_ref, live_ref,
    load_sem, level_sems, low_sems, up_sems,
):
    load = pltpu.make_async_copy(old_hbm, old_ref, load_sem)
    load.start()
    slot_digits(slab_ref, digits_ref)
    mark_live(digits_ref, live_ref)
    segments(total_ref, left_ref, high_ref, lambda step: lower_rows(slab_ref, step), digits_ref, 4)
    groups = slab_ref.shape[0] // 16

    def more(group, carry):
        @pl.when(live_ref[group] > 0)
        def _():
            add_segments(total_ref, digits_ref, 16 + 2 * group, upper_rows(slab_ref, group))

        return carry

    lax.fori_loop(0, groups, more, 0)
    load.wait()
    inverse = 1.0 / (total_ref[:, HIGHS * LANES :] + 1.0)
    stores = []
    for high in range(HIGHS):
        lines = lane_slice(high, LOW)
        mass = total_ref[:, lane_slice(high)] + old_ref[lines, :].astype(F32)
        level = mass * jnp.broadcast_to(inverse[:, high : high + 1], mass.shape)
        level_ref[lines, :] = level
        table_ref[:, lane_slice(high)] = level.astype(BF16)
        stores.append(
            pltpu.make_async_copy(level_ref.at[lines], level_hbm.at[lines], level_sems.at[high])
        )
        stores[-1].start()

    def subtract(at, count, rows):
        label = down_rows(digits_ref, at, count)
        low = label & (LOW - 1)
        high = lax.shift_right_arithmetic(label, 9)
        lane = iota(label.shape, 1)
        left = jnp.concatenate(
            [
                jnp.where(low == lane + part * LANES, 1.0, 0.0).astype(BF16)
                for part in range(LOW // LANES)
            ],
            axis=1,
        )
        for pair in range(HIGHS // 2):
            found = dot(left, table_ref[:, lane_slice(pair, 2 * LANES)])
            for side in range(2):
                rows -= jnp.where(high == 2 * pair + side, found[:, lane_slice(side)], 0.0)
        return rows.astype(BF16)

    for step in range(4):
        sources = lane_slice(step, 32)
        residual_ref[sources, 0:HALF, :] = subtract(
            4 * step, 4, lower_rows(slab_ref, step)
        ).reshape(32, HALF, LANES)
        part = (sources, slice(0, HALF))
        stores.append(
            pltpu.make_async_copy(residual_ref.at[part], residual_hbm.at[part], low_sems.at[step])
        )
        stores[-1].start()

    def upper_copy(group):
        part = (pl.ds(group * 16, 16), pl.ds(HALF, HALF))
        return pltpu.make_async_copy(residual_ref.at[part], residual_hbm.at[part], up_sems.at[group])

    def finish(group, carry):
        sources = pl.ds(group * 16, 16)
        @pl.when(live_ref[group] > 0)
        def _():
            residual_ref[sources, HALF:CAP, :] = subtract(
                16 + 2 * group, 2, upper_rows(slab_ref, group)
            ).reshape(16, HALF, LANES)

        @pl.when(live_ref[group] == 0)
        def _():
            residual_ref[sources, HALF:CAP, :] = slab_ref[sources, HALF:CAP, :]

        upper_copy(group).start()
        return carry

    lax.fori_loop(0, groups, finish, 0)
    for store in stores:
        store.wait()

    def settle(group, carry):
        upper_copy(group).wait()
        return carry

    lax.fori_loop(0, groups, settle, 0)


def finish_kernel(parts_ref, send_in, level_ref, send_hbm, column_ref, top_ref, sem):
    total = parts_ref[0].astype(F32)
    for source in range(1, parts_ref.shape[0]):
        total += parts_ref[source].astype(F32)
    tail = total[272:280].T
    me = lax.axis_index("cent")
    chosen = jnp.where(me < 8, tail[:, 4:5] + tail[:, 6:7], tail[:, 5:6] + tail[:, 7:8])
    column_ref[...] = jnp.broadcast_to(chosen, (LANES, LANES))
    weight = column_ref[pl.ds(pl.multiple_of((me % 8) * TOP, TOP), TOP), :]
    top = (total[256:272] / weight).astype(BF16)
    top_ref[...] = jnp.broadcast_to(top[None], top_ref.shape)
    store = pltpu.make_async_copy(top_ref, send_hbm.at[:, pl.ds(CAP, TOP), :], sem)
    store.start()
    for half in range(2):
        weight = tail[:, half : half + 1] + tail[:, half + 2 : half + 3]
        lines = slice(half * LANES, (half + 1) * LANES)
        level_ref[lines, :] = total[lines] / jnp.broadcast_to(weight, (LANES, LANES))
    store.wait()


def unpack_kernel(back_ref, returned_ref, residual_ref, level_ref):
    groups, owners, rows, lanes = returned_ref.shape
    for pair in range(groups // 2):
        right = jnp.concatenate(
            [
                returned_ref[2 * pair + side, :, 0:CAP, :].reshape(owners * CAP, lanes)
                for side in range(2)
            ],
            axis=1,
        )
        residual_ref[:, lane_slice(pair, 2 * lanes)] = dot(back_ref[...], right).astype(BF16)
    for group in range(groups):
        top = returned_ref[group, :, CAP:rows, :].astype(F32)
        level_ref[:, lane_slice(group)] = top.reshape(owners * TOP, lanes)


def shape(dims, kind):
    return jax.ShapeDtypeStruct(dims, kind)


def swap(value, axes):
    return lax.all_to_all(value, axes, split_axis=0, concat_axis=0, tiled=True)


def on_device(points, assign, parent_one, parent_two, old_level_one):
    count, width = points.shape
    owners = lax.axis_size("cent")
    groups = lax.axis_size("dp")
    devices = owners * groups
    block, lanes = old_level_one.shape
    slots = owners * CAP
    rows = CAP + EXTRA
    total_dims = (LOW, (HIGHS + 1) * LANES)
    work = 2 * LOW * block * (HIGHS + 1) * LANES

    send, back = call(
        pack_kernel,
        (shape((groups, owners, rows, lanes), BF16), shape((count, slots), BF16)),
        [HBM, HBM],
        (HBM, HBM),
        FULL,
        [
            pltpu.VMEM((1, count), I32),
            pltpu.VMEM((count, width), BF16),
            pltpu.VMEM((groups, owners, rows, lanes), BF16),
            pltpu.VMEM((count, slots), BF16),
            pltpu.SemaphoreType.DMA((2 + groups // 2 + groups,)),
        ],
        flops=2 * slots * count * width,
    )(assign.reshape(1, count), points)
    slab = swap(send.reshape(devices, rows, lanes), BOTH)

    start = call(
        parent_kernel,
        shape(total_dims, F32),
        [VMEM, VMEM],
        VMEM,
        FULL,
        [
            pltpu.VMEM((64, LANES), F32),
            pltpu.VMEM((LOW, block), BF16),
            pltpu.VMEM((block, LANES), I32),
        ],
        flops=work,
    )(parent_one.reshape(block // LANES, LANES), old_level_one)
    grid = parent_one.reshape(64, 64).T
    table = jnp.concatenate([lax.shift_right_logical(grid, 6), grid & 63], axis=0) + 1
    table = jnp.pad(table, ((0, 0), (0, 64))).astype(BF16)

    share = call(
        upper_kernel,
        shape((owners, 280, lanes), BF16),
        [VMEM, VMEM, VMEM, HBM],
        HBM,
        UPPER,
        [
            pltpu.VMEM((64, LANES), F32),
            pltpu.VMEM((64, LANES), F32),
            pltpu.VMEM(total_dims, F32),
            pltpu.VMEM((LOW, 2048), BF16),
            pltpu.VMEM((2048, LANES), I32),
            pltpu.VMEM(total_dims, F32),
            pltpu.VMEM((owners, 280, lanes), BF16),
            pltpu.VMEM((HIGHS * LOW, 2 * LANES), BF16),
            pltpu.SMEM((groups,), I32),
            pltpu.SemaphoreType.DMA((5,)),
        ],
        flops=work,
    )(slab, table, parent_two.reshape(-1, LANES), start)
    shares = swap(share, "cent")

    level_one, answer = call(
        level_kernel,
        (shape((block, lanes), F32), shape((devices, CAP + TOP, lanes), BF16)),
        [VMEM, HBM],
        (HBM, HBM),
        LEVEL,
        [
            pltpu.VMEM((64, LANES), F32),
            pltpu.VMEM(total_dims, F32),
            pltpu.VMEM((LOW, HIGHS * LANES), BF16),
            pltpu.VMEM((LOW, 2048), BF16),
            pltpu.VMEM((2048, LANES), I32),
            pltpu.VMEM((block, lanes), BF16),
            pltpu.VMEM((block, lanes), F32),
            pltpu.VMEM((devices, CAP, lanes), BF16),
            pltpu.SMEM((groups,), I32),
            pltpu.SemaphoreType.DMA(()),
            pltpu.SemaphoreType.DMA((HIGHS,)),
            pltpu.SemaphoreType.DMA((4,)),
            pltpu.SemaphoreType.DMA((groups,)),
        ],
        flops=2 * work,
    )(slab, old_level_one)

    level_two, answer = call(
        finish_kernel,
        (shape((256, lanes), F32), shape((devices, CAP + TOP, lanes), BF16)),
        [VMEM, HBM],
        (VMEM, HBM),
        SMALL,
        [
            pltpu.VMEM((LANES, LANES), F32),
            pltpu.VMEM((devices, TOP, lanes), BF16),
            pltpu.SemaphoreType.DMA(()),
        ],
        alias={1: 1},
    )(shares, answer)
    returned = swap(answer, BOTH)
    residual, level_three = call(
        unpack_kernel,
        (shape((count, width), BF16), shape((owners * TOP, width), F32)),
        [VMEM, VMEM],
        (VMEM, VMEM),
        SMALL,
        flops=2 * slots * count * width,
    )(back, returned.reshape(groups, owners, CAP + TOP, lanes))
    return (level_one, level_two, level_three, residual)


def solution(mesh):
    in_specs = (P(("dp", "cent"), None), P(("dp", "cent")), P("cent"), P(), P("cent", "dp"))
    out_specs = (P("cent", "dp"), P("cent", "dp"), P(), P(("dp", "cent"), None))
    return jax.shard_map(
        on_device, mesh=mesh, in_specs=in_specs, out_specs=out_specs, check_vma=False
    )
```

```python
import jax
import jax.numpy as jnp
from jax import lax
from jax.experimental import pallas as pl
from jax.experimental.pallas import tpu as pltpu
from jax.sharding import PartitionSpec as P

F32 = jnp.float32
BF16 = jnp.bfloat16
I32 = jnp.int32
LANES = 128
LOW = 512
HIGHS = 8
CAP = 32
HALF = 16
EXTRA = 8
TOP = 16
BOTH = ("dp", "cent")


def iota(shape, axis):
    return lax.broadcasted_iota(I32, shape, axis)


def dot(left, right):
    return jnp.dot(left, right, preferred_element_type=F32)


def dot_nt(left, right):
    return lax.dot_general(left, right, (((1,), (1,)), ((), ())), preferred_element_type=F32)


def lane_slice(at, width=LANES):
    return slice(at * width, (at + 1) * width)


HBM = pl.BlockSpec(memory_space=pltpu.HBM)
VMEM = pl.BlockSpec(memory_space=pltpu.VMEM)


FULL = 62_900_000
UPPER = 59_000_000
LEVEL = 48_000_000
SMALL = 16_000_000


def call(body, out_shape, ins, outs, vmem, scratch=(), flops=0, size=4 << 20, alias=None):
    return pl.pallas_call(
        body,
        out_shape=out_shape,
        in_specs=ins,
        out_specs=outs,
        scratch_shapes=list(scratch),
        input_output_aliases=alias or {},
        compiler_params=pltpu.CompilerParams(vmem_limit_bytes=vmem),
        cost_estimate=pl.CostEstimate(flops=flops, bytes_accessed=size, transcendentals=0),
    )


def pack_kernel(
    assign_hbm, points_hbm, send_hbm, back_hbm, assign_ref, points_ref, send_ref, back_ref, sems
):
    owners = send_ref.shape[1]
    parts = send_ref.shape[0]
    count = points_ref.shape[0]
    load = pltpu.make_async_copy(assign_hbm, assign_ref, sems.at[0])
    load.start()
    loads = []
    for pair in range(parts // 2):
        at = lane_slice(pair, 2 * LANES)
        loads.append(
            pltpu.make_async_copy(points_hbm.at[:, at], points_ref.at[:, at], sems.at[1 + pair])
        )
        loads[-1].start()
    before = jnp.where(iota((count, count), 0) <= iota((count, count), 1), 1.0, 0.0).astype(BF16)
    same = jnp.where(iota((count, count), 0) == iota((count, count), 1), 1.0, 0.0).astype(BF16)
    load.wait()
    label = assign_ref[...]
    owner = lax.shift_right_logical(label, 12)
    local = label & 4095
    mine = iota((owners, count), 0) == owner
    mine_f = jnp.where(mine, 1.0, 0.0)
    running = dot(mine_f.astype(BF16), before)
    place = jnp.sum(running * mine_f, axis=0, keepdims=True).astype(I32) - 1
    slot = owner * CAP + place
    table = jnp.where(iota((owners * CAP, count), 0) == slot, 1.0, 0.0).astype(BF16)
    shift = (lax.axis_index("cent") % 8) * HALF
    line = iota((LANES, count), 0)
    row = iota((owners, EXTRA, LANES), 1)
    digits = [(lax.shift_right_logical(local, 6) + 1).astype(F32), ((local & 63) + 1).astype(F32)]
    digits = [(mine_f * digit).astype(BF16) for digit in digits]
    extra = jnp.zeros((owners, EXTRA, LANES), F32)
    for half in range(2):
        first = half * HALF
        inside = (place >= first) & (place < first + HALF)
        lane = jnp.where(inside, place - first + shift, -1)
        lane_table = jnp.where(line == lane, 1.0, 0.0).astype(BF16)
        for kind in range(2):
            found = dot_nt(digits[kind], lane_table)
            extra = jnp.where(row == 2 * kind + half, found[:, None, :], extra)
    extra = extra.astype(BF16)
    stores = []
    for part in range(parts):
        if part % 2 == 0:
            loads[part // 2].wait()
            both = dot(table, points_ref[:, lane_slice(part // 2, 2 * LANES)]).astype(BF16)
        rows = both[:, lane_slice(part % 2)]
        send_ref[part, :, 0:CAP, :] = rows.reshape(owners, CAP, LANES)
        send_ref[part, :, CAP : CAP + EXTRA, :] = extra
        stores.append(
            pltpu.make_async_copy(send_ref.at[part], send_hbm.at[part], sems.at[1 + parts // 2 + part])
        )
        stores[-1].start()
        if part == 0:
            back_ref[...] = dot_nt(same, table).astype(BF16)
            stores.append(pltpu.make_async_copy(back_ref, back_hbm, sems.at[1 + parts // 2 + parts]))
            stores[-1].start()
    for store in stores:
        store.wait()


def slot_digits(slab_ref, digits_ref):
    rows = slab_ref[:, CAP : CAP + EXTRA, :].astype(F32).reshape(-1, LANES).astype(BF16)
    shape = (64, rows.shape[0])
    column, line = iota(shape, 1), iota(shape, 0)
    pick = (lax.shift_right_logical(column, 6) == (line & 15)) & (
        (column & 7) == lax.shift_right_logical(line, 4)
    )
    digits_ref[...] = dot(jnp.where(pick, 1.0, 0.0).astype(BF16), rows)


def across_lanes(digits_ref, at, count):
    found = []
    for part in range(count):
        high, low = digits_ref[pl.ds(at + part, 1), :], digits_ref[pl.ds(at + part + 32, 1), :]
        found.append((high * 64.0 + low).astype(I32) - 65)
    return found


def down_rows(digits_ref, at, count):
    same = iota((LANES, LANES), 0) == iota((LANES, LANES), 1)
    parts = []
    for part in range(count):
        high, low = digits_ref[pl.ds(at + part, 1), :], digits_ref[pl.ds(at + part + 32, 1), :]
        parts.append(
            jnp.concatenate([jnp.where(same, high, 0.0), jnp.where(same, low, 0.0)], axis=1)
        )
    left = jnp.concatenate(parts, axis=0).astype(BF16)
    right = jnp.where(iota((2 * LANES, LANES), 0) < LANES, 64.0, 1.0).astype(BF16)
    return dot(left, right).astype(I32) - 65


def low_table(labels):
    line = iota((LOW, LANES), 0)
    return jnp.concatenate(
        [jnp.where(line == (label & (LOW - 1)), 1.0, 0.0).astype(BF16) for label in labels], axis=1
    )


def masked(rows, high, which):
    return jnp.where(high == which, rows, 0.0).astype(BF16)


def counting(high):
    lane = iota(high.shape, 1)
    return jnp.where((high == (lane & 7)) & (lane < 16), 1.0, 0.0).astype(BF16)


def segments(total_ref, left_ref, high_ref, rows_of, digits_ref, steps):
    for step in range(steps):
        left_ref[:, lane_slice(step, 512)] = low_table(across_lanes(digits_ref, 4 * step, 4))
        high_ref[lane_slice(step, 512), :] = lax.shift_right_arithmetic(
            down_rows(digits_ref, 4 * step, 4), 9
        )
    left = left_ref[:, 0 : steps * 512]
    for pair in range(HIGHS // 2):
        right = []
        for step in range(steps):
            high, rows = high_ref[lane_slice(step, 512), :], rows_of(step)
            right.append(
                jnp.concatenate([masked(rows, high, 2 * pair + side) for side in range(2)], axis=1)
            )
        total_ref[:, lane_slice(pair, 2 * LANES)] = dot(left, jnp.concatenate(right, axis=0))
    total_ref[:, HIGHS * LANES :] = dot(left, counting(high_ref[0 : steps * 512, :]))


def add_segments(total_ref, digits_ref, at, rows):
    left = low_table(across_lanes(digits_ref, at, 2))
    high = lax.shift_right_arithmetic(down_rows(digits_ref, at, 2), 9)
    for pair in range(HIGHS // 2):
        right = jnp.concatenate([masked(rows, high, 2 * pair + side) for side in range(2)], axis=1)
        total_ref[:, lane_slice(pair, 2 * LANES)] += dot(left, right)
    total_ref[:, HIGHS * LANES :] += dot(left, counting(high))


def lower_rows(slab_ref, step):
    return slab_ref[lane_slice(step, 32), 0:HALF, :].reshape(512, LANES).astype(F32)


def upper_rows(slab_ref, group):
    return slab_ref[pl.ds(group * 16, 16), HALF:CAP, :].reshape(256, LANES).astype(F32)


def mark_live(digits_ref, live_ref):
    for group in range(live_ref.shape[0]):
        most = jnp.max(digits_ref[16 + 2 * group : 18 + 2 * group, :])
        live_ref[group] = jnp.where(most > 0.0, 1, 0)


def parent_kernel(parent_ref, old_ref, total_ref, digits_ref, left_ref, high_ref):
    parent = parent_ref[...]
    digits_ref[0:32, :] = (lax.shift_right_logical(parent, 6) + 1).astype(F32)
    digits_ref[32:64, :] = ((parent & 63) + 1).astype(F32)
    segments(
        total_ref,
        left_ref,
        high_ref,
        lambda step: old_ref[lane_slice(step, 512), :].astype(F32),
        digits_ref,
        old_ref.shape[0] // 512,
    )


def find_parents(digits_ref, parents_ref, table_ref, at, count):
    line = iota((LANES, LANES), 0)
    rows = [(digits_ref[pl.ds(at + n, 1), :], digits_ref[pl.ds(at + n + 32, 1), :]) for n in range(count)]
    left = [jnp.where(line == high.astype(I32) - 1, 1.0, 0.0).astype(BF16) for high, _ in rows]
    found = dot(table_ref[...], jnp.concatenate(left, axis=1))
    for n in range(count):
        chosen = jnp.where((line & 63) == rows[n][1].astype(I32) - 1, found[:, lane_slice(n)], 0.0)
        parents_ref[pl.ds(at + n, 1), :] = jnp.sum(chosen[0:64], axis=0, keepdims=True)
        parents_ref[pl.ds(at + n + 32, 1), :] = jnp.sum(chosen[64:128], axis=0, keepdims=True)


def upper_kernel(
    slab_ref, table_ref, top_ref, start_hbm, send_hbm,
    digits_ref, parents_ref, total_ref, left_ref, high_ref, start_ref, send_ref, right_ref, live_ref, sems,
):
    load = pltpu.make_async_copy(start_hbm, start_ref, sems.at[0])
    load.start()
    slot_digits(slab_ref, digits_ref)
    mark_live(digits_ref, live_ref)
    for step in range(4):
        find_parents(digits_ref, parents_ref, table_ref, 4 * step, 4)
    segments(total_ref, left_ref, high_ref, lambda step: lower_rows(slab_ref, step), parents_ref, 4)

    def more(group, carry):
        @pl.when(live_ref[group] > 0)
        def _():
            find_parents(digits_ref, parents_ref, table_ref, 16 + 2 * group, 2)
            add_segments(total_ref, parents_ref, 16 + 2 * group, upper_rows(slab_ref, group))

        return carry

    lax.fori_loop(0, slab_ref.shape[0] // 16, more, 0)
    load.wait()
    at = slice(HIGHS * LANES, (HIGHS + 1) * LANES)
    weights = total_ref[:, at] + start_ref[:, at]
    coarse = weights.astype(BF16).astype(F32)
    lane = iota((LOW, LANES), 1)
    split = jnp.where(lane < HIGHS, coarse, weights - coarse)
    diagonal = jnp.where(iota((16, LANES), 0) == iota((16, LANES), 1), 1.0, 0.0).astype(BF16)
    across = dot_nt(diagonal, split.astype(BF16))
    tops = []
    for high in range(HIGHS):
        mass = (total_ref[:, lane_slice(high)] + start_ref[:, lane_slice(high)]).astype(BF16)
        for half in range(2):
            send_ref[2 * high + half, 0:256, :] = mass[half * 256 : (half + 1) * 256]
        right_ref[lane_slice(high, LOW), 0:LANES] = mass
        right_ref[lane_slice(high, LOW), LANES:] = jnp.where((lane & 7) == high, split, 0.0).astype(BF16)
        for part in range(4):
            hit = iota((256, LANES), 0) == top_ref[high * 4 + part : high * 4 + part + 1, :]
            tops.append(jnp.where(hit, 1.0, 0.0).astype(BF16))
    tops = dot(jnp.concatenate(tops, axis=1), right_ref[...])
    top_mass = tops[:, :LANES].astype(BF16)
    first = jnp.where(iota((8, LANES), 1) < 16, 1.0, 0.0)
    top_weight = lax.dot_general(
        first,
        tops[:, LANES:],
        (((1,), (1,)), ((), ())),
        precision=lax.Precision.HIGHEST,
        preferred_element_type=F32,
    )[0:1]
    top_coarse = top_weight.astype(BF16).astype(F32)
    top_fine = top_weight - top_coarse
    top_rows = [part[:, lane_slice(half)] for part in (top_coarse, top_fine) for half in range(2)]
    stores = []
    for owner in range(send_ref.shape[0]):
        send_ref[owner, 256:272, :] = top_mass[owner * TOP : (owner + 1) * TOP]
        high = owner // 2
        rows = [
            across[line : line + 1, lane_slice(owner % 2 * 2 + half)]
            for line in (high, high + HIGHS)
            for half in range(2)
        ]
        send_ref[owner, 272:280, :] = jnp.concatenate(rows + top_rows, axis=0).astype(BF16)
        if owner % 4 == 3:
            part = pl.ds(owner - 3, 4)
            stores.append(
                pltpu.make_async_copy(send_ref.at[part], send_hbm.at[part], sems.at[1 + owner // 4])
            )
            stores[-1].start()
    for store in stores:
        store.wait()


def level_kernel(
    slab_ref, old_hbm, level_hbm, residual_hbm,
    digits_ref, total_ref, table_ref, left_ref, high_ref, old_ref, level_ref, residual_ref, live_ref,
    load_sem, level_sems, low_sems, up_sems,
):
    load = pltpu.make_async_copy(old_hbm, old_ref, load_sem)
    load.start()
    slot_digits(slab_ref, digits_ref)
    mark_live(digits_ref, live_ref)
    segments(total_ref, left_ref, high_ref, lambda step: lower_rows(slab_ref, step), digits_ref, 4)
    groups = slab_ref.shape[0] // 16

    def more(group, carry):
        @pl.when(live_ref[group] > 0)
        def _():
            add_segments(total_ref, digits_ref, 16 + 2 * group, upper_rows(slab_ref, group))

        return carry

    lax.fori_loop(0, groups, more, 0)
    load.wait()
    inverse = 1.0 / (total_ref[:, HIGHS * LANES :] + 1.0)
    stores = []
    for high in range(HIGHS):
        lines = lane_slice(high, LOW)
        mass = total_ref[:, lane_slice(high)] + old_ref[lines, :].astype(F32)
        level = mass * jnp.broadcast_to(inverse[:, high : high + 1], mass.shape)
        level_ref[lines, :] = level
        table_ref[:, lane_slice(high)] = level.astype(BF16)
        stores.append(
            pltpu.make_async_copy(level_ref.at[lines], level_hbm.at[lines], level_sems.at[high])
        )
        stores[-1].start()

    def subtract(at, count, rows):
        label = down_rows(digits_ref, at, count)
        low = label & (LOW - 1)
        high = lax.shift_right_arithmetic(label, 9)
        lane = iota(label.shape, 1)
        left = jnp.concatenate(
            [
                jnp.where(low == lane + part * LANES, 1.0, 0.0).astype(BF16)
                for part in range(LOW // LANES)
            ],
            axis=1,
        )
        for pair in range(HIGHS // 2):
            found = dot(left, table_ref[:, lane_slice(pair, 2 * LANES)])
            for side in range(2):
                rows -= jnp.where(high == 2 * pair + side, found[:, lane_slice(side)], 0.0)
        return rows.astype(BF16)

    for step in range(4):
        sources = lane_slice(step, 32)
        residual_ref[sources, 0:HALF, :] = subtract(
            4 * step, 4, lower_rows(slab_ref, step)
        ).reshape(32, HALF, LANES)
        part = (sources, slice(0, HALF))
        stores.append(
            pltpu.make_async_copy(residual_ref.at[part], residual_hbm.at[part], low_sems.at[step])
        )
        stores[-1].start()

    def upper_copy(group):
        part = (pl.ds(group * 16, 16), pl.ds(HALF, HALF))
        return pltpu.make_async_copy(residual_ref.at[part], residual_hbm.at[part], up_sems.at[group])

    def finish(group, carry):
        sources = pl.ds(group * 16, 16)
        @pl.when(live_ref[group] > 0)
        def _():
            residual_ref[sources, HALF:CAP, :] = subtract(
                16 + 2 * group, 2, upper_rows(slab_ref, group)
            ).reshape(16, HALF, LANES)

        @pl.when(live_ref[group] == 0)
        def _():
            residual_ref[sources, HALF:CAP, :] = slab_ref[sources, HALF:CAP, :]

        upper_copy(group).start()
        return carry

    lax.fori_loop(0, groups, finish, 0)
    for store in stores:
        store.wait()

    def settle(group, carry):
        upper_copy(group).wait()
        return carry

    lax.fori_loop(0, groups, settle, 0)


def finish_kernel(parts_ref, send_in, level_ref, send_hbm, column_ref, top_ref, sem):
    total = parts_ref[0].astype(F32)
    for source in range(1, parts_ref.shape[0]):
        total += parts_ref[source].astype(F32)
    tail = total[272:280].T
    me = lax.axis_index("cent")
    chosen = jnp.where(me < 8, tail[:, 4:5] + tail[:, 6:7], tail[:, 5:6] + tail[:, 7:8])
    column_ref[...] = jnp.broadcast_to(chosen, (LANES, LANES))
    weight = column_ref[pl.ds(pl.multiple_of((me % 8) * TOP, TOP), TOP), :]
    top = (total[256:272] / weight).astype(BF16)
    top_ref[...] = jnp.broadcast_to(top[None], top_ref.shape)
    store = pltpu.make_async_copy(top_ref, send_hbm.at[:, pl.ds(CAP, TOP), :], sem)
    store.start()
    for half in range(2):
        weight = tail[:, half : half + 1] + tail[:, half + 2 : half + 3]
        lines = slice(half * LANES, (half + 1) * LANES)
        level_ref[lines, :] = total[lines] / jnp.broadcast_to(weight, (LANES, LANES))
    store.wait()


def unpack_kernel(back_ref, returned_ref, residual_ref, level_ref):
    groups, owners, rows, lanes = returned_ref.shape
    for pair in range(groups // 2):
        right = jnp.concatenate(
            [
                returned_ref[2 * pair + side, :, 0:CAP, :].reshape(owners * CAP, lanes)
                for side in range(2)
            ],
            axis=1,
        )
        residual_ref[:, lane_slice(pair, 2 * lanes)] = dot(back_ref[...], right).astype(BF16)
    for group in range(groups):
        top = returned_ref[group, :, CAP:rows, :].astype(F32)
        level_ref[:, lane_slice(group)] = top.reshape(owners * TOP, lanes)


def shape(dims, kind):
    return jax.ShapeDtypeStruct(dims, kind)


def swap(value, axes):
    return lax.all_to_all(value, axes, split_axis=0, concat_axis=0, tiled=True)


def on_device(points, assign, parent_one, parent_two, old_level_one):
    count, width = points.shape
    owners = lax.axis_size("cent")
    groups = lax.axis_size("dp")
    devices = owners * groups
    block, lanes = old_level_one.shape
    slots = owners * CAP
    rows = CAP + EXTRA
    total_dims = (LOW, (HIGHS + 1) * LANES)
    work = 2 * LOW * block * (HIGHS + 1) * LANES

    send, back = call(
        pack_kernel,
        (shape((groups, owners, rows, lanes), BF16), shape((count, slots), BF16)),
        [HBM, HBM],
        (HBM, HBM),
        FULL,
        [
            pltpu.VMEM((1, count), I32),
            pltpu.VMEM((count, width), BF16),
            pltpu.VMEM((groups, owners, rows, lanes), BF16),
            pltpu.VMEM((count, slots), BF16),
            pltpu.SemaphoreType.DMA((2 + groups // 2 + groups,)),
        ],
        flops=2 * slots * count * width,
    )(assign.reshape(1, count), points)
    slab = swap(send.reshape(devices, rows, lanes), BOTH)

    start = call(
        parent_kernel,
        shape(total_dims, F32),
        [VMEM, VMEM],
        VMEM,
        FULL,
        [
            pltpu.VMEM((64, LANES), F32),
            pltpu.VMEM((LOW, block), BF16),
            pltpu.VMEM((block, LANES), I32),
        ],
        flops=work,
    )(parent_one.reshape(block // LANES, LANES), old_level_one)
    grid = parent_one.reshape(64, 64).T
    table = jnp.concatenate([lax.shift_right_logical(grid, 6), grid & 63], axis=0) + 1
    table = jnp.pad(table, ((0, 0), (0, 64))).astype(BF16)

    share = call(
        upper_kernel,
        shape((owners, 280, lanes), BF16),
        [VMEM, VMEM, VMEM, HBM],
        HBM,
        UPPER,
        [
            pltpu.VMEM((64, LANES), F32),
            pltpu.VMEM((64, LANES), F32),
            pltpu.VMEM(total_dims, F32),
            pltpu.VMEM((LOW, 2048), BF16),
            pltpu.VMEM((2048, LANES), I32),
            pltpu.VMEM(total_dims, F32),
            pltpu.VMEM((owners, 280, lanes), BF16),
            pltpu.VMEM((HIGHS * LOW, 2 * LANES), BF16),
            pltpu.SMEM((groups,), I32),
            pltpu.SemaphoreType.DMA((5,)),
        ],
        flops=work,
    )(slab, table, parent_two.reshape(-1, LANES), start)
    shares = swap(share, "cent")

    level_one, answer = call(
        level_kernel,
        (shape((block, lanes), F32), shape((devices, CAP + TOP, lanes), BF16)),
        [VMEM, HBM],
        (HBM, HBM),
        LEVEL,
        [
            pltpu.VMEM((64, LANES), F32),
            pltpu.VMEM(total_dims, F32),
            pltpu.VMEM((LOW, HIGHS * LANES), BF16),
            pltpu.VMEM((LOW, 2048), BF16),
            pltpu.VMEM((2048, LANES), I32),
            pltpu.VMEM((block, lanes), BF16),
            pltpu.VMEM((block, lanes), F32),
            pltpu.VMEM((devices, CAP, lanes), BF16),
            pltpu.SMEM((groups,), I32),
            pltpu.SemaphoreType.DMA(()),
            pltpu.SemaphoreType.DMA((HIGHS,)),
            pltpu.SemaphoreType.DMA((4,)),
            pltpu.SemaphoreType.DMA((groups,)),
        ],
        flops=2 * work,
    )(slab, old_level_one)

    level_two, answer = call(
        finish_kernel,
        (shape((256, lanes), F32), shape((devices, CAP + TOP, lanes), BF16)),
        [VMEM, HBM],
        (VMEM, HBM),
        SMALL,
        [
            pltpu.VMEM((LANES, LANES), F32),
            pltpu.VMEM((devices, TOP, lanes), BF16),
            pltpu.SemaphoreType.DMA(()),
        ],
        alias={1: 1},
    )(shares, answer)
    returned = swap(answer, BOTH)
    residual, level_three = call(
        unpack_kernel,
        (shape((count, width), BF16), shape((owners * TOP, width), F32)),
        [VMEM, VMEM],
        (VMEM, VMEM),
        SMALL,
        flops=2 * slots * count * width,
    )(back, returned.reshape(groups, owners, CAP + TOP, lanes))
    return (level_one, level_two, level_three, residual)


def solution(mesh):
    in_specs = (P(("dp", "cent"), None), P(("dp", "cent")), P("cent"), P(), P("cent", "dp"))
    out_specs = (P("cent", "dp"), P("cent", "dp"), P(), P(("dp", "cent"), None))
    return jax.shard_map(
        on_device, mesh=mesh, in_specs=in_specs, out_specs=out_specs, check_vma=False
    )
```

```python
import jax
import jax.numpy as jnp
from jax import lax
from jax.experimental import pallas as pl
from jax.experimental.pallas import tpu as pltpu
from jax.sharding import PartitionSpec as P

F32 = jnp.float32
BF16 = jnp.bfloat16
I32 = jnp.int32
LANES = 128
LOW = 512
HIGHS = 8
CAP = 32
HALF = 16
EXTRA = 8
TOP = 16
BOTH = ("dp", "cent")


def iota(shape, axis):
    return lax.broadcasted_iota(I32, shape, axis)


def dot(left, right):
    return jnp.dot(left, right, preferred_element_type=F32)


def dot_nt(left, right):
    return lax.dot_general(left, right, (((1,), (1,)), ((), ())), preferred_element_type=F32)


def lane_slice(at, width=LANES):
    return slice(at * width, (at + 1) * width)


HBM = pl.BlockSpec(memory_space=pltpu.HBM)
VMEM = pl.BlockSpec(memory_space=pltpu.VMEM)


FULL = 62_900_000
UPPER = 50_000_000
LEVEL = 48_000_000
SMALL = 16_000_000
SPARE = 12


def call(body, out_shape, ins, outs, vmem, scratch=(), flops=0, size=4 << 20, alias=None):
    return pl.pallas_call(
        body,
        out_shape=out_shape,
        in_specs=ins,
        out_specs=outs,
        scratch_shapes=list(scratch),
        input_output_aliases=alias or {},
        compiler_params=pltpu.CompilerParams(vmem_limit_bytes=vmem),
        cost_estimate=pl.CostEstimate(flops=flops, bytes_accessed=size, transcendentals=0),
    )


def pack_kernel(
    assign_hbm, points_hbm, send_hbm, back_hbm, assign_ref, points_ref, send_ref, back_ref, sems
):
    owners = send_ref.shape[1]
    parts = send_ref.shape[0]
    count = points_ref.shape[0]
    load = pltpu.make_async_copy(assign_hbm, assign_ref, sems.at[0])
    load.start()
    loads = []
    for pair in range(parts // 2):
        at = lane_slice(pair, 2 * LANES)
        loads.append(
            pltpu.make_async_copy(points_hbm.at[:, at], points_ref.at[:, at], sems.at[1 + pair])
        )
        loads[-1].start()
    before = jnp.where(iota((count, count), 0) <= iota((count, count), 1), 1.0, 0.0).astype(BF16)
    same = jnp.where(iota((count, count), 0) == iota((count, count), 1), 1.0, 0.0).astype(BF16)
    load.wait()
    label = assign_ref[...]
    owner = lax.shift_right_logical(label, 12)
    local = label & 4095
    mine = iota((owners, count), 0) == owner
    mine_f = jnp.where(mine, 1.0, 0.0)
    running = dot(mine_f.astype(BF16), before)
    place = jnp.sum(running * mine_f, axis=0, keepdims=True).astype(I32) - 1
    slot = owner * CAP + place
    table = jnp.where(iota((owners * CAP, count), 0) == slot, 1.0, 0.0).astype(BF16)
    shift = (lax.axis_index("cent") % 8) * HALF
    line = iota((LANES, count), 0)
    row = iota((owners, EXTRA, LANES), 1)
    digits = [(lax.shift_right_logical(local, 6) + 1).astype(F32), ((local & 63) + 1).astype(F32)]
    digits = [(mine_f * digit).astype(BF16) for digit in digits]
    extra = jnp.zeros((owners, EXTRA, LANES), F32)
    for half in range(2):
        first = half * HALF
        inside = (place >= first) & (place < first + HALF)
        lane = jnp.where(inside, place - first + shift, -1)
        lane_table = jnp.where(line == lane, 1.0, 0.0).astype(BF16)
        for kind in range(2):
            found = dot_nt(digits[kind], lane_table)
            extra = jnp.where(row == 2 * kind + half, found[:, None, :], extra)
    extra = extra.astype(BF16)
    stores = []
    for part in range(parts):
        if part % 2 == 0:
            loads[part // 2].wait()
            both = dot(table, points_ref[:, lane_slice(part // 2, 2 * LANES)]).astype(BF16)
        rows = both[:, lane_slice(part % 2)]
        send_ref[part, :, 0:CAP, :] = rows.reshape(owners, CAP, LANES)
        send_ref[part, :, CAP : CAP + EXTRA, :] = extra
        stores.append(
            pltpu.make_async_copy(send_ref.at[part], send_hbm.at[part], sems.at[1 + parts // 2 + part])
        )
        stores[-1].start()
        if part == 0:
            back_ref[...] = dot_nt(same, table).astype(BF16)
            stores.append(pltpu.make_async_copy(back_ref, back_hbm, sems.at[1 + parts // 2 + parts]))
            stores[-1].start()
    for store in stores:
        store.wait()


def slot_digits(slab_ref, digits_ref):
    rows = slab_ref[:, CAP : CAP + EXTRA, :].astype(F32).reshape(-1, LANES).astype(BF16)
    shape = (64, rows.shape[0])
    column, line = iota(shape, 1), iota(shape, 0)
    pick = (lax.shift_right_logical(column, 6) == (line & 15)) & (
        (column & 7) == lax.shift_right_logical(line, 4)
    )
    digits_ref[...] = dot(jnp.where(pick, 1.0, 0.0).astype(BF16), rows)


def across_lanes(digits_ref, at, count):
    found = []
    for part in range(count):
        high, low = digits_ref[pl.ds(at + part, 1), :], digits_ref[pl.ds(at + part + 32, 1), :]
        found.append((high * 64.0 + low).astype(I32) - 65)
    return found


def down_rows(digits_ref, at, count):
    same = iota((LANES, LANES), 0) == iota((LANES, LANES), 1)
    parts = []
    for part in range(count):
        high, low = digits_ref[pl.ds(at + part, 1), :], digits_ref[pl.ds(at + part + 32, 1), :]
        parts.append(
            jnp.concatenate([jnp.where(same, high, 0.0), jnp.where(same, low, 0.0)], axis=1)
        )
    left = jnp.concatenate(parts, axis=0).astype(BF16)
    right = jnp.where(iota((2 * LANES, LANES), 0) < LANES, 64.0, 1.0).astype(BF16)
    return dot(left, right).astype(I32) - 65


def low_table(labels):
    line = iota((LOW, LANES), 0)
    return jnp.concatenate(
        [jnp.where(line == (label & (LOW - 1)), 1.0, 0.0).astype(BF16) for label in labels], axis=1
    )


def masked(rows, high, which):
    return jnp.where(high == which, rows, 0.0).astype(BF16)


def counting(high):
    lane = iota(high.shape, 1)
    return jnp.where((high == (lane & 7)) & (lane < 16), 1.0, 0.0).astype(BF16)


def segments(total_ref, left_ref, high_ref, rows_of, digits_ref, steps):
    for step in range(steps):
        left_ref[:, lane_slice(step, 512)] = low_table(across_lanes(digits_ref, 4 * step, 4))
        high_ref[lane_slice(step, 512), :] = lax.shift_right_arithmetic(
            down_rows(digits_ref, 4 * step, 4), 9
        )
    left = left_ref[:, 0 : steps * 512]
    for pair in range(HIGHS // 2):
        right = []
        for step in range(steps):
            high, rows = high_ref[lane_slice(step, 512), :], rows_of(step)
            right.append(
                jnp.concatenate([masked(rows, high, 2 * pair + side) for side in range(2)], axis=1)
            )
        total_ref[:, lane_slice(pair, 2 * LANES)] = dot(left, jnp.concatenate(right, axis=0))
    total_ref[:, HIGHS * LANES :] = dot(left, counting(high_ref[0 : steps * 512, :]))


def add_segments(total_ref, digits_ref, at, rows):
    left = low_table(across_lanes(digits_ref, at, 2))
    high = lax.shift_right_arithmetic(down_rows(digits_ref, at, 2), 9)
    for pair in range(HIGHS // 2):
        right = jnp.concatenate([masked(rows, high, 2 * pair + side) for side in range(2)], axis=1)
        total_ref[:, lane_slice(pair, 2 * LANES)] += dot(left, right)
    total_ref[:, HIGHS * LANES :] += dot(left, counting(high))


def lower_rows(slab_ref, step):
    return slab_ref[lane_slice(step, 32), 0:HALF, :].reshape(512, LANES).astype(F32)


def upper_rows(slab_ref, group):
    return slab_ref[pl.ds(group * 16, 16), HALF:CAP, :].reshape(256, LANES).astype(F32)


def mark_live(digits_ref, live_ref):
    for group in range(live_ref.shape[0]):
        most = jnp.max(digits_ref[16 + 2 * group : 18 + 2 * group, :])
        live_ref[group] = jnp.where(most > 0.0, 1, 0)


def parent_kernel(parent_ref, old_ref, total_hbm, digits_ref, left_ref, high_ref, total_ref, sem):
    parent = parent_ref[...]
    digits_ref[0:32, :] = (lax.shift_right_logical(parent, 6) + 1).astype(F32)
    digits_ref[32:64, :] = ((parent & 63) + 1).astype(F32)
    segments(
        total_ref,
        left_ref,
        high_ref,
        lambda step: old_ref[lane_slice(step, 512), :].astype(F32),
        digits_ref,
        old_ref.shape[0] // 512,
    )
    store = pltpu.make_async_copy(total_ref, total_hbm.at[0], sem)
    store.start()
    store.wait()


def find_parents(digits_ref, parents_ref, table_ref, at, count):
    line = iota((LANES, LANES), 0)
    rows = [(digits_ref[pl.ds(at + n, 1), :], digits_ref[pl.ds(at + n + 32, 1), :]) for n in range(count)]
    left = [jnp.where(line == high.astype(I32) - 1, 1.0, 0.0).astype(BF16) for high, _ in rows]
    found = dot(table_ref[...], jnp.concatenate(left, axis=1))
    for n in range(count):
        chosen = jnp.where((line & 63) == rows[n][1].astype(I32) - 1, found[:, lane_slice(n)], 0.0)
        parents_ref[pl.ds(at + n, 1), :] = jnp.sum(chosen[0:64], axis=0, keepdims=True)
        parents_ref[pl.ds(at + n + 32, 1), :] = jnp.sum(chosen[64:128], axis=0, keepdims=True)


def upper_kernel(
    slab_ref, table_ref, top_ref, start_hbm, send_hbm,
    digits_ref, parents_ref, total_ref, left_ref, high_ref, start_ref, send_ref, right_ref, tail_ref, live_ref,
    sems,
):
    load = pltpu.make_async_copy(start_hbm.at[0], start_ref, sems.at[0])
    load.start()
    slot_digits(slab_ref, digits_ref)
    mark_live(digits_ref, live_ref)
    for step in range(4):
        find_parents(digits_ref, parents_ref, table_ref, 4 * step, 4)
    segments(total_ref, left_ref, high_ref, lambda step: lower_rows(slab_ref, step), parents_ref, 4)

    def more(group, carry):
        @pl.when(live_ref[group] > 0)
        def _():
            find_parents(digits_ref, parents_ref, table_ref, 16 + 2 * group, 2)
            add_segments(total_ref, parents_ref, 16 + 2 * group, upper_rows(slab_ref, group))

        return carry

    lax.fori_loop(0, slab_ref.shape[0] // 16, more, 0)
    load.wait()
    at = slice(HIGHS * LANES, (HIGHS + 1) * LANES)
    weights = total_ref[:, at] + start_ref[:, at]
    coarse = weights.astype(BF16).astype(F32)
    lane = iota((LOW, LANES), 1)
    split = jnp.where(lane < HIGHS, coarse, weights - coarse)
    diagonal = jnp.where(iota((16, LANES), 0) == iota((16, LANES), 1), 1.0, 0.0).astype(BF16)
    across = dot_nt(diagonal, split.astype(BF16))
    tops = []
    stores = []
    for high in range(HIGHS):
        mass = (total_ref[:, lane_slice(high)] + start_ref[:, lane_slice(high)]).astype(BF16)
        for half in range(2):
            send_ref[2 * high + half, 0:32] = mass[half * 256 : (half + 1) * 256].reshape(32, 8, LANES)
        part = (pl.ds(2 * high, 2), pl.ds(0, 32))
        stores.append(pltpu.make_async_copy(send_ref.at[part], send_hbm.at[part], sems.at[1 + high]))
        stores[-1].start()
        right_ref[lane_slice(high, LOW), 0:LANES] = mass
        right_ref[lane_slice(high, LOW), LANES:] = jnp.where((lane & 7) == high, split, 0.0).astype(BF16)
        for part in range(4):
            hit = iota((256, LANES), 0) == top_ref[high * 4 + part : high * 4 + part + 1, :]
            tops.append(jnp.where(hit, 1.0, 0.0).astype(BF16))
    for half in range(2):
        for kind in range(2):
            lines = slice(kind * HIGHS, (kind + 1) * HIGHS)
            for side in range(2):
                tail_ref[pl.ds(side, HIGHS, 2), 2 * kind + half, :] = across[lines, lane_slice(2 * side + half)]
    tops = dot(jnp.concatenate(tops, axis=1), right_ref[...])
    owners = send_ref.shape[0]
    send_ref[:, 32:34] = tops[:, :LANES].astype(BF16).reshape(owners, 2, 8, LANES)
    first = jnp.where(iota((8, LANES), 1) < 16, 1.0, 0.0).astype(BF16)
    heavy = tops[:, LANES:]
    heavy_coarse = heavy.astype(BF16)
    heavy_fine = (heavy - heavy_coarse.astype(F32)).astype(BF16)
    top_weight = (dot_nt(first, heavy_coarse) + dot_nt(first, heavy_fine))[0:1]
    top_coarse = top_weight.astype(BF16).astype(F32)
    for kind, value in enumerate((top_coarse, top_weight - top_coarse)):
        for half in range(2):
            tail_ref[:, 4 + 2 * kind + half, :] = jnp.broadcast_to(value[:, lane_slice(half)], (owners, LANES))
    send_ref[:, 34:35] = tail_ref[...].astype(BF16)[:, None]
    part = (slice(None), pl.ds(32, 3))
    stores.append(pltpu.make_async_copy(send_ref.at[part], send_hbm.at[part], sems.at[1 + HIGHS]))
    stores[-1].start()
    for store in stores:
        store.wait()


def level_kernel(
    slab_ref, old_hbm, level_hbm, residual_hbm,
    digits_ref, total_ref, table_ref, left_ref, high_ref, old_ref, level_ref, residual_ref, live_ref,
    load_sem, level_sems, low_sems, up_sems,
):
    load = pltpu.make_async_copy(old_hbm, old_ref, load_sem)
    load.start()
    slot_digits(slab_ref, digits_ref)
    mark_live(digits_ref, live_ref)
    segments(total_ref, left_ref, high_ref, lambda step: lower_rows(slab_ref, step), digits_ref, 4)
    groups = slab_ref.shape[0] // 16

    def more(group, carry):
        @pl.when(live_ref[group] > 0)
        def _():
            add_segments(total_ref, digits_ref, 16 + 2 * group, upper_rows(slab_ref, group))

        return carry

    lax.fori_loop(0, groups, more, 0)
    load.wait()
    inverse = 1.0 / (total_ref[:, HIGHS * LANES :] + 1.0)
    stores = []
    for high in range(HIGHS):
        lines = lane_slice(high, LOW)
        mass = total_ref[:, lane_slice(high)] + old_ref[lines, :].astype(F32)
        level = mass * jnp.broadcast_to(inverse[:, high : high + 1], mass.shape)
        level_ref[lines, :] = level
        table_ref[:, lane_slice(high)] = level.astype(BF16)
        stores.append(
            pltpu.make_async_copy(level_ref.at[lines], level_hbm.at[lines], level_sems.at[high])
        )
        stores[-1].start()

    def subtract(at, count, rows):
        label = down_rows(digits_ref, at, count)
        low = label & (LOW - 1)
        high = lax.shift_right_arithmetic(label, 9)
        lane = iota(label.shape, 1)
        left = jnp.concatenate(
            [
                jnp.where(low == lane + part * LANES, 1.0, 0.0).astype(BF16)
                for part in range(LOW // LANES)
            ],
            axis=1,
        )
        for pair in range(HIGHS // 2):
            found = dot(left, table_ref[:, lane_slice(pair, 2 * LANES)])
            for side in range(2):
                rows -= jnp.where(high == 2 * pair + side, found[:, lane_slice(side)], 0.0)
        return rows.astype(BF16)

    for step in range(4):
        sources = lane_slice(step, 32)
        residual_ref[sources, 0:HALF, :] = subtract(
            4 * step, 4, lower_rows(slab_ref, step)
        ).reshape(32, HALF, LANES)
        part = (sources, slice(0, HALF))
        stores.append(
            pltpu.make_async_copy(residual_ref.at[part], residual_hbm.at[part], low_sems.at[step])
        )
        stores[-1].start()

    def upper_copy(group):
        part = (pl.ds(group * 16, 16), pl.ds(HALF, HALF))
        return pltpu.make_async_copy(residual_ref.at[part], residual_hbm.at[part], up_sems.at[group])

    def finish(group, carry):
        sources = pl.ds(group * 16, 16)
        @pl.when(live_ref[group] > 0)
        def _():
            residual_ref[sources, HALF:CAP, :] = subtract(
                16 + 2 * group, 2, upper_rows(slab_ref, group)
            ).reshape(16, HALF, LANES)

        @pl.when(live_ref[group] == 0)
        def _():
            residual_ref[sources, HALF:CAP, :] = slab_ref[sources, HALF:CAP, :]

        upper_copy(group).start()
        return carry

    lax.fori_loop(0, groups, finish, 0)
    for store in stores:
        store.wait()

    def settle(group, carry):
        upper_copy(group).wait()
        return carry

    lax.fori_loop(0, groups, settle, 0)


def finish_kernel(parts_ref, send_in, level_ref, send_hbm, column_ref, top_ref, sem):
    total = parts_ref[0].astype(F32)
    for source in range(1, parts_ref.shape[0]):
        total += parts_ref[source].astype(F32)
    total = total.reshape(-1, LANES)
    tail = total[272:280].T
    me = lax.axis_index("cent")
    chosen = jnp.where(me < 8, tail[:, 4:5] + tail[:, 6:7], tail[:, 5:6] + tail[:, 7:8])
    column_ref[...] = jnp.broadcast_to(chosen, (LANES, LANES))
    weight = column_ref[pl.ds(pl.multiple_of((me % 8) * TOP, TOP), TOP), :]
    top = (total[256:272] / weight).astype(BF16)
    top_ref[...] = jnp.broadcast_to(top[None], top_ref.shape)
    store = pltpu.make_async_copy(top_ref, send_hbm.at[:, pl.ds(CAP, TOP), :], sem)
    store.start()
    for half in range(2):
        weight = tail[:, half : half + 1] + tail[:, half + 2 : half + 3]
        lines = slice(half * LANES, (half + 1) * LANES)
        level_ref[lines, :] = total[lines] / jnp.broadcast_to(weight, (LANES, LANES))
    store.wait()


def unpack_kernel(back_ref, returned_ref, residual_hbm, level_hbm, residual_ref, level_ref, sems):
    groups, owners, rows, lanes = returned_ref.shape
    stores = []
    for pair in range(groups // 2):
        for side in range(2):
            top = returned_ref[2 * pair + side, :, CAP:rows, :].astype(F32)
            level_ref[:, lane_slice(2 * pair + side)] = top.reshape(owners * TOP, lanes)
        right = jnp.concatenate(
            [
                returned_ref[2 * pair + side, :, 0:CAP, :].reshape(owners * CAP, lanes)
                for side in range(2)
            ],
            axis=1,
        )
        at = lane_slice(pair, 2 * lanes)
        stores.append(pltpu.make_async_copy(level_ref.at[:, at], level_hbm.at[:, at], sems.at[2 * pair]))
        stores[-1].start()
        residual_ref[:, at] = dot(back_ref[...], right).astype(BF16)
        stores.append(
            pltpu.make_async_copy(residual_ref.at[:, at], residual_hbm.at[:, at], sems.at[2 * pair + 1])
        )
        stores[-1].start()
    for store in stores:
        store.wait()


def shape(dims, kind):
    return jax.ShapeDtypeStruct(dims, kind)


def swap(value, axes):
    return lax.all_to_all(value, axes, split_axis=0, concat_axis=0, tiled=True)


def on_device(points, assign, parent_one, parent_two, old_level_one):
    count, width = points.shape
    owners = lax.axis_size("cent")
    groups = lax.axis_size("dp")
    devices = owners * groups
    block, lanes = old_level_one.shape
    slots = owners * CAP
    rows = CAP + EXTRA
    total_dims = (LOW, (HIGHS + 1) * LANES)
    work = 2 * LOW * block * (HIGHS + 1) * LANES

    send, back = call(
        pack_kernel,
        (shape((groups, owners, rows, lanes), BF16), shape((count, slots), BF16)),
        [HBM, HBM],
        (HBM, HBM),
        FULL,
        [
            pltpu.VMEM((1, count), I32),
            pltpu.VMEM((count, width), BF16),
            pltpu.VMEM((groups, owners, rows, lanes), BF16),
            pltpu.VMEM((count, slots), BF16),
            pltpu.SemaphoreType.DMA((2 + groups // 2 + groups,)),
        ],
        flops=2 * slots * count * width,
    )(assign.reshape(1, count), points)
    slab = swap(send.reshape(devices, rows, lanes), BOTH)

    start = call(
        parent_kernel,
        shape((SPARE, *total_dims), F32),
        [VMEM, VMEM],
        HBM,
        FULL,
        [
            pltpu.VMEM((64, LANES), F32),
            pltpu.VMEM((LOW, block), BF16),
            pltpu.VMEM((block, LANES), I32),
            pltpu.VMEM(total_dims, F32),
            pltpu.SemaphoreType.DMA(()),
        ],
        flops=work,
    )(parent_one.reshape(block // LANES, LANES), old_level_one)
    grid = parent_one.reshape(64, 64).T
    table = jnp.concatenate([lax.shift_right_logical(grid, 6), grid & 63], axis=0) + 1
    table = jnp.pad(table, ((0, 0), (0, 64))).astype(BF16)

    share = call(
        upper_kernel,
        shape((owners, 35, 8, lanes), BF16),
        [VMEM, VMEM, VMEM, HBM],
        HBM,
        UPPER,
        [
            pltpu.VMEM((64, LANES), F32),
            pltpu.VMEM((64, LANES), F32),
            pltpu.VMEM(total_dims, F32),
            pltpu.VMEM((LOW, 2048), BF16),
            pltpu.VMEM((2048, LANES), I32),
            pltpu.VMEM(total_dims, F32),
            pltpu.VMEM((owners, 35, 8, lanes), BF16),
            pltpu.VMEM((HIGHS * LOW, 2 * LANES), BF16),
            pltpu.VMEM((owners, 8, lanes), F32),
            pltpu.SMEM((groups,), I32),
            pltpu.SemaphoreType.DMA((2 + HIGHS,)),
        ],
        flops=work,
    )(slab, table, parent_two.reshape(-1, LANES), start)
    shares = swap(share, "cent")

    level_one, answer = call(
        level_kernel,
        (shape((block, lanes), F32), shape((devices, CAP + TOP, lanes), BF16)),
        [VMEM, HBM],
        (HBM, HBM),
        LEVEL,
        [
            pltpu.VMEM((64, LANES), F32),
            pltpu.VMEM(total_dims, F32),
            pltpu.VMEM((LOW, HIGHS * LANES), BF16),
            pltpu.VMEM((LOW, 2048), BF16),
            pltpu.VMEM((2048, LANES), I32),
            pltpu.VMEM((block, lanes), BF16),
            pltpu.VMEM((block, lanes), F32),
            pltpu.VMEM((devices, CAP, lanes), BF16),
            pltpu.SMEM((groups,), I32),
            pltpu.SemaphoreType.DMA(()),
            pltpu.SemaphoreType.DMA((HIGHS,)),
            pltpu.SemaphoreType.DMA((4,)),
            pltpu.SemaphoreType.DMA((groups,)),
        ],
        flops=2 * work,
    )(slab, old_level_one)

    level_two, answer = call(
        finish_kernel,
        (shape((256, lanes), F32), shape((devices, CAP + TOP, lanes), BF16)),
        [VMEM, HBM],
        (VMEM, HBM),
        SMALL,
        [
            pltpu.VMEM((LANES, LANES), F32),
            pltpu.VMEM((devices, TOP, lanes), BF16),
            pltpu.SemaphoreType.DMA(()),
        ],
        alias={1: 1},
    )(shares, answer)
    returned = swap(answer, BOTH)
    residual, level_three = call(
        unpack_kernel,
        (shape((count, width), BF16), shape((owners * TOP, width), F32)),
        [VMEM, VMEM],
        (HBM, HBM),
        SMALL,
        [
            pltpu.VMEM((count, width), BF16),
            pltpu.VMEM((owners * TOP, width), F32),
            pltpu.SemaphoreType.DMA((groups,)),
        ],
        flops=2 * slots * count * width,
    )(back, returned.reshape(groups, owners, CAP + TOP, lanes))
    return (level_one, level_two, level_three, residual)


def solution(mesh):
    in_specs = (P(("dp", "cent"), None), P(("dp", "cent")), P("cent"), P(), P("cent", "dp"))
    out_specs = (P("cent", "dp"), P("cent", "dp"), P(), P(("dp", "cent"), None))
    return jax.shard_map(
        on_device, mesh=mesh, in_specs=in_specs, out_specs=out_specs, check_vma=False
    )
```

```python
import jax
import jax.numpy as jnp
from jax import lax
from jax.experimental import pallas as pl
from jax.experimental.pallas import tpu as pltpu
from jax.sharding import PartitionSpec as P

F32 = jnp.float32
BF16 = jnp.bfloat16
I32 = jnp.int32
LANES = 128
LOW = 512
HIGHS = 8
CAP = 32
HALF = 16
EXTRA = 8
TOP = 16
BOTH = ("dp", "cent")


def iota(shape, axis):
    return lax.broadcasted_iota(I32, shape, axis)


def dot(left, right):
    return jnp.dot(left, right, preferred_element_type=F32)


def dot_nt(left, right):
    return lax.dot_general(left, right, (((1,), (1,)), ((), ())), preferred_element_type=F32)


def lane_slice(at, width=LANES):
    return slice(at * width, (at + 1) * width)


HBM = pl.BlockSpec(memory_space=pltpu.HBM)
VMEM = pl.BlockSpec(memory_space=pltpu.VMEM)


FULL = 62_900_000
UPPER = 50_000_000
LEVEL = 48_000_000
SMALL = 16_000_000
SPARE = 12


def call(body, out_shape, ins, outs, vmem, scratch=(), flops=0, size=4 << 20, alias=None):
    return pl.pallas_call(
        body,
        out_shape=out_shape,
        in_specs=ins,
        out_specs=outs,
        scratch_shapes=list(scratch),
        input_output_aliases=alias or {},
        compiler_params=pltpu.CompilerParams(vmem_limit_bytes=vmem),
        cost_estimate=pl.CostEstimate(flops=flops, bytes_accessed=size, transcendentals=0),
    )


def pack_kernel(
    assign_hbm, points_hbm, send_hbm, back_hbm, assign_ref, points_ref, send_ref, back_ref, sems
):
    owners = send_ref.shape[1]
    parts = send_ref.shape[0]
    count = points_ref.shape[0]
    load = pltpu.make_async_copy(assign_hbm, assign_ref, sems.at[0])
    load.start()
    loads = []
    for pair in range(parts // 2):
        at = lane_slice(pair, 2 * LANES)
        loads.append(
            pltpu.make_async_copy(points_hbm.at[:, at], points_ref.at[:, at], sems.at[1 + pair])
        )
        loads[-1].start()
    before = jnp.where(iota((count, count), 0) <= iota((count, count), 1), 1.0, 0.0).astype(BF16)
    same = jnp.where(iota((count, count), 0) == iota((count, count), 1), 1.0, 0.0).astype(BF16)
    load.wait()
    label = assign_ref[...]
    owner = lax.shift_right_logical(label, 12)
    local = label & 4095
    mine = iota((owners, count), 0) == owner
    mine_f = jnp.where(mine, 1.0, 0.0)
    running = dot(mine_f.astype(BF16), before)
    place = jnp.sum(running * mine_f, axis=0, keepdims=True).astype(I32) - 1
    slot = owner * CAP + place
    table = jnp.where(iota((owners * CAP, count), 0) == slot, 1.0, 0.0).astype(BF16)
    shift = (lax.axis_index("cent") % 8) * HALF
    line = iota((LANES, count), 0)
    row = iota((owners, EXTRA, LANES), 1)
    digits = [(lax.shift_right_logical(local, 6) + 1).astype(F32), ((local & 63) + 1).astype(F32)]
    digits = [(mine_f * digit).astype(BF16) for digit in digits]
    extra = jnp.zeros((owners, EXTRA, LANES), F32)
    for half in range(2):
        first = half * HALF
        inside = (place >= first) & (place < first + HALF)
        lane = jnp.where(inside, place - first + shift, -1)
        lane_table = jnp.where(line == lane, 1.0, 0.0).astype(BF16)
        for kind in range(2):
            found = dot_nt(digits[kind], lane_table)
            extra = jnp.where(row == 2 * kind + half, found[:, None, :], extra)
    extra = extra.astype(BF16)
    stores = []
    for part in range(parts):
        if part % 2 == 0:
            loads[part // 2].wait()
            both = dot(table, points_ref[:, lane_slice(part // 2, 2 * LANES)]).astype(BF16)
        rows = both[:, lane_slice(part % 2)]
        send_ref[part, :, 0:CAP, :] = rows.reshape(owners, CAP, LANES)
        send_ref[part, :, CAP : CAP + EXTRA, :] = extra
        stores.append(
            pltpu.make_async_copy(send_ref.at[part], send_hbm.at[part], sems.at[1 + parts // 2 + part])
        )
        stores[-1].start()
        if part == 0:
            back_ref[...] = dot_nt(same, table).astype(BF16)
            stores.append(pltpu.make_async_copy(back_ref, back_hbm, sems.at[1 + parts // 2 + parts]))
            stores[-1].start()
    for store in stores:
        store.wait()


def slot_digits(slab_ref, digits_ref):
    rows = slab_ref[:, CAP : CAP + EXTRA, :].astype(F32).reshape(-1, LANES).astype(BF16)
    shape = (64, rows.shape[0])
    column, line = iota(shape, 1), iota(shape, 0)
    pick = (lax.shift_right_logical(column, 6) == (line & 15)) & (
        (column & 7) == lax.shift_right_logical(line, 4)
    )
    digits_ref[...] = dot(jnp.where(pick, 1.0, 0.0).astype(BF16), rows)


def across_lanes(digits_ref, at, count):
    found = []
    for part in range(count):
        high, low = digits_ref[pl.ds(at + part, 1), :], digits_ref[pl.ds(at + part + 32, 1), :]
        found.append((high * 64.0 + low).astype(I32) - 65)
    return found


def down_rows(digits_ref, at, count):
    same = iota((LANES, LANES), 0) == iota((LANES, LANES), 1)
    parts = []
    for part in range(count):
        high, low = digits_ref[pl.ds(at + part, 1), :], digits_ref[pl.ds(at + part + 32, 1), :]
        parts.append(
            jnp.concatenate([jnp.where(same, high, 0.0), jnp.where(same, low, 0.0)], axis=1)
        )
    left = jnp.concatenate(parts, axis=0).astype(BF16)
    right = jnp.where(iota((2 * LANES, LANES), 0) < LANES, 64.0, 1.0).astype(BF16)
    return dot(left, right).astype(I32) - 65


def low_table(labels):
    line = iota((LOW, LANES), 0)
    return jnp.concatenate(
        [jnp.where(line == (label & (LOW - 1)), 1.0, 0.0).astype(BF16) for label in labels], axis=1
    )


def masked(rows, high, which):
    return jnp.where(high == which, rows, 0.0).astype(BF16)


def counting(high):
    lane = iota(high.shape, 1)
    return jnp.where((high == (lane & 7)) & (lane < 16), 1.0, 0.0).astype(BF16)


def segments(total_ref, left_ref, high_ref, rows_of, digits_ref, steps):
    for step in range(steps):
        left_ref[:, lane_slice(step, 512)] = low_table(across_lanes(digits_ref, 4 * step, 4))
        high_ref[lane_slice(step, 512), :] = lax.shift_right_arithmetic(
            down_rows(digits_ref, 4 * step, 4), 9
        )
    left = left_ref[:, 0 : steps * 512]
    for pair in range(HIGHS // 2):
        right = []
        for step in range(steps):
            high, rows = high_ref[lane_slice(step, 512), :], rows_of(step)
            right.append(
                jnp.concatenate([masked(rows, high, 2 * pair + side) for side in range(2)], axis=1)
            )
        total_ref[:, lane_slice(pair, 2 * LANES)] = dot(left, jnp.concatenate(right, axis=0))
    total_ref[:, HIGHS * LANES :] = dot(left, counting(high_ref[0 : steps * 512, :]))


def add_segments(total_ref, digits_ref, at, rows):
    left = low_table(across_lanes(digits_ref, at, 2))
    high = lax.shift_right_arithmetic(down_rows(digits_ref, at, 2), 9)
    for pair in range(HIGHS // 2):
        right = jnp.concatenate([masked(rows, high, 2 * pair + side) for side in range(2)], axis=1)
        total_ref[:, lane_slice(pair, 2 * LANES)] += dot(left, right)
    total_ref[:, HIGHS * LANES :] += dot(left, counting(high))


def lower_rows(slab_ref, step):
    return slab_ref[lane_slice(step, 32), 0:HALF, :].reshape(512, LANES).astype(F32)


def upper_rows(slab_ref, group):
    return slab_ref[pl.ds(group * 16, 16), HALF:CAP, :].reshape(256, LANES).astype(F32)


def mark_live(digits_ref, live_ref):
    for group in range(live_ref.shape[0]):
        most = jnp.max(digits_ref[16 + 2 * group : 18 + 2 * group, :])
        live_ref[group] = jnp.where(most > 0.0, 1, 0)


def parent_kernel(parent_ref, old_ref, total_hbm, digits_ref, left_ref, high_ref, total_ref, sem):
    parent = parent_ref[...]
    digits_ref[0:32, :] = (lax.shift_right_logical(parent, 6) + 1).astype(F32)
    digits_ref[32:64, :] = ((parent & 63) + 1).astype(F32)
    segments(
        total_ref,
        left_ref,
        high_ref,
        lambda step: old_ref[lane_slice(step, 512), :].astype(F32),
        digits_ref,
        old_ref.shape[0] // 512,
    )
    store = pltpu.make_async_copy(total_ref, total_hbm.at[0], sem)
    store.start()
    store.wait()


def find_parents(digits_ref, parents_ref, table_ref, at, count):
    line = iota((LANES, LANES), 0)
    rows = [(digits_ref[pl.ds(at + n, 1), :], digits_ref[pl.ds(at + n + 32, 1), :]) for n in range(count)]
    left = [jnp.where(line == high.astype(I32) - 1, 1.0, 0.0).astype(BF16) for high, _ in rows]
    found = dot(table_ref[...], jnp.concatenate(left, axis=1))
    for n in range(count):
        chosen = jnp.where((line & 63) == rows[n][1].astype(I32) - 1, found[:, lane_slice(n)], 0.0)
        parents_ref[pl.ds(at + n, 1), :] = jnp.sum(chosen[0:64], axis=0, keepdims=True)
        parents_ref[pl.ds(at + n + 32, 1), :] = jnp.sum(chosen[64:128], axis=0, keepdims=True)


def upper_kernel(
    slab_ref, table_ref, top_ref, start_hbm, send_hbm,
    digits_ref, parents_ref, total_ref, left_ref, high_ref, start_ref, send_ref, right_ref, tail_ref, live_ref,
    sems,
):
    load = pltpu.make_async_copy(start_hbm.at[0], start_ref, sems.at[0])
    load.start()
    slot_digits(slab_ref, digits_ref)
    mark_live(digits_ref, live_ref)
    for step in range(4):
        find_parents(digits_ref, parents_ref, table_ref, 4 * step, 4)
    segments(total_ref, left_ref, high_ref, lambda step: lower_rows(slab_ref, step), parents_ref, 4)

    def more(group, carry):
        @pl.when(live_ref[group] > 0)
        def _():
            find_parents(digits_ref, parents_ref, table_ref, 16 + 2 * group, 2)
            add_segments(total_ref, parents_ref, 16 + 2 * group, upper_rows(slab_ref, group))

        return carry

    lax.fori_loop(0, slab_ref.shape[0] // 16, more, 0)
    load.wait()
    at = slice(HIGHS * LANES, (HIGHS + 1) * LANES)
    weights = total_ref[:, at] + start_ref[:, at]
    coarse = weights.astype(BF16).astype(F32)
    lane = iota((LOW, LANES), 1)
    split = jnp.where(lane < HIGHS, coarse, weights - coarse)
    diagonal = jnp.where(iota((16, LANES), 0) == iota((16, LANES), 1), 1.0, 0.0).astype(BF16)
    across = dot_nt(diagonal, split.astype(BF16))
    tops = []
    stores = []
    for high in range(HIGHS):
        mass = (total_ref[:, lane_slice(high)] + start_ref[:, lane_slice(high)]).astype(BF16)
        for half in range(2):
            send_ref[2 * high + half, 0:32] = mass[half * 256 : (half + 1) * 256].reshape(32, 8, LANES)
        part = (pl.ds(2 * high, 2), pl.ds(0, 32))
        stores.append(pltpu.make_async_copy(send_ref.at[part], send_hbm.at[part], sems.at[1 + high]))
        stores[-1].start()
        right_ref[lane_slice(high, LOW), 0:LANES] = mass
        right_ref[lane_slice(high, LOW), LANES:] = jnp.where((lane & 7) == high, split, 0.0).astype(BF16)
        for part in range(4):
            hit = iota((256, LANES), 0) == top_ref[high * 4 + part : high * 4 + part + 1, :]
            tops.append(jnp.where(hit, 1.0, 0.0).astype(BF16))
    for half in range(2):
        for kind in range(2):
            lines = slice(kind * HIGHS, (kind + 1) * HIGHS)
            for side in range(2):
                tail_ref[pl.ds(side, HIGHS, 2), 2 * kind + half, :] = across[lines, lane_slice(2 * side + half)]
    tops = dot(jnp.concatenate(tops, axis=1), right_ref[...])
    owners = send_ref.shape[0]
    send_ref[:, 32:34] = tops[:, :LANES].astype(BF16).reshape(owners, 2, 8, LANES)
    first = jnp.where(iota((8, LANES), 1) < 16, 1.0, 0.0).astype(BF16)
    heavy = tops[:, LANES:]
    heavy_coarse = heavy.astype(BF16)
    heavy_fine = (heavy - heavy_coarse.astype(F32)).astype(BF16)
    top_weight = (dot_nt(first, heavy_coarse) + dot_nt(first, heavy_fine))[0:1]
    top_coarse = top_weight.astype(BF16).astype(F32)
    for kind, value in enumerate((top_coarse, top_weight - top_coarse)):
        for half in range(2):
            tail_ref[:, 4 + 2 * kind + half, :] = jnp.broadcast_to(value[:, lane_slice(half)], (owners, LANES))
    send_ref[:, 34:35] = tail_ref[...].astype(BF16)[:, None]
    part = (slice(None), pl.ds(32, 3))
    stores.append(pltpu.make_async_copy(send_ref.at[part], send_hbm.at[part], sems.at[1 + HIGHS]))
    stores[-1].start()
    for store in stores:
        store.wait()


def level_kernel(
    slab_ref, old_hbm, level_hbm, residual_hbm,
    digits_ref, total_ref, table_ref, left_ref, high_ref, old_ref, level_ref, residual_ref, live_ref,
    load_sem, level_sems, low_sems, up_sems,
):
    load = pltpu.make_async_copy(old_hbm, old_ref, load_sem)
    load.start()
    slot_digits(slab_ref, digits_ref)
    mark_live(digits_ref, live_ref)
    segments(total_ref, left_ref, high_ref, lambda step: lower_rows(slab_ref, step), digits_ref, 4)
    groups = slab_ref.shape[0] // 16

    def more(group, carry):
        @pl.when(live_ref[group] > 0)
        def _():
            add_segments(total_ref, digits_ref, 16 + 2 * group, upper_rows(slab_ref, group))

        return carry

    lax.fori_loop(0, groups, more, 0)
    load.wait()
    inverse = 1.0 / (total_ref[:, HIGHS * LANES :] + 1.0)
    stores = []
    for high in range(HIGHS):
        lines = lane_slice(high, LOW)
        mass = total_ref[:, lane_slice(high)] + old_ref[lines, :].astype(F32)
        level = mass * jnp.broadcast_to(inverse[:, high : high + 1], mass.shape)
        level_ref[lines, :] = level
        table_ref[:, lane_slice(high)] = level.astype(BF16)
        stores.append(
            pltpu.make_async_copy(level_ref.at[lines], level_hbm.at[lines], level_sems.at[high])
        )
        stores[-1].start()

    def subtract(at, count, rows):
        label = down_rows(digits_ref, at, count)
        low = label & (LOW - 1)
        high = lax.shift_right_arithmetic(label, 9)
        lane = iota(label.shape, 1)
        left = jnp.concatenate(
            [
                jnp.where(low == lane + part * LANES, 1.0, 0.0).astype(BF16)
                for part in range(LOW // LANES)
            ],
            axis=1,
        )
        for pair in range(HIGHS // 2):
            found = dot(left, table_ref[:, lane_slice(pair, 2 * LANES)])
            for side in range(2):
                rows -= jnp.where(high == 2 * pair + side, found[:, lane_slice(side)], 0.0)
        return rows.astype(BF16)

    for step in range(4):
        sources = lane_slice(step, 32)
        residual_ref[sources, 0:HALF, :] = subtract(
            4 * step, 4, lower_rows(slab_ref, step)
        ).reshape(32, HALF, LANES)
        part = (sources, slice(0, HALF))
        stores.append(
            pltpu.make_async_copy(residual_ref.at[part], residual_hbm.at[part], low_sems.at[step])
        )
        stores[-1].start()

    def upper_copy(group):
        part = (pl.ds(group * 16, 16), pl.ds(HALF, HALF))
        return pltpu.make_async_copy(residual_ref.at[part], residual_hbm.at[part], up_sems.at[group])

    def finish(group, carry):
        sources = pl.ds(group * 16, 16)
        @pl.when(live_ref[group] > 0)
        def _():
            residual_ref[sources, HALF:CAP, :] = subtract(
                16 + 2 * group, 2, upper_rows(slab_ref, group)
            ).reshape(16, HALF, LANES)

        @pl.when(live_ref[group] == 0)
        def _():
            residual_ref[sources, HALF:CAP, :] = slab_ref[sources, HALF:CAP, :]

        upper_copy(group).start()
        return carry

    lax.fori_loop(0, groups, finish, 0)
    for store in stores:
        store.wait()

    def settle(group, carry):
        upper_copy(group).wait()
        return carry

    lax.fori_loop(0, groups, settle, 0)


def finish_kernel(parts_ref, send_in, level_ref, send_hbm, column_ref, top_ref, sem):
    total = parts_ref[0].astype(F32)
    for source in range(1, parts_ref.shape[0]):
        total += parts_ref[source].astype(F32)
    tail = total[272:280].T
    me = lax.axis_index("cent")
    chosen = jnp.where(me < 8, tail[:, 4:5] + tail[:, 6:7], tail[:, 5:6] + tail[:, 7:8])
    column_ref[...] = jnp.broadcast_to(chosen, (LANES, LANES))
    weight = column_ref[pl.ds(pl.multiple_of((me % 8) * TOP, TOP), TOP), :]
    top = (total[256:272] / weight).astype(BF16)
    top_ref[...] = jnp.broadcast_to(top[None], top_ref.shape)
    store = pltpu.make_async_copy(top_ref, send_hbm.at[:, pl.ds(CAP, TOP), :], sem)
    store.start()
    for half in range(2):
        weight = tail[:, half : half + 1] + tail[:, half + 2 : half + 3]
        lines = slice(half * LANES, (half + 1) * LANES)
        level_ref[lines, :] = total[lines] / jnp.broadcast_to(weight, (LANES, LANES))
    store.wait()


def unpack_kernel(back_ref, returned_ref, residual_hbm, level_hbm, residual_ref, level_ref, sems):
    groups, owners, rows, lanes = returned_ref.shape
    stores = []
    for pair in range(groups // 2):
        for side in range(2):
            top = returned_ref[2 * pair + side, :, CAP:rows, :].astype(F32)
            level_ref[:, lane_slice(2 * pair + side)] = top.reshape(owners * TOP, lanes)
        right = jnp.concatenate(
            [
                returned_ref[2 * pair + side, :, 0:CAP, :].reshape(owners * CAP, lanes)
                for side in range(2)
            ],
            axis=1,
        )
        at = lane_slice(pair, 2 * lanes)
        stores.append(pltpu.make_async_copy(level_ref.at[:, at], level_hbm.at[:, at], sems.at[2 * pair]))
        stores[-1].start()
        residual_ref[:, at] = dot(back_ref[...], right).astype(BF16)
        stores.append(
            pltpu.make_async_copy(residual_ref.at[:, at], residual_hbm.at[:, at], sems.at[2 * pair + 1])
        )
        stores[-1].start()
    for store in stores:
        store.wait()


def shape(dims, kind):
    return jax.ShapeDtypeStruct(dims, kind)


def swap(value, axes):
    return lax.all_to_all(value, axes, split_axis=0, concat_axis=0, tiled=True)


def on_device(points, assign, parent_one, parent_two, old_level_one):
    count, width = points.shape
    owners = lax.axis_size("cent")
    groups = lax.axis_size("dp")
    devices = owners * groups
    block, lanes = old_level_one.shape
    slots = owners * CAP
    rows = CAP + EXTRA
    total_dims = (LOW, (HIGHS + 1) * LANES)
    work = 2 * LOW * block * (HIGHS + 1) * LANES

    send, back = call(
        pack_kernel,
        (shape((groups, owners, rows, lanes), BF16), shape((count, slots), BF16)),
        [HBM, HBM],
        (HBM, HBM),
        FULL,
        [
            pltpu.VMEM((1, count), I32),
            pltpu.VMEM((count, width), BF16),
            pltpu.VMEM((groups, owners, rows, lanes), BF16),
            pltpu.VMEM((count, slots), BF16),
            pltpu.SemaphoreType.DMA((2 + groups // 2 + groups,)),
        ],
        flops=2 * slots * count * width,
    )(assign.reshape(1, count), points)
    slab = swap(send.reshape(devices, rows, lanes), BOTH)

    start = call(
        parent_kernel,
        shape((SPARE, *total_dims), F32),
        [VMEM, VMEM],
        HBM,
        FULL,
        [
            pltpu.VMEM((64, LANES), F32),
            pltpu.VMEM((LOW, block), BF16),
            pltpu.VMEM((block, LANES), I32),
            pltpu.VMEM(total_dims, F32),
            pltpu.SemaphoreType.DMA(()),
        ],
        flops=work,
    )(parent_one.reshape(block // LANES, LANES), old_level_one)
    grid = parent_one.reshape(64, 64).T
    table = jnp.concatenate([lax.shift_right_logical(grid, 6), grid & 63], axis=0) + 1
    table = jnp.pad(table, ((0, 0), (0, 64))).astype(BF16)

    share = call(
        upper_kernel,
        shape((owners, 35, 8, lanes), BF16),
        [VMEM, VMEM, VMEM, HBM],
        HBM,
        UPPER,
        [
            pltpu.VMEM((64, LANES), F32),
            pltpu.VMEM((64, LANES), F32),
            pltpu.VMEM(total_dims, F32),
            pltpu.VMEM((LOW, 2048), BF16),
            pltpu.VMEM((2048, LANES), I32),
            pltpu.VMEM(total_dims, F32),
            pltpu.VMEM((owners, 35, 8, lanes), BF16),
            pltpu.VMEM((HIGHS * LOW, 2 * LANES), BF16),
            pltpu.VMEM((owners, 8, lanes), F32),
            pltpu.SMEM((groups,), I32),
            pltpu.SemaphoreType.DMA((2 + HIGHS,)),
        ],
        flops=work,
    )(slab, table, parent_two.reshape(-1, LANES), start)
    shares = swap(share, "cent")

    level_one, answer = call(
        level_kernel,
        (shape((block, lanes), F32), shape((devices, CAP + TOP, lanes), BF16)),
        [VMEM, HBM],
        (HBM, HBM),
        LEVEL,
        [
            pltpu.VMEM((64, LANES), F32),
            pltpu.VMEM(total_dims, F32),
            pltpu.VMEM((LOW, HIGHS * LANES), BF16),
            pltpu.VMEM((LOW, 2048), BF16),
            pltpu.VMEM((2048, LANES), I32),
            pltpu.VMEM((block, lanes), BF16),
            pltpu.VMEM((block, lanes), F32),
            pltpu.VMEM((devices, CAP, lanes), BF16),
            pltpu.SMEM((groups,), I32),
            pltpu.SemaphoreType.DMA(()),
            pltpu.SemaphoreType.DMA((HIGHS,)),
            pltpu.SemaphoreType.DMA((4,)),
            pltpu.SemaphoreType.DMA((groups,)),
        ],
        flops=2 * work,
    )(slab, old_level_one)

    level_two, answer = call(
        finish_kernel,
        (shape((256, lanes), F32), shape((devices, CAP + TOP, lanes), BF16)),
        [VMEM, HBM],
        (VMEM, HBM),
        SMALL,
        [
            pltpu.VMEM((LANES, LANES), F32),
            pltpu.VMEM((devices, TOP, lanes), BF16),
            pltpu.SemaphoreType.DMA(()),
        ],
        alias={1: 1},
    )(shares.reshape(owners, -1, lanes), answer)
    returned = swap(answer, BOTH)
    residual, level_three = call(
        unpack_kernel,
        (shape((count, width), BF16), shape((owners * TOP, width), F32)),
        [VMEM, VMEM],
        (HBM, HBM),
        SMALL,
        [
            pltpu.VMEM((count, width), BF16),
            pltpu.VMEM((owners * TOP, width), F32),
            pltpu.SemaphoreType.DMA((groups,)),
        ],
        flops=2 * slots * count * width,
    )(back, returned.reshape(groups, owners, CAP + TOP, lanes))
    return (level_one, level_two, level_three, residual)


def solution(mesh):
    in_specs = (P(("dp", "cent"), None), P(("dp", "cent")), P("cent"), P(), P("cent", "dp"))
    out_specs = (P("cent", "dp"), P("cent", "dp"), P(), P(("dp", "cent"), None))
    return jax.shard_map(
        on_device, mesh=mesh, in_specs=in_specs, out_specs=out_specs, check_vma=False
    )
```

```python
import jax
import jax.numpy as jnp
from jax import lax
from jax.experimental import pallas as pl
from jax.experimental.pallas import tpu as pltpu
from jax.sharding import PartitionSpec as P

F32 = jnp.float32
BF16 = jnp.bfloat16
I32 = jnp.int32
LANES = 128
LOW = 512
HIGHS = 8
CAP = 32
HALF = 16
EXTRA = 8
TOP = 16
BOTH = ("dp", "cent")


def iota(shape, axis):
    return lax.broadcasted_iota(I32, shape, axis)


def dot(left, right):
    return jnp.dot(left, right, preferred_element_type=F32)


def dot_nt(left, right):
    return lax.dot_general(left, right, (((1,), (1,)), ((), ())), preferred_element_type=F32)


def lane_slice(at, width=LANES):
    return slice(at * width, (at + 1) * width)


HBM = pl.BlockSpec(memory_space=pltpu.HBM)
VMEM = pl.BlockSpec(memory_space=pltpu.VMEM)


FULL = 62_900_000
UPPER = 50_000_000
LEVEL = 48_000_000
SMALL = 16_000_000
SPARE = 12


def call(body, out_shape, ins, outs, vmem, scratch=(), flops=0, size=4 << 20, alias=None):
    return pl.pallas_call(
        body,
        out_shape=out_shape,
        in_specs=ins,
        out_specs=outs,
        scratch_shapes=list(scratch),
        input_output_aliases=alias or {},
        compiler_params=pltpu.CompilerParams(vmem_limit_bytes=vmem),
        cost_estimate=pl.CostEstimate(flops=flops, bytes_accessed=size, transcendentals=0),
    )


def pack_kernel(
    assign_hbm, points_hbm, send_hbm, back_hbm, assign_ref, points_ref, send_ref, back_ref, sems
):
    owners = send_ref.shape[1]
    parts = send_ref.shape[0]
    count = points_ref.shape[0]
    load = pltpu.make_async_copy(assign_hbm, assign_ref, sems.at[0])
    load.start()
    loads = []
    for pair in range(parts // 2):
        at = lane_slice(pair, 2 * LANES)
        loads.append(
            pltpu.make_async_copy(points_hbm.at[:, at], points_ref.at[:, at], sems.at[1 + pair])
        )
        loads[-1].start()
    before = jnp.where(iota((count, count), 0) <= iota((count, count), 1), 1.0, 0.0).astype(BF16)
    same = jnp.where(iota((count, count), 0) == iota((count, count), 1), 1.0, 0.0).astype(BF16)
    load.wait()
    label = assign_ref[...]
    owner = lax.shift_right_logical(label, 12)
    local = label & 4095
    mine = iota((owners, count), 0) == owner
    mine_f = jnp.where(mine, 1.0, 0.0)
    running = dot(mine_f.astype(BF16), before)
    place = jnp.sum(running * mine_f, axis=0, keepdims=True).astype(I32) - 1
    slot = owner * CAP + place
    table = jnp.where(iota((owners * CAP, count), 0) == slot, 1.0, 0.0).astype(BF16)
    shift = (lax.axis_index("cent") % 8) * HALF
    line = iota((LANES, count), 0)
    row = iota((owners, EXTRA, LANES), 1)
    digits = [(lax.shift_right_logical(local, 6) + 1).astype(F32), ((local & 63) + 1).astype(F32)]
    digits = [(mine_f * digit).astype(BF16) for digit in digits]
    extra = jnp.zeros((owners, EXTRA, LANES), F32)
    for half in range(2):
        first = half * HALF
        inside = (place >= first) & (place < first + HALF)
        lane = jnp.where(inside, place - first + shift, -1)
        lane_table = jnp.where(line == lane, 1.0, 0.0).astype(BF16)
        for kind in range(2):
            found = dot_nt(digits[kind], lane_table)
            extra = jnp.where(row == 2 * kind + half, found[:, None, :], extra)
    extra = extra.astype(BF16)
    stores = []
    for part in range(parts):
        if part % 2 == 0:
            loads[part // 2].wait()
            both = dot(table, points_ref[:, lane_slice(part // 2, 2 * LANES)]).astype(BF16)
        rows = both[:, lane_slice(part % 2)]
        send_ref[part, :, 0:CAP, :] = rows.reshape(owners, CAP, LANES)
        send_ref[part, :, CAP : CAP + EXTRA, :] = extra
        stores.append(
            pltpu.make_async_copy(send_ref.at[part], send_hbm.at[part], sems.at[1 + parts // 2 + part])
        )
        stores[-1].start()
        if part == 0:
            back_ref[...] = dot_nt(same, table).astype(BF16)
            stores.append(pltpu.make_async_copy(back_ref, back_hbm, sems.at[1 + parts // 2 + parts]))
            stores[-1].start()
    for store in stores:
        store.wait()


def slot_digits(slab_ref, digits_ref):
    rows = slab_ref[:, CAP : CAP + EXTRA, :].astype(F32).reshape(-1, LANES).astype(BF16)
    shape = (64, rows.shape[0])
    column, line = iota(shape, 1), iota(shape, 0)
    pick = (lax.shift_right_logical(column, 6) == (line & 15)) & (
        (column & 7) == lax.shift_right_logical(line, 4)
    )
    digits_ref[...] = dot(jnp.where(pick, 1.0, 0.0).astype(BF16), rows)


def across_lanes(digits_ref, at, count):
    found = []
    for part in range(count):
        high, low = digits_ref[pl.ds(at + part, 1), :], digits_ref[pl.ds(at + part + 32, 1), :]
        found.append((high * 64.0 + low).astype(I32) - 65)
    return found


def down_rows(digits_ref, at, count):
    same = iota((LANES, LANES), 0) == iota((LANES, LANES), 1)
    parts = []
    for part in range(count):
        high, low = digits_ref[pl.ds(at + part, 1), :], digits_ref[pl.ds(at + part + 32, 1), :]
        parts.append(
            jnp.concatenate([jnp.where(same, high, 0.0), jnp.where(same, low, 0.0)], axis=1)
        )
    left = jnp.concatenate(parts, axis=0).astype(BF16)
    right = jnp.where(iota((2 * LANES, LANES), 0) < LANES, 64.0, 1.0).astype(BF16)
    return dot(left, right).astype(I32) - 65


def low_table(labels):
    line = iota((LOW, LANES), 0)
    return jnp.concatenate(
        [jnp.where(line == (label & (LOW - 1)), 1.0, 0.0).astype(BF16) for label in labels], axis=1
    )


def masked(rows, high, which):
    return jnp.where(high == which, rows, 0.0).astype(BF16)


def counting(high):
    lane = iota(high.shape, 1)
    return jnp.where((high == (lane & 7)) & (lane < 16), 1.0, 0.0).astype(BF16)


def segments(total_ref, left_ref, high_ref, rows_of, digits_ref, steps):
    for step in range(steps):
        left_ref[:, lane_slice(step, 512)] = low_table(across_lanes(digits_ref, 4 * step, 4))
        high_ref[lane_slice(step, 512), :] = lax.shift_right_arithmetic(
            down_rows(digits_ref, 4 * step, 4), 9
        )
    left = left_ref[:, 0 : steps * 512]
    for pair in range(HIGHS // 2):
        right = []
        for step in range(steps):
            high, rows = high_ref[lane_slice(step, 512), :], rows_of(step)
            right.append(
                jnp.concatenate([masked(rows, high, 2 * pair + side) for side in range(2)], axis=1)
            )
        total_ref[:, lane_slice(pair, 2 * LANES)] = dot(left, jnp.concatenate(right, axis=0))
    total_ref[:, HIGHS * LANES :] = dot(left, counting(high_ref[0 : steps * 512, :]))


def add_segments(total_ref, digits_ref, at, rows):
    left = low_table(across_lanes(digits_ref, at, 2))
    high = lax.shift_right_arithmetic(down_rows(digits_ref, at, 2), 9)
    for pair in range(HIGHS // 2):
        right = jnp.concatenate([masked(rows, high, 2 * pair + side) for side in range(2)], axis=1)
        total_ref[:, lane_slice(pair, 2 * LANES)] += dot(left, right)
    total_ref[:, HIGHS * LANES :] += dot(left, counting(high))


def lower_rows(slab_ref, step):
    return slab_ref[lane_slice(step, 32), 0:HALF, :].reshape(512, LANES).astype(F32)


def upper_rows(slab_ref, group):
    return slab_ref[pl.ds(group * 16, 16), HALF:CAP, :].reshape(256, LANES).astype(F32)


def mark_live(digits_ref, live_ref):
    for group in range(live_ref.shape[0]):
        most = jnp.max(digits_ref[16 + 2 * group : 18 + 2 * group, :])
        live_ref[group] = jnp.where(most > 0.0, 1, 0)


def parent_kernel(parent_ref, old_ref, total_hbm, digits_ref, left_ref, high_ref, total_ref, sem):
    parent = parent_ref[...]
    digits_ref[0:32, :] = (lax.shift_right_logical(parent, 6) + 1).astype(F32)
    digits_ref[32:64, :] = ((parent & 63) + 1).astype(F32)
    segments(
        total_ref,
        left_ref,
        high_ref,
        lambda step: old_ref[lane_slice(step, 512), :].astype(F32),
        digits_ref,
        old_ref.shape[0] // 512,
    )
    store = pltpu.make_async_copy(total_ref, total_hbm.at[0], sem)
    store.start()
    store.wait()


def find_parents(digits_ref, parents_ref, table_ref, at, count):
    line = iota((LANES, LANES), 0)
    rows = [(digits_ref[pl.ds(at + n, 1), :], digits_ref[pl.ds(at + n + 32, 1), :]) for n in range(count)]
    left = [jnp.where(line == high.astype(I32) - 1, 1.0, 0.0).astype(BF16) for high, _ in rows]
    found = dot(table_ref[...], jnp.concatenate(left, axis=1))
    for n in range(count):
        chosen = jnp.where((line & 63) == rows[n][1].astype(I32) - 1, found[:, lane_slice(n)], 0.0)
        parents_ref[pl.ds(at + n, 1), :] = jnp.sum(chosen[0:64], axis=0, keepdims=True)
        parents_ref[pl.ds(at + n + 32, 1), :] = jnp.sum(chosen[64:128], axis=0, keepdims=True)


def upper_kernel(
    slab_ref, table_ref, top_ref, start_hbm, send_hbm,
    digits_ref, parents_ref, total_ref, left_ref, high_ref, start_ref, send_ref, right_ref, tail_ref, live_ref,
    sems,
):
    load = pltpu.make_async_copy(start_hbm.at[0], start_ref, sems.at[0])
    load.start()
    slot_digits(slab_ref, digits_ref)
    mark_live(digits_ref, live_ref)
    for step in range(4):
        find_parents(digits_ref, parents_ref, table_ref, 4 * step, 4)
    segments(total_ref, left_ref, high_ref, lambda step: lower_rows(slab_ref, step), parents_ref, 4)

    def more(group, carry):
        @pl.when(live_ref[group] > 0)
        def _():
            find_parents(digits_ref, parents_ref, table_ref, 16 + 2 * group, 2)
            add_segments(total_ref, parents_ref, 16 + 2 * group, upper_rows(slab_ref, group))

        return carry

    lax.fori_loop(0, slab_ref.shape[0] // 16, more, 0)
    load.wait()
    at = slice(HIGHS * LANES, (HIGHS + 1) * LANES)
    weights = total_ref[:, at] + start_ref[:, at]
    coarse = weights.astype(BF16).astype(F32)
    lane = iota((LOW, LANES), 1)
    split = jnp.where(lane < HIGHS, coarse, weights - coarse)
    diagonal = jnp.where(iota((16, LANES), 0) == iota((16, LANES), 1), 1.0, 0.0).astype(BF16)
    across = dot_nt(diagonal, split.astype(BF16))
    tops = []
    stores = []
    for high in range(HIGHS):
        mass = (total_ref[:, lane_slice(high)] + start_ref[:, lane_slice(high)]).astype(BF16)
        for half in range(2):
            send_ref[2 * high + half, 0:32] = mass[half * 256 : (half + 1) * 256].reshape(32, 8, LANES)
        part = (pl.ds(2 * high, 2), pl.ds(0, 32))
        stores.append(pltpu.make_async_copy(send_ref.at[part], send_hbm.at[part], sems.at[1 + high]))
        stores[-1].start()
        right_ref[lane_slice(high, LOW), 0:LANES] = mass
        right_ref[lane_slice(high, LOW), LANES:] = jnp.where((lane & 7) == high, split, 0.0).astype(BF16)
        for part in range(4):
            hit = iota((256, LANES), 0) == top_ref[high * 4 + part : high * 4 + part + 1, :]
            tops.append(jnp.where(hit, 1.0, 0.0).astype(BF16))
    for half in range(2):
        for kind in range(2):
            lines = slice(kind * HIGHS, (kind + 1) * HIGHS)
            for side in range(2):
                tail_ref[pl.ds(side, HIGHS, 2), 2 * kind + half, :] = across[lines, lane_slice(2 * side + half)]
    tops = dot(jnp.concatenate(tops, axis=1), right_ref[...])
    owners = send_ref.shape[0]
    send_ref[:, 32:34] = tops[:, :LANES].astype(BF16).reshape(owners, 2, 8, LANES)
    first = jnp.where(iota((8, LANES), 1) < 16, 1.0, 0.0).astype(BF16)
    heavy = tops[:, LANES:]
    heavy_coarse = heavy.astype(BF16)
    heavy_fine = (heavy - heavy_coarse.astype(F32)).astype(BF16)
    top_weight = (dot_nt(first, heavy_coarse) + dot_nt(first, heavy_fine))[0:1]
    top_coarse = top_weight.astype(BF16).astype(F32)
    for kind, value in enumerate((top_coarse, top_weight - top_coarse)):
        for half in range(2):
            tail_ref[:, 4 + 2 * kind + half, :] = jnp.broadcast_to(value[:, lane_slice(half)], (owners, LANES))
    send_ref[:, 34:35] = tail_ref[...].astype(BF16)[:, None]
    part = (slice(None), pl.ds(32, 3))
    stores.append(pltpu.make_async_copy(send_ref.at[part], send_hbm.at[part], sems.at[1 + HIGHS]))
    stores[-1].start()
    for store in stores:
        store.wait()


def level_kernel(
    slab_ref, old_hbm, level_hbm, residual_hbm,
    digits_ref, total_ref, table_ref, left_ref, high_ref, old_ref, level_ref, residual_ref, live_ref,
    load_sem, level_sems, low_sems, up_sems,
):
    load = pltpu.make_async_copy(old_hbm, old_ref, load_sem)
    load.start()
    slot_digits(slab_ref, digits_ref)
    mark_live(digits_ref, live_ref)
    segments(total_ref, left_ref, high_ref, lambda step: lower_rows(slab_ref, step), digits_ref, 4)
    groups = slab_ref.shape[0] // 16

    def more(group, carry):
        @pl.when(live_ref[group] > 0)
        def _():
            add_segments(total_ref, digits_ref, 16 + 2 * group, upper_rows(slab_ref, group))

        return carry

    lax.fori_loop(0, groups, more, 0)
    load.wait()
    inverse = 1.0 / (total_ref[:, HIGHS * LANES :] + 1.0)
    stores = []
    for high in range(HIGHS):
        lines = lane_slice(high, LOW)
        mass = total_ref[:, lane_slice(high)] + old_ref[lines, :].astype(F32)
        level = mass * jnp.broadcast_to(inverse[:, high : high + 1], mass.shape)
        level_ref[lines, :] = level
        table_ref[:, lane_slice(high)] = level.astype(BF16)
        stores.append(
            pltpu.make_async_copy(level_ref.at[lines], level_hbm.at[lines], level_sems.at[high])
        )
        stores[-1].start()

    def subtract(at, count, rows):
        label = down_rows(digits_ref, at, count)
        low = label & (LOW - 1)
        high = lax.shift_right_arithmetic(label, 9)
        lane = iota(label.shape, 1)
        left = jnp.concatenate(
            [
                jnp.where(low == lane + part * LANES, 1.0, 0.0).astype(BF16)
                for part in range(LOW // LANES)
            ],
            axis=1,
        )
        for pair in range(HIGHS // 2):
            found = dot(left, table_ref[:, lane_slice(pair, 2 * LANES)])
            for side in range(2):
                rows -= jnp.where(high == 2 * pair + side, found[:, lane_slice(side)], 0.0)
        return rows.astype(BF16)

    for step in range(4):
        sources = lane_slice(step, 32)
        residual_ref[sources, 0 : HALF // 8] = subtract(
            4 * step, 4, lower_rows(slab_ref, step)
        ).reshape(32, HALF // 8, 8, LANES)
        part = (sources, slice(0, HALF // 8))
        stores.append(
            pltpu.make_async_copy(residual_ref.at[part], residual_hbm.at[part], low_sems.at[step])
        )
        stores[-1].start()

    def upper_copy(group):
        part = (pl.ds(group * 16, 16), pl.ds(HALF // 8, HALF // 8))
        return pltpu.make_async_copy(residual_ref.at[part], residual_hbm.at[part], up_sems.at[group])

    def finish(group, carry):
        sources = pl.ds(group * 16, 16)
        @pl.when(live_ref[group] > 0)
        def _():
            residual_ref[sources, HALF // 8 : CAP // 8] = subtract(
                16 + 2 * group, 2, upper_rows(slab_ref, group)
            ).reshape(16, HALF // 8, 8, LANES)

        @pl.when(live_ref[group] == 0)
        def _():
            empty = slab_ref[sources, HALF:CAP, :]
            residual_ref[sources, HALF // 8 : CAP // 8] = empty.reshape(16, HALF // 8, 8, LANES)

        upper_copy(group).start()
        return carry

    lax.fori_loop(0, groups, finish, 0)
    for store in stores:
        store.wait()

    def settle(group, carry):
        upper_copy(group).wait()
        return carry

    lax.fori_loop(0, groups, settle, 0)


def finish_kernel(parts_ref, send_in, level_ref, send_hbm, column_ref, top_ref, sem):
    total = parts_ref[0].astype(F32)
    for source in range(1, parts_ref.shape[0]):
        total += parts_ref[source].astype(F32)
    tail = total[272:280].T
    me = lax.axis_index("cent")
    owners = parts_ref.shape[0]
    chosen = jnp.where(me < 8, tail[:, 4:5] + tail[:, 6:7], tail[:, 5:6] + tail[:, 7:8])
    column_ref[...] = jnp.broadcast_to(chosen, (LANES, LANES))
    weight = column_ref[pl.ds(pl.multiple_of((me % 8) * TOP, TOP), TOP), :]
    top = (total[256:272] / weight).astype(BF16)
    for group in range(top_ref.shape[0] // owners):
        first = group % 2 * (TOP // 2)
        part = jnp.broadcast_to(top[first : first + TOP // 2][None, None], (owners, 1, TOP // 2, LANES))
        top_ref[group * owners : (group + 1) * owners] = part
    store = pltpu.make_async_copy(top_ref, send_hbm.at[:, pl.ds(CAP // 8, 1)], sem)
    store.start()
    for half in range(2):
        weight = tail[:, half : half + 1] + tail[:, half + 2 : half + 3]
        lines = slice(half * LANES, (half + 1) * LANES)
        level_ref[lines, :] = total[lines] / jnp.broadcast_to(weight, (LANES, LANES))
    store.wait()


def unpack_kernel(back_ref, returned_ref, residual_hbm, level_hbm, residual_ref, level_ref, sems):
    groups, owners, rows, lanes = returned_ref.shape
    core = lax.axis_index("dp") % 2
    stores = []
    for pair in range(groups // 2):
        for side in range(2):
            top = returned_ref[2 * pair + side, :, CAP:rows, :].astype(F32)
            level_ref[:, 0, :, lane_slice(2 * pair + side)] = top
        right = jnp.concatenate(
            [
                returned_ref[2 * pair + side, :, 0:CAP, :].reshape(owners * CAP, lanes)
                for side in range(2)
            ],
            axis=1,
        )
        at = lane_slice(pair, 2 * lanes)
        residual_ref[:, at] = dot(back_ref[...], right).astype(BF16)
        stores.append(pltpu.make_async_copy(residual_ref.at[:, at], residual_hbm.at[:, at], sems.at[pair]))
        stores[-1].start()
    stores.append(pltpu.make_async_copy(level_ref, level_hbm.at[:, pl.ds(core, 1)], sems.at[groups // 2]))
    stores[-1].start()
    for store in stores:
        store.wait()


def other_kernel(parts_ref, level_in, level_hbm, level_ref, sem):
    core = lax.axis_index("dp") % 2
    for group in range(parts_ref.shape[0]):
        level_ref[:, 0, :, lane_slice(group)] = parts_ref[group].astype(F32)
    store = pltpu.make_async_copy(level_ref, level_hbm.at[:, pl.ds(1 - core, 1)], sem)
    store.start()
    store.wait()


def shape(dims, kind):
    return jax.ShapeDtypeStruct(dims, kind)


def swap(value, axes):
    return lax.all_to_all(value, axes, split_axis=0, concat_axis=0, tiled=True)


def on_device(points, assign, parent_one, parent_two, old_level_one):
    count, width = points.shape
    owners = lax.axis_size("cent")
    groups = lax.axis_size("dp")
    devices = owners * groups
    block, lanes = old_level_one.shape
    slots = owners * CAP
    rows = CAP + EXTRA
    total_dims = (LOW, (HIGHS + 1) * LANES)
    answer_dims = (devices, (CAP + TOP // 2) // 8, 8, lanes)
    work = 2 * LOW * block * (HIGHS + 1) * LANES

    send, back = call(
        pack_kernel,
        (shape((groups, owners, rows, lanes), BF16), shape((count, slots), BF16)),
        [HBM, HBM],
        (HBM, HBM),
        FULL,
        [
            pltpu.VMEM((1, count), I32),
            pltpu.VMEM((count, width), BF16),
            pltpu.VMEM((groups, owners, rows, lanes), BF16),
            pltpu.VMEM((count, slots), BF16),
            pltpu.SemaphoreType.DMA((2 + groups // 2 + groups,)),
        ],
        flops=2 * slots * count * width,
    )(assign.reshape(1, count), points)
    slab = swap(send.reshape(devices, rows, lanes), BOTH)

    start = call(
        parent_kernel,
        shape((SPARE, *total_dims), F32),
        [VMEM, VMEM],
        HBM,
        FULL,
        [
            pltpu.VMEM((64, LANES), F32),
            pltpu.VMEM((LOW, block), BF16),
            pltpu.VMEM((block, LANES), I32),
            pltpu.VMEM(total_dims, F32),
            pltpu.SemaphoreType.DMA(()),
        ],
        flops=work,
    )(parent_one.reshape(block // LANES, LANES), old_level_one)
    grid = parent_one.reshape(64, 64).T
    table = jnp.concatenate([lax.shift_right_logical(grid, 6), grid & 63], axis=0) + 1
    table = jnp.pad(table, ((0, 0), (0, 64))).astype(BF16)

    share = call(
        upper_kernel,
        shape((owners, 35, 8, lanes), BF16),
        [VMEM, VMEM, VMEM, HBM],
        HBM,
        UPPER,
        [
            pltpu.VMEM((64, LANES), F32),
            pltpu.VMEM((64, LANES), F32),
            pltpu.VMEM(total_dims, F32),
            pltpu.VMEM((LOW, 2048), BF16),
            pltpu.VMEM((2048, LANES), I32),
            pltpu.VMEM(total_dims, F32),
            pltpu.VMEM((owners, 35, 8, lanes), BF16),
            pltpu.VMEM((HIGHS * LOW, 2 * LANES), BF16),
            pltpu.VMEM((owners, 8, lanes), F32),
            pltpu.SMEM((groups,), I32),
            pltpu.SemaphoreType.DMA((2 + HIGHS,)),
        ],
        flops=work,
    )(slab, table, parent_two.reshape(-1, LANES), start)
    shares = swap(share, "cent")

    level_one, answer = call(
        level_kernel,
        (shape((block, lanes), F32), shape(answer_dims, BF16)),
        [VMEM, HBM],
        (HBM, HBM),
        LEVEL,
        [
            pltpu.VMEM((64, LANES), F32),
            pltpu.VMEM(total_dims, F32),
            pltpu.VMEM((LOW, HIGHS * LANES), BF16),
            pltpu.VMEM((LOW, 2048), BF16),
            pltpu.VMEM((2048, LANES), I32),
            pltpu.VMEM((block, lanes), BF16),
            pltpu.VMEM((block, lanes), F32),
            pltpu.VMEM((devices, CAP // 8, 8, lanes), BF16),
            pltpu.SMEM((groups,), I32),
            pltpu.SemaphoreType.DMA(()),
            pltpu.SemaphoreType.DMA((HIGHS,)),
            pltpu.SemaphoreType.DMA((4,)),
            pltpu.SemaphoreType.DMA((groups,)),
        ],
        flops=2 * work,
    )(slab, old_level_one)

    level_two, answer = call(
        finish_kernel,
        (shape((256, lanes), F32), shape(answer_dims, BF16)),
        [VMEM, HBM],
        (VMEM, HBM),
        SMALL,
        [
            pltpu.VMEM((LANES, LANES), F32),
            pltpu.VMEM((devices, 1, TOP // 2, lanes), BF16),
            pltpu.SemaphoreType.DMA(()),
        ],
        alias={1: 1},
    )(shares.reshape(owners, -1, lanes), answer)
    returned = swap(answer, BOTH)
    half = returned[:, CAP // 8]
    half = lax.ppermute(half, "dp", [(group, group ^ 1) for group in range(groups)])
    top_dims = (owners, 2, TOP // 2, width)
    residual, level_three = call(
        unpack_kernel,
        (shape((count, width), BF16), shape(top_dims, F32)),
        [VMEM, VMEM],
        (HBM, HBM),
        SMALL,
        [
            pltpu.VMEM((count, width), BF16),
            pltpu.VMEM((owners, 1, TOP // 2, width), F32),
            pltpu.SemaphoreType.DMA((1 + groups // 2,)),
        ],
        flops=2 * slots * count * width,
    )(back, returned.reshape(groups, owners, CAP + TOP // 2, lanes))
    level_three = call(
        other_kernel,
        shape(top_dims, F32),
        [VMEM, HBM],
        HBM,
        SMALL,
        [pltpu.VMEM((owners, 1, TOP // 2, width), F32), pltpu.SemaphoreType.DMA(())],
        alias={1: 0},
    )(half.reshape(groups, owners, TOP // 2, lanes), level_three)
    level_three = level_three.reshape(owners * TOP, width)
    return (level_one, level_two, level_three, residual)


def solution(mesh):
    in_specs = (P(("dp", "cent"), None), P(("dp", "cent")), P("cent"), P(), P("cent", "dp"))
    out_specs = (P("cent", "dp"), P("cent", "dp"), P(), P(("dp", "cent"), None))
    return jax.shard_map(
        on_device, mesh=mesh, in_specs=in_specs, out_specs=out_specs, check_vma=False
    )
```

```python
import jax
import jax.numpy as jnp
from jax import lax
from jax.experimental import pallas as pl
from jax.experimental.pallas import tpu as pltpu
from jax.sharding import PartitionSpec as P

F32 = jnp.float32
BF16 = jnp.bfloat16
I32 = jnp.int32
LANES = 128
LOW = 512
HIGHS = 8
CAP = 32
HALF = 16
EXTRA = 8
TOP = 16
BOTH = ("dp", "cent")


def iota(shape, axis):
    return lax.broadcasted_iota(I32, shape, axis)


def dot(left, right):
    return jnp.dot(left, right, preferred_element_type=F32)


def dot_nt(left, right):
    return lax.dot_general(left, right, (((1,), (1,)), ((), ())), preferred_element_type=F32)


def lane_slice(at, width=LANES):
    return slice(at * width, (at + 1) * width)


HBM = pl.BlockSpec(memory_space=pltpu.HBM)
VMEM = pl.BlockSpec(memory_space=pltpu.VMEM)


FULL = 62_900_000
UPPER = 48_000_000
LEVEL = 48_000_000
SMALL = 16_000_000


def call(body, out_shape, ins, outs, vmem, scratch=(), flops=0, size=4 << 20, alias=None):
    return pl.pallas_call(
        body,
        out_shape=out_shape,
        in_specs=ins,
        out_specs=outs,
        scratch_shapes=list(scratch),
        input_output_aliases=alias or {},
        compiler_params=pltpu.CompilerParams(vmem_limit_bytes=vmem),
        cost_estimate=pl.CostEstimate(flops=flops, bytes_accessed=size, transcendentals=0),
    )


def pack_kernel(
    assign_hbm, points_hbm, send_hbm, back_hbm, assign_ref, points_ref, send_ref, back_ref, sems
):
    owners = send_ref.shape[1]
    parts = send_ref.shape[0]
    count = points_ref.shape[0]
    load = pltpu.make_async_copy(assign_hbm, assign_ref, sems.at[0])
    load.start()
    loads = []
    for pair in range(parts // 2):
        at = lane_slice(pair, 2 * LANES)
        loads.append(
            pltpu.make_async_copy(points_hbm.at[:, at], points_ref.at[:, at], sems.at[1 + pair])
        )
        loads[-1].start()
    before = jnp.where(iota((count, count), 0) <= iota((count, count), 1), 1.0, 0.0).astype(BF16)
    same = jnp.where(iota((count, count), 0) == iota((count, count), 1), 1.0, 0.0).astype(BF16)
    load.wait()
    label = assign_ref[...]
    owner = lax.shift_right_logical(label, 12)
    local = label & 4095
    mine = iota((owners, count), 0) == owner
    mine_f = jnp.where(mine, 1.0, 0.0)
    running = dot(mine_f.astype(BF16), before)
    place = jnp.sum(running * mine_f, axis=0, keepdims=True).astype(I32) - 1
    slot = owner * CAP + place
    table = jnp.where(iota((owners * CAP, count), 0) == slot, 1.0, 0.0).astype(BF16)
    shift = (lax.axis_index("cent") % 8) * HALF
    line = iota((LANES, count), 0)
    row = iota((owners, EXTRA, LANES), 1)
    digits = [(lax.shift_right_logical(local, 6) + 1).astype(F32), ((local & 63) + 1).astype(F32)]
    digits = [(mine_f * digit).astype(BF16) for digit in digits]
    extra = jnp.zeros((owners, EXTRA, LANES), F32)
    for half in range(2):
        first = half * HALF
        inside = (place >= first) & (place < first + HALF)
        lane = jnp.where(inside, place - first + shift, -1)
        lane_table = jnp.where(line == lane, 1.0, 0.0).astype(BF16)
        for kind in range(2):
            found = dot_nt(digits[kind], lane_table)
            extra = jnp.where(row == 2 * kind + half, found[:, None, :], extra)
    extra = extra.astype(BF16)
    stores = []
    for part in range(parts):
        if part % 2 == 0:
            loads[part // 2].wait()
            both = dot(table, points_ref[:, lane_slice(part // 2, 2 * LANES)]).astype(BF16)
        rows = both[:, lane_slice(part % 2)]
        send_ref[part, :, 0:CAP, :] = rows.reshape(owners, CAP, LANES)
        send_ref[part, :, CAP : CAP + EXTRA, :] = extra
        stores.append(
            pltpu.make_async_copy(send_ref.at[part], send_hbm.at[part], sems.at[1 + parts // 2 + part])
        )
        stores[-1].start()
        if part == 0:
            back_ref[...] = dot_nt(same, table).astype(BF16)
            stores.append(pltpu.make_async_copy(back_ref, back_hbm, sems.at[1 + parts // 2 + parts]))
            stores[-1].start()
    for store in stores:
        store.wait()


def slot_digits(slab_ref, digits_ref):
    rows = slab_ref[:, CAP : CAP + EXTRA, :].astype(F32).reshape(-1, LANES).astype(BF16)
    shape = (64, rows.shape[0])
    column, line = iota(shape, 1), iota(shape, 0)
    pick = (lax.shift_right_logical(column, 6) == (line & 15)) & (
        (column & 7) == lax.shift_right_logical(line, 4)
    )
    digits_ref[...] = dot(jnp.where(pick, 1.0, 0.0).astype(BF16), rows)


def across_lanes(digits_ref, at, count):
    found = []
    for part in range(count):
        high, low = digits_ref[pl.ds(at + part, 1), :], digits_ref[pl.ds(at + part + 32, 1), :]
        found.append((high * 64.0 + low).astype(I32) - 65)
    return found


def down_rows(digits_ref, at, count):
    same = iota((LANES, LANES), 0) == iota((LANES, LANES), 1)
    parts = []
    for part in range(count):
        high, low = digits_ref[pl.ds(at + part, 1), :], digits_ref[pl.ds(at + part + 32, 1), :]
        parts.append(
            jnp.concatenate([jnp.where(same, high, 0.0), jnp.where(same, low, 0.0)], axis=1)
        )
    left = jnp.concatenate(parts, axis=0).astype(BF16)
    right = jnp.where(iota((2 * LANES, LANES), 0) < LANES, 64.0, 1.0).astype(BF16)
    return dot(left, right).astype(I32) - 65


def low_table(labels):
    line = iota((LOW, LANES), 0)
    return jnp.concatenate(
        [jnp.where(line == (label & (LOW - 1)), 1.0, 0.0).astype(BF16) for label in labels], axis=1
    )


def masked(rows, high, which):
    return jnp.where(high == which, rows, 0.0).astype(BF16)


def counting(high):
    lane = iota(high.shape, 1)
    return jnp.where((high == (lane & 7)) & (lane < 16), 1.0, 0.0).astype(BF16)


def segments(total_ref, left_ref, high_ref, rows_of, digits_ref, steps):
    for step in range(steps):
        left_ref[:, lane_slice(step, 512)] = low_table(across_lanes(digits_ref, 4 * step, 4))
        high_ref[lane_slice(step, 512), :] = lax.shift_right_arithmetic(
            down_rows(digits_ref, 4 * step, 4), 9
        )
    left = left_ref[:, 0 : steps * 512]
    for pair in range(HIGHS // 2):
        right = []
        for step in range(steps):
            high, rows = high_ref[lane_slice(step, 512), :], rows_of(step)
            right.append(
                jnp.concatenate([masked(rows, high, 2 * pair + side) for side in range(2)], axis=1)
            )
        total_ref[:, lane_slice(pair, 2 * LANES)] = dot(left, jnp.concatenate(right, axis=0))
    total_ref[:, HIGHS * LANES :] = dot(left, counting(high_ref[0 : steps * 512, :]))


def add_segments(total_ref, digits_ref, at, rows):
    left = low_table(across_lanes(digits_ref, at, 2))
    high = lax.shift_right_arithmetic(down_rows(digits_ref, at, 2), 9)
    for pair in range(HIGHS // 2):
        right = jnp.concatenate([masked(rows, high, 2 * pair + side) for side in range(2)], axis=1)
        total_ref[:, lane_slice(pair, 2 * LANES)] += dot(left, right)
    total_ref[:, HIGHS * LANES :] += dot(left, counting(high))


def lower_rows(slab_ref, step):
    return slab_ref[lane_slice(step, 32), 0:HALF, :].reshape(512, LANES).astype(F32)


def upper_rows(slab_ref, group):
    return slab_ref[pl.ds(group * 16, 16), HALF:CAP, :].reshape(256, LANES).astype(F32)


def mark_live(digits_ref, live_ref):
    for group in range(live_ref.shape[0]):
        most = jnp.max(digits_ref[16 + 2 * group : 18 + 2 * group, :])
        live_ref[group] = jnp.where(most > 0.0, 1, 0)


def parent_kernel(parent_ref, old_ref, total_hbm, digits_ref, left_ref, high_ref, total_ref, sem):
    parent = parent_ref[...]
    digits_ref[0:32, :] = (lax.shift_right_logical(parent, 6) + 1).astype(F32)
    digits_ref[32:64, :] = ((parent & 63) + 1).astype(F32)
    segments(
        total_ref,
        left_ref,
        high_ref,
        lambda step: old_ref[lane_slice(step, 512), :].astype(F32),
        digits_ref,
        old_ref.shape[0] // 512,
    )
    store = pltpu.make_async_copy(total_ref, total_hbm, sem)
    store.start()
    store.wait()


def find_parents(digits_ref, parents_ref, table_ref, at, count):
    line = iota((LANES, LANES), 0)
    rows = [(digits_ref[pl.ds(at + n, 1), :], digits_ref[pl.ds(at + n + 32, 1), :]) for n in range(count)]
    left = [jnp.where(line == high.astype(I32) - 1, 1.0, 0.0).astype(BF16) for high, _ in rows]
    found = dot(table_ref[...], jnp.concatenate(left, axis=1))
    for n in range(count):
        chosen = jnp.where((line & 63) == rows[n][1].astype(I32) - 1, found[:, lane_slice(n)], 0.0)
        parents_ref[pl.ds(at + n, 1), :] = jnp.sum(chosen[0:64], axis=0, keepdims=True)
        parents_ref[pl.ds(at + n + 32, 1), :] = jnp.sum(chosen[64:128], axis=0, keepdims=True)


def upper_kernel(
    slab_ref, table_ref, top_ref, start_hbm, send_hbm, slab_hbm,
    digits_ref, parents_ref, total_ref, left_ref, high_ref, start_ref, send_ref, right_ref, tail_ref, live_ref,
    sems,
):
    load = pltpu.make_async_copy(start_hbm, start_ref, sems.at[0])
    load.start()
    keep = pltpu.make_async_copy(slab_ref, slab_hbm, sems.at[2 + HIGHS])
    keep.start()
    slot_digits(slab_ref, digits_ref)
    mark_live(digits_ref, live_ref)
    for step in range(4):
        find_parents(digits_ref, parents_ref, table_ref, 4 * step, 4)
    segments(total_ref, left_ref, high_ref, lambda step: lower_rows(slab_ref, step), parents_ref, 4)

    def more(group, carry):
        @pl.when(live_ref[group] > 0)
        def _():
            find_parents(digits_ref, parents_ref, table_ref, 16 + 2 * group, 2)
            add_segments(total_ref, parents_ref, 16 + 2 * group, upper_rows(slab_ref, group))

        return carry

    lax.fori_loop(0, slab_ref.shape[0] // 16, more, 0)
    load.wait()
    at = slice(HIGHS * LANES, (HIGHS + 1) * LANES)
    weights = total_ref[:, at] + start_ref[:, at]
    coarse = weights.astype(BF16).astype(F32)
    lane = iota((LOW, LANES), 1)
    split = jnp.where(lane < HIGHS, coarse, weights - coarse)
    diagonal = jnp.where(iota((16, LANES), 0) == iota((16, LANES), 1), 1.0, 0.0).astype(BF16)
    across = dot_nt(diagonal, split.astype(BF16))
    tops = []
    stores = [keep]
    for high in range(HIGHS):
        mass = (total_ref[:, lane_slice(high)] + start_ref[:, lane_slice(high)]).astype(BF16)
        for half in range(2):
            send_ref[2 * high + half, 0:32] = mass[half * 256 : (half + 1) * 256].reshape(32, 8, LANES)
        part = (pl.ds(2 * high, 2), pl.ds(0, 32))
        stores.append(pltpu.make_async_copy(send_ref.at[part], send_hbm.at[part], sems.at[1 + high]))
        stores[-1].start()
        right_ref[lane_slice(high, LOW), 0:LANES] = mass
        right_ref[lane_slice(high, LOW), LANES:] = jnp.where((lane & 7) == high, split, 0.0).astype(BF16)
        for part in range(4):
            hit = iota((256, LANES), 0) == top_ref[high * 4 + part : high * 4 + part + 1, :]
            tops.append(jnp.where(hit, 1.0, 0.0).astype(BF16))
    for half in range(2):
        for kind in range(2):
            lines = slice(kind * HIGHS, (kind + 1) * HIGHS)
            for side in range(2):
                tail_ref[pl.ds(side, HIGHS, 2), 2 * kind + half, :] = across[lines, lane_slice(2 * side + half)]
    tops = dot(jnp.concatenate(tops, axis=1), right_ref[...])
    owners = send_ref.shape[0]
    send_ref[:, 32:34] = tops[:, :LANES].astype(BF16).reshape(owners, 2, 8, LANES)
    first = jnp.where(iota((8, LANES), 1) < 16, 1.0, 0.0).astype(BF16)
    heavy = tops[:, LANES:]
    heavy_coarse = heavy.astype(BF16)
    heavy_fine = (heavy - heavy_coarse.astype(F32)).astype(BF16)
    top_weight = (dot_nt(first, heavy_coarse) + dot_nt(first, heavy_fine))[0:1]
    top_coarse = top_weight.astype(BF16).astype(F32)
    for kind, value in enumerate((top_coarse, top_weight - top_coarse)):
        for half in range(2):
            tail_ref[:, 4 + 2 * kind + half, :] = jnp.broadcast_to(value[:, lane_slice(half)], (owners, LANES))
    send_ref[:, 34:35] = tail_ref[...].astype(BF16)[:, None]
    part = (slice(None), pl.ds(32, 3))
    stores.append(pltpu.make_async_copy(send_ref.at[part], send_hbm.at[part], sems.at[1 + HIGHS]))
    stores[-1].start()
    for store in stores:
        store.wait()


def level_kernel(
    slab_hbm, old_hbm, level_hbm, residual_hbm,
    slab_ref, digits_ref, total_ref, table_ref, left_ref, high_ref, old_ref, level_ref, residual_ref, live_ref,
    load_sem, slab_sem, level_sems, low_sems, up_sems,
):
    fetch = pltpu.make_async_copy(slab_hbm, slab_ref, slab_sem)
    fetch.start()
    load = pltpu.make_async_copy(old_hbm, old_ref, load_sem)
    load.start()
    fetch.wait()
    slot_digits(slab_ref, digits_ref)
    mark_live(digits_ref, live_ref)
    segments(total_ref, left_ref, high_ref, lambda step: lower_rows(slab_ref, step), digits_ref, 4)
    groups = slab_ref.shape[0] // 16

    def more(group, carry):
        @pl.when(live_ref[group] > 0)
        def _():
            add_segments(total_ref, digits_ref, 16 + 2 * group, upper_rows(slab_ref, group))

        return carry

    lax.fori_loop(0, groups, more, 0)
    load.wait()
    inverse = 1.0 / (total_ref[:, HIGHS * LANES :] + 1.0)
    stores = []
    for high in range(HIGHS):
        lines = lane_slice(high, LOW)
        mass = total_ref[:, lane_slice(high)] + old_ref[lines, :].astype(F32)
        level = mass * jnp.broadcast_to(inverse[:, high : high + 1], mass.shape)
        level_ref[lines, :] = level
        table_ref[:, lane_slice(high)] = level.astype(BF16)
        stores.append(
            pltpu.make_async_copy(level_ref.at[lines], level_hbm.at[lines], level_sems.at[high])
        )
        stores[-1].start()

    def subtract(at, count, rows):
        label = down_rows(digits_ref, at, count)
        low = label & (LOW - 1)
        high = lax.shift_right_arithmetic(label, 9)
        lane = iota(label.shape, 1)
        left = jnp.concatenate(
            [
                jnp.where(low == lane + part * LANES, 1.0, 0.0).astype(BF16)
                for part in range(LOW // LANES)
            ],
            axis=1,
        )
        for pair in range(HIGHS // 2):
            found = dot(left, table_ref[:, lane_slice(pair, 2 * LANES)])
            for side in range(2):
                rows -= jnp.where(high == 2 * pair + side, found[:, lane_slice(side)], 0.0)
        return rows.astype(BF16)

    for step in range(4):
        sources = lane_slice(step, 32)
        residual_ref[sources, 0 : HALF // 8] = subtract(
            4 * step, 4, lower_rows(slab_ref, step)
        ).reshape(32, HALF // 8, 8, LANES)
        part = (sources, slice(0, HALF // 8))
        stores.append(
            pltpu.make_async_copy(residual_ref.at[part], residual_hbm.at[part], low_sems.at[step])
        )
        stores[-1].start()

    def upper_copy(group):
        part = (pl.ds(group * 16, 16), pl.ds(HALF // 8, HALF // 8))
        return pltpu.make_async_copy(residual_ref.at[part], residual_hbm.at[part], up_sems.at[group])

    def finish(group, carry):
        sources = pl.ds(group * 16, 16)
        @pl.when(live_ref[group] > 0)
        def _():
            residual_ref[sources, HALF // 8 : CAP // 8] = subtract(
                16 + 2 * group, 2, upper_rows(slab_ref, group)
            ).reshape(16, HALF // 8, 8, LANES)

        @pl.when(live_ref[group] == 0)
        def _():
            empty = slab_ref[sources, HALF:CAP, :]
            residual_ref[sources, HALF // 8 : CAP // 8] = empty.reshape(16, HALF // 8, 8, LANES)

        upper_copy(group).start()
        return carry

    lax.fori_loop(0, groups, finish, 0)
    for store in stores:
        store.wait()

    def settle(group, carry):
        upper_copy(group).wait()
        return carry

    lax.fori_loop(0, groups, settle, 0)


def finish_kernel(parts_ref, send_in, level_ref, send_hbm, column_ref, top_ref, sem):
    total = parts_ref[0].astype(F32)
    for source in range(1, parts_ref.shape[0]):
        total += parts_ref[source].astype(F32)
    tail = total[272:280].T
    me = lax.axis_index("cent")
    owners = parts_ref.shape[0]
    chosen = jnp.where(me < 8, tail[:, 4:5] + tail[:, 6:7], tail[:, 5:6] + tail[:, 7:8])
    column_ref[...] = jnp.broadcast_to(chosen, (LANES, LANES))
    weight = column_ref[pl.ds(pl.multiple_of((me % 8) * TOP, TOP), TOP), :]
    top = (total[256:272] / weight).astype(BF16)
    for group in range(top_ref.shape[0] // owners):
        first = group % 2 * (TOP // 2)
        part = jnp.broadcast_to(top[first : first + TOP // 2][None, None], (owners, 1, TOP // 2, LANES))
        top_ref[group * owners : (group + 1) * owners] = part
    store = pltpu.make_async_copy(top_ref, send_hbm.at[:, pl.ds(CAP // 8, 1)], sem)
    store.start()
    for half in range(2):
        weight = tail[:, half : half + 1] + tail[:, half + 2 : half + 3]
        lines = slice(half * LANES, (half + 1) * LANES)
        level_ref[lines, :] = total[lines] / jnp.broadcast_to(weight, (LANES, LANES))
    store.wait()


def unpack_kernel(back_ref, returned_ref, residual_hbm, level_hbm, residual_ref, level_ref, sems):
    groups, owners, rows, lanes = returned_ref.shape
    core = lax.axis_index("dp") % 2
    stores = []
    for pair in range(groups // 2):
        for side in range(2):
            top = returned_ref[2 * pair + side, :, CAP:rows, :].astype(F32)
            level_ref[:, 0, :, lane_slice(2 * pair + side)] = top
        right = jnp.concatenate(
            [
                returned_ref[2 * pair + side, :, 0:CAP, :].reshape(owners * CAP, lanes)
                for side in range(2)
            ],
            axis=1,
        )
        at = lane_slice(pair, 2 * lanes)
        residual_ref[:, at] = dot(back_ref[...], right).astype(BF16)
        stores.append(pltpu.make_async_copy(residual_ref.at[:, at], residual_hbm.at[:, at], sems.at[pair]))
        stores[-1].start()
    stores.append(pltpu.make_async_copy(level_ref, level_hbm.at[:, pl.ds(core, 1)], sems.at[groups // 2]))
    stores[-1].start()
    for store in stores:
        store.wait()


def other_kernel(parts_ref, level_in, level_hbm, level_ref, sem):
    core = lax.axis_index("dp") % 2
    for group in range(parts_ref.shape[0]):
        level_ref[:, 0, :, lane_slice(group)] = parts_ref[group].astype(F32)
    store = pltpu.make_async_copy(level_ref, level_hbm.at[:, pl.ds(1 - core, 1)], sem)
    store.start()
    store.wait()


def shape(dims, kind):
    return jax.ShapeDtypeStruct(dims, kind)


def in_hbm(value):
    return pltpu.with_memory_space_constraint(value, pltpu.HBM)


def swap(value, axes):
    return lax.all_to_all(value, axes, split_axis=0, concat_axis=0, tiled=True)


def on_device(points, assign, parent_one, parent_two, old_level_one):
    count, width = points.shape
    owners = lax.axis_size("cent")
    groups = lax.axis_size("dp")
    devices = owners * groups
    block, lanes = old_level_one.shape
    slots = owners * CAP
    rows = CAP + EXTRA
    total_dims = (LOW, (HIGHS + 1) * LANES)
    answer_dims = (devices, (CAP + TOP // 2) // 8, 8, lanes)
    work = 2 * LOW * block * (HIGHS + 1) * LANES

    send, back = call(
        pack_kernel,
        (shape((groups, owners, rows, lanes), BF16), shape((count, slots), BF16)),
        [HBM, HBM],
        (HBM, HBM),
        FULL,
        [
            pltpu.VMEM((1, count), I32),
            pltpu.VMEM((count, width), BF16),
            pltpu.VMEM((groups, owners, rows, lanes), BF16),
            pltpu.VMEM((count, slots), BF16),
            pltpu.SemaphoreType.DMA((2 + groups // 2 + groups,)),
        ],
        flops=2 * slots * count * width,
    )(assign.reshape(1, count), points)
    slab = swap(send.reshape(devices, rows, lanes), BOTH)

    start = call(
        parent_kernel,
        pltpu.HBM(total_dims, F32),
        [VMEM, VMEM],
        HBM,
        FULL,
        [
            pltpu.VMEM((64, LANES), F32),
            pltpu.VMEM((LOW, block), BF16),
            pltpu.VMEM((block, LANES), I32),
            pltpu.VMEM(total_dims, F32),
            pltpu.SemaphoreType.DMA(()),
        ],
        flops=work,
    )(parent_one.reshape(block // LANES, LANES), old_level_one)
    grid = parent_one.reshape(64, 64).T
    table = jnp.concatenate([lax.shift_right_logical(grid, 6), grid & 63], axis=0) + 1
    table = jnp.pad(table, ((0, 0), (0, 64))).astype(BF16)

    share, slab_kept = call(
        upper_kernel,
        (pltpu.HBM((owners, 35, 8, lanes), BF16), pltpu.HBM((devices, rows, lanes), BF16)),
        [VMEM, VMEM, VMEM, HBM],
        (HBM, HBM),
        UPPER,
        [
            pltpu.VMEM((64, LANES), F32),
            pltpu.VMEM((64, LANES), F32),
            pltpu.VMEM(total_dims, F32),
            pltpu.VMEM((LOW, 2048), BF16),
            pltpu.VMEM((2048, LANES), I32),
            pltpu.VMEM(total_dims, F32),
            pltpu.VMEM((owners, 35, 8, lanes), BF16),
            pltpu.VMEM((HIGHS * LOW, 2 * LANES), BF16),
            pltpu.VMEM((owners, 8, lanes), F32),
            pltpu.SMEM((groups,), I32),
            pltpu.SemaphoreType.DMA((3 + HIGHS,)),
        ],
        flops=work,
    )(slab, table, parent_two.reshape(-1, LANES), in_hbm(start))
    shares = swap(share, "cent")

    level_one, answer = call(
        level_kernel,
        (shape((block, lanes), F32), shape(answer_dims, BF16)),
        [HBM, HBM],
        (HBM, HBM),
        LEVEL,
        [
            pltpu.VMEM((devices, rows, lanes), BF16),
            pltpu.VMEM((64, LANES), F32),
            pltpu.VMEM(total_dims, F32),
            pltpu.VMEM((LOW, HIGHS * LANES), BF16),
            pltpu.VMEM((LOW, 2048), BF16),
            pltpu.VMEM((2048, LANES), I32),
            pltpu.VMEM((block, lanes), BF16),
            pltpu.VMEM((block, lanes), F32),
            pltpu.VMEM((devices, CAP // 8, 8, lanes), BF16),
            pltpu.SMEM((groups,), I32),
            pltpu.SemaphoreType.DMA(()),
            pltpu.SemaphoreType.DMA(()),
            pltpu.SemaphoreType.DMA((HIGHS,)),
            pltpu.SemaphoreType.DMA((4,)),
            pltpu.SemaphoreType.DMA((groups,)),
        ],
        flops=2 * work,
    )(in_hbm(slab_kept), in_hbm(old_level_one))

    level_two, answer = call(
        finish_kernel,
        (shape((256, lanes), F32), shape(answer_dims, BF16)),
        [VMEM, HBM],
        (VMEM, HBM),
        SMALL,
        [
            pltpu.VMEM((LANES, LANES), F32),
            pltpu.VMEM((devices, 1, TOP // 2, lanes), BF16),
            pltpu.SemaphoreType.DMA(()),
        ],
        alias={1: 1},
    )(shares.reshape(owners, -1, lanes), answer)
    returned = swap(answer, BOTH)
    half = returned[:, CAP // 8]
    half = lax.ppermute(half, "dp", [(group, group ^ 1) for group in range(groups)])
    top_dims = (owners, 2, TOP // 2, width)
    residual, level_three = call(
        unpack_kernel,
        (shape((count, width), BF16), shape(top_dims, F32)),
        [VMEM, VMEM],
        (HBM, HBM),
        SMALL,
        [
            pltpu.VMEM((count, width), BF16),
            pltpu.VMEM((owners, 1, TOP // 2, width), F32),
            pltpu.SemaphoreType.DMA((1 + groups // 2,)),
        ],
        flops=2 * slots * count * width,
    )(back, returned.reshape(groups, owners, CAP + TOP // 2, lanes))
    level_three = call(
        other_kernel,
        shape(top_dims, F32),
        [VMEM, HBM],
        HBM,
        SMALL,
        [pltpu.VMEM((owners, 1, TOP // 2, width), F32), pltpu.SemaphoreType.DMA(())],
        alias={1: 0},
    )(half.reshape(groups, owners, TOP // 2, lanes), level_three)
    level_three = level_three.reshape(owners * TOP, width)
    return (level_one, level_two, level_three, residual)


def solution(mesh):
    in_specs = (P(("dp", "cent"), None), P(("dp", "cent")), P("cent"), P(), P("cent", "dp"))
    out_specs = (P("cent", "dp"), P("cent", "dp"), P(), P(("dp", "cent"), None))
    return jax.shard_map(
        on_device, mesh=mesh, in_specs=in_specs, out_specs=out_specs, check_vma=False
    )
```

```python
import jax
import jax.numpy as jnp
from jax import lax
from jax.experimental import pallas as pl
from jax.experimental.pallas import tpu as pltpu
from jax.sharding import PartitionSpec as P

F32 = jnp.float32
BF16 = jnp.bfloat16
I32 = jnp.int32
LANES = 128
LOW = 512
HIGHS = 8
CAP = 32
HALF = 16
EXTRA = 8
TOP = 16
BOTH = ("dp", "cent")


def iota(shape, axis):
    return lax.broadcasted_iota(I32, shape, axis)


def dot(left, right):
    return jnp.dot(left, right, preferred_element_type=F32)


def dot_nt(left, right):
    return lax.dot_general(left, right, (((1,), (1,)), ((), ())), preferred_element_type=F32)


def lane_slice(at, width=LANES):
    return slice(at * width, (at + 1) * width)


HBM = pl.BlockSpec(memory_space=pltpu.HBM)
VMEM = pl.BlockSpec(memory_space=pltpu.VMEM)


FULL = 62_900_000
UPPER = 48_000_000
LEVEL = 48_000_000
SMALL = 16_000_000


def call(body, out_shape, ins, outs, vmem, scratch=(), flops=0, size=4 << 20, alias=None):
    return pl.pallas_call(
        body,
        out_shape=out_shape,
        in_specs=ins,
        out_specs=outs,
        scratch_shapes=list(scratch),
        input_output_aliases=alias or {},
        compiler_params=pltpu.CompilerParams(vmem_limit_bytes=vmem),
        cost_estimate=pl.CostEstimate(flops=flops, bytes_accessed=size, transcendentals=0),
    )


def owner_slots(label, owners):
    count = label.shape[1]
    owner = lax.shift_right_logical(label, 12)
    mine = jnp.where(iota((owners, count), 0) == owner, 1.0, 0.0)
    before = jnp.where(iota((count, count), 0) <= iota((count, count), 1), 1.0, 0.0).astype(BF16)
    place = jnp.sum(dot(mine.astype(BF16), before) * mine, axis=0, keepdims=True).astype(I32) - 1
    return mine, place, owner * CAP + place


def slot_table(slot, slots):
    return jnp.where(iota((slots, slot.shape[1]), 0) == slot, 1.0, 0.0).astype(BF16)


def pack_kernel(assign_hbm, points_hbm, send_hbm, assign_ref, points_ref, send_ref, sems):
    owners = send_ref.shape[1]
    parts = send_ref.shape[0]
    load = pltpu.make_async_copy(assign_hbm, assign_ref, sems.at[0])
    load.start()
    loads = []
    for pair in range(parts // 2):
        at = lane_slice(pair, 2 * LANES)
        loads.append(
            pltpu.make_async_copy(points_hbm.at[:, at], points_ref.at[:, at], sems.at[1 + pair])
        )
        loads[-1].start()
    load.wait()
    label = assign_ref[...]
    mine, place, slot = owner_slots(label, owners)
    local = label & 4095
    table = slot_table(slot, owners * CAP)
    shift = (lax.axis_index("cent") % 8) * HALF
    line = iota((LANES, points_ref.shape[0]), 0)
    row = iota((owners, EXTRA, LANES), 1)
    digits = [(lax.shift_right_logical(local, 6) + 1).astype(F32), ((local & 63) + 1).astype(F32)]
    digits = [(mine * digit).astype(BF16) for digit in digits]
    extra = jnp.zeros((owners, EXTRA, LANES), F32)
    for half in range(2):
        first = half * HALF
        inside = (place >= first) & (place < first + HALF)
        lane = jnp.where(inside, place - first + shift, -1)
        lane_table = jnp.where(line == lane, 1.0, 0.0).astype(BF16)
        for kind in range(2):
            found = dot_nt(digits[kind], lane_table)
            extra = jnp.where(row == 2 * kind + half, found[:, None, :], extra)
    extra = extra.astype(BF16)
    stores = []
    for part in range(parts):
        if part % 2 == 0:
            loads[part // 2].wait()
            both = dot(table, points_ref[:, lane_slice(part // 2, 2 * LANES)]).astype(BF16)
        rows = both[:, lane_slice(part % 2)]
        send_ref[part, :, 0:CAP, :] = rows.reshape(owners, CAP, LANES)
        send_ref[part, :, CAP : CAP + EXTRA, :] = extra
        stores.append(
            pltpu.make_async_copy(send_ref.at[part], send_hbm.at[part], sems.at[1 + parts // 2 + part])
        )
        stores[-1].start()
    for store in stores:
        store.wait()


def slot_digits(slab_ref, digits_ref):
    rows = slab_ref[:, CAP : CAP + EXTRA, :].astype(F32).reshape(-1, LANES).astype(BF16)
    shape = (64, rows.shape[0])
    column, line = iota(shape, 1), iota(shape, 0)
    pick = (lax.shift_right_logical(column, 6) == (line & 15)) & (
        (column & 7) == lax.shift_right_logical(line, 4)
    )
    digits_ref[...] = dot(jnp.where(pick, 1.0, 0.0).astype(BF16), rows)


def across_lanes(digits_ref, at, count):
    found = []
    for part in range(count):
        high, low = digits_ref[pl.ds(at + part, 1), :], digits_ref[pl.ds(at + part + 32, 1), :]
        found.append((high * 64.0 + low).astype(I32) - 65)
    return found


def down_rows(digits_ref, at, count):
    same = iota((LANES, LANES), 0) == iota((LANES, LANES), 1)
    parts = []
    for part in range(count):
        high, low = digits_ref[pl.ds(at + part, 1), :], digits_ref[pl.ds(at + part + 32, 1), :]
        parts.append(
            jnp.concatenate([jnp.where(same, high, 0.0), jnp.where(same, low, 0.0)], axis=1)
        )
    left = jnp.concatenate(parts, axis=0).astype(BF16)
    right = jnp.where(iota((2 * LANES, LANES), 0) < LANES, 64.0, 1.0).astype(BF16)
    return dot(left, right).astype(I32) - 65


def low_table(labels):
    line = iota((LOW, LANES), 0)
    return jnp.concatenate(
        [jnp.where(line == (label & (LOW - 1)), 1.0, 0.0).astype(BF16) for label in labels], axis=1
    )


def masked(rows, high, which):
    return jnp.where(high == which, rows, 0.0).astype(BF16)


def counting(high):
    lane = iota(high.shape, 1)
    return jnp.where((high == (lane & 7)) & (lane < 16), 1.0, 0.0).astype(BF16)


def segments(total_ref, left_ref, high_ref, rows_of, digits_ref, steps):
    for step in range(steps):
        left_ref[:, lane_slice(step, 512)] = low_table(across_lanes(digits_ref, 4 * step, 4))
        high_ref[lane_slice(step, 512), :] = lax.shift_right_arithmetic(
            down_rows(digits_ref, 4 * step, 4), 9
        )
    left = left_ref[:, 0 : steps * 512]
    for pair in range(HIGHS // 2):
        right = []
        for step in range(steps):
            high, rows = high_ref[lane_slice(step, 512), :], rows_of(step)
            right.append(
                jnp.concatenate([masked(rows, high, 2 * pair + side) for side in range(2)], axis=1)
            )
        total_ref[:, lane_slice(pair, 2 * LANES)] = dot(left, jnp.concatenate(right, axis=0))
    total_ref[:, HIGHS * LANES :] = dot(left, counting(high_ref[0 : steps * 512, :]))


def add_segments(total_ref, digits_ref, at, rows):
    left = low_table(across_lanes(digits_ref, at, 2))
    high = lax.shift_right_arithmetic(down_rows(digits_ref, at, 2), 9)
    for pair in range(HIGHS // 2):
        right = jnp.concatenate([masked(rows, high, 2 * pair + side) for side in range(2)], axis=1)
        total_ref[:, lane_slice(pair, 2 * LANES)] += dot(left, right)
    total_ref[:, HIGHS * LANES :] += dot(left, counting(high))


def lower_rows(slab_ref, step):
    return slab_ref[lane_slice(step, 32), 0:HALF, :].reshape(512, LANES).astype(F32)


def upper_rows(slab_ref, group):
    return slab_ref[pl.ds(group * 16, 16), HALF:CAP, :].reshape(256, LANES).astype(F32)


def mark_live(digits_ref, live_ref):
    for group in range(live_ref.shape[0]):
        most = jnp.max(digits_ref[16 + 2 * group : 18 + 2 * group, :])
        live_ref[group] = jnp.where(most > 0.0, 1, 0)


def parent_kernel(
    parent_ref, old_ref, assign_ref, total_hbm, back_ref, digits_ref, left_ref, high_ref, total_ref, sem
):
    count, slots = back_ref.shape
    unused, unused, slot = owner_slots(assign_ref[...], slots // CAP)
    same = jnp.where(iota((count, count), 0) == iota((count, count), 1), 1.0, 0.0).astype(BF16)
    back_ref[...] = dot_nt(same, slot_table(slot, slots)).astype(BF16)
    parent = parent_ref[...]
    digits_ref[0:32, :] = (lax.shift_right_logical(parent, 6) + 1).astype(F32)
    digits_ref[32:64, :] = ((parent & 63) + 1).astype(F32)
    segments(
        total_ref,
        left_ref,
        high_ref,
        lambda step: old_ref[lane_slice(step, 512), :].astype(F32),
        digits_ref,
        old_ref.shape[0] // 512,
    )
    store = pltpu.make_async_copy(total_ref, total_hbm, sem)
    store.start()
    store.wait()


def find_parents(digits_ref, parents_ref, table_ref, at, count):
    line = iota((LANES, LANES), 0)
    rows = [(digits_ref[pl.ds(at + n, 1), :], digits_ref[pl.ds(at + n + 32, 1), :]) for n in range(count)]
    left = [jnp.where(line == high.astype(I32) - 1, 1.0, 0.0).astype(BF16) for high, _ in rows]
    found = dot(table_ref[...], jnp.concatenate(left, axis=1))
    for n in range(count):
        chosen = jnp.where((line & 63) == rows[n][1].astype(I32) - 1, found[:, lane_slice(n)], 0.0)
        parents_ref[pl.ds(at + n, 1), :] = jnp.sum(chosen[0:64], axis=0, keepdims=True)
        parents_ref[pl.ds(at + n + 32, 1), :] = jnp.sum(chosen[64:128], axis=0, keepdims=True)


def upper_kernel(
    slab_ref, table_ref, top_ref, start_hbm, send_hbm, slab_hbm,
    digits_ref, parents_ref, total_ref, left_ref, high_ref, start_ref, send_ref, right_ref, hits_ref, tail_ref,
    live_ref, sems,
):
    load = pltpu.make_async_copy(start_hbm, start_ref, sems.at[0])
    load.start()
    keep = pltpu.make_async_copy(slab_ref, slab_hbm, sems.at[2 + HIGHS])
    keep.start()
    slot_digits(slab_ref, digits_ref)
    mark_live(digits_ref, live_ref)
    for part in range(HIGHS * 4):
        hit = iota((256, LANES), 0) == top_ref[part : part + 1, :]
        hits_ref[:, lane_slice(part)] = jnp.where(hit, 1.0, 0.0).astype(BF16)
    for step in range(4):
        find_parents(digits_ref, parents_ref, table_ref, 4 * step, 4)
    segments(total_ref, left_ref, high_ref, lambda step: lower_rows(slab_ref, step), parents_ref, 4)

    def more(group, carry):
        @pl.when(live_ref[group] > 0)
        def _():
            find_parents(digits_ref, parents_ref, table_ref, 16 + 2 * group, 2)
            add_segments(total_ref, parents_ref, 16 + 2 * group, upper_rows(slab_ref, group))

        return carry

    lax.fori_loop(0, slab_ref.shape[0] // 16, more, 0)
    load.wait()
    at = slice(HIGHS * LANES, (HIGHS + 1) * LANES)
    weights = total_ref[:, at] + start_ref[:, at]
    coarse = weights.astype(BF16).astype(F32)
    lane = iota((LOW, LANES), 1)
    split = jnp.where(lane < HIGHS, coarse, weights - coarse)
    diagonal = jnp.where(iota((16, LANES), 0) == iota((16, LANES), 1), 1.0, 0.0).astype(BF16)
    across = dot_nt(diagonal, split.astype(BF16))
    stores = [keep]
    for high in range(HIGHS):
        mass = (total_ref[:, lane_slice(high)] + start_ref[:, lane_slice(high)]).astype(BF16)
        for half in range(2):
            send_ref[2 * high + half, 0:32] = mass[half * 256 : (half + 1) * 256].reshape(32, 8, LANES)
        part = (pl.ds(2 * high, 2), pl.ds(0, 32))
        stores.append(pltpu.make_async_copy(send_ref.at[part], send_hbm.at[part], sems.at[1 + high]))
        stores[-1].start()
        right_ref[lane_slice(high, LOW), 0:LANES] = mass
        right_ref[lane_slice(high, LOW), LANES:] = jnp.where((lane & 7) == high, split, 0.0).astype(BF16)
    for half in range(2):
        for kind in range(2):
            lines = slice(kind * HIGHS, (kind + 1) * HIGHS)
            for side in range(2):
                tail_ref[pl.ds(side, HIGHS, 2), 2 * kind + half, :] = across[lines, lane_slice(2 * side + half)]
    tops = dot(hits_ref[...], right_ref[...])
    owners = send_ref.shape[0]
    send_ref[:, 32:34] = tops[:, :LANES].astype(BF16).reshape(owners, 2, 8, LANES)
    first = jnp.where(iota((8, LANES), 1) < 16, 1.0, 0.0).astype(BF16)
    heavy = tops[:, LANES:]
    heavy_coarse = heavy.astype(BF16)
    heavy_fine = (heavy - heavy_coarse.astype(F32)).astype(BF16)
    top_weight = (dot_nt(first, heavy_coarse) + dot_nt(first, heavy_fine))[0:1]
    top_coarse = top_weight.astype(BF16).astype(F32)
    for kind, value in enumerate((top_coarse, top_weight - top_coarse)):
        for half in range(2):
            tail_ref[:, 4 + 2 * kind + half, :] = jnp.broadcast_to(value[:, lane_slice(half)], (owners, LANES))
    send_ref[:, 34:35] = tail_ref[...].astype(BF16)[:, None]
    part = (slice(None), pl.ds(32, 3))
    stores.append(pltpu.make_async_copy(send_ref.at[part], send_hbm.at[part], sems.at[1 + HIGHS]))
    stores[-1].start()
    for store in stores:
        store.wait()


def level_kernel(
    slab_hbm, old_hbm, level_hbm, residual_hbm,
    slab_ref, digits_ref, total_ref, table_ref, left_ref, high_ref, old_ref, level_ref, residual_ref, live_ref,
    load_sem, slab_sem, level_sems, low_sems, up_sems,
):
    fetch = pltpu.make_async_copy(slab_hbm, slab_ref, slab_sem)
    fetch.start()
    load = pltpu.make_async_copy(old_hbm, old_ref, load_sem)
    load.start()
    fetch.wait()
    slot_digits(slab_ref, digits_ref)
    mark_live(digits_ref, live_ref)
    segments(total_ref, left_ref, high_ref, lambda step: lower_rows(slab_ref, step), digits_ref, 4)
    groups = slab_ref.shape[0] // 16

    def more(group, carry):
        @pl.when(live_ref[group] > 0)
        def _():
            add_segments(total_ref, digits_ref, 16 + 2 * group, upper_rows(slab_ref, group))

        return carry

    lax.fori_loop(0, groups, more, 0)
    load.wait()
    inverse = 1.0 / (total_ref[:, HIGHS * LANES :] + 1.0)
    stores = []
    for high in range(HIGHS):
        lines = lane_slice(high, LOW)
        mass = total_ref[:, lane_slice(high)] + old_ref[lines, :].astype(F32)
        level = mass * jnp.broadcast_to(inverse[:, high : high + 1], mass.shape)
        level_ref[lines, :] = level
        table_ref[:, lane_slice(high)] = level.astype(BF16)
        stores.append(
            pltpu.make_async_copy(level_ref.at[lines], level_hbm.at[lines], level_sems.at[high])
        )
        stores[-1].start()

    def subtract(at, count, rows):
        label = down_rows(digits_ref, at, count)
        low = label & (LOW - 1)
        high = lax.shift_right_arithmetic(label, 9)
        lane = iota(label.shape, 1)
        left = jnp.concatenate(
            [
                jnp.where(low == lane + part * LANES, 1.0, 0.0).astype(BF16)
                for part in range(LOW // LANES)
            ],
            axis=1,
        )
        for pair in range(HIGHS // 2):
            found = dot(left, table_ref[:, lane_slice(pair, 2 * LANES)])
            for side in range(2):
                rows -= jnp.where(high == 2 * pair + side, found[:, lane_slice(side)], 0.0)
        return rows.astype(BF16)

    for step in range(4):
        sources = lane_slice(step, 32)
        residual_ref[sources, 0 : HALF // 8] = subtract(
            4 * step, 4, lower_rows(slab_ref, step)
        ).reshape(32, HALF // 8, 8, LANES)
        part = (sources, slice(0, HALF // 8))
        stores.append(
            pltpu.make_async_copy(residual_ref.at[part], residual_hbm.at[part], low_sems.at[step])
        )
        stores[-1].start()

    def upper_copy(group):
        part = (pl.ds(group * 16, 16), pl.ds(HALF // 8, HALF // 8))
        return pltpu.make_async_copy(residual_ref.at[part], residual_hbm.at[part], up_sems.at[group])

    def finish(group, carry):
        sources = pl.ds(group * 16, 16)
        @pl.when(live_ref[group] > 0)
        def _():
            residual_ref[sources, HALF // 8 : CAP // 8] = subtract(
                16 + 2 * group, 2, upper_rows(slab_ref, group)
            ).reshape(16, HALF // 8, 8, LANES)

        @pl.when(live_ref[group] == 0)
        def _():
            empty = slab_ref[sources, HALF:CAP, :]
            residual_ref[sources, HALF // 8 : CAP // 8] = empty.reshape(16, HALF // 8, 8, LANES)

        upper_copy(group).start()
        return carry

    lax.fori_loop(0, groups, finish, 0)
    for store in stores:
        store.wait()

    def settle(group, carry):
        upper_copy(group).wait()
        return carry

    lax.fori_loop(0, groups, settle, 0)


def add_parts(parts_ref, lines):
    total = parts_ref[0, lines].astype(F32)
    for source in range(1, parts_ref.shape[0]):
        total += parts_ref[source, lines].astype(F32)
    return total


def middle_kernel(parts_ref, level_ref):
    tail = add_parts(parts_ref, slice(272, 280)).T
    for half in range(2):
        weight = tail[:, half : half + 1] + tail[:, half + 2 : half + 3]
        lines = slice(half * LANES, (half + 1) * LANES)
        level_ref[lines, :] = add_parts(parts_ref, lines) / jnp.broadcast_to(weight, (LANES, LANES))


def top_kernel(parts_ref, send_in, send_hbm, column_ref, top_ref, sem):
    owners = parts_ref.shape[0]
    total = add_parts(parts_ref, slice(256, 280))
    tail = total[16:24].T
    me = lax.axis_index("cent")
    chosen = jnp.where(me < 8, tail[:, 4:5] + tail[:, 6:7], tail[:, 5:6] + tail[:, 7:8])
    column_ref[...] = jnp.broadcast_to(chosen, (LANES, LANES))
    weight = column_ref[pl.ds(pl.multiple_of((me % 8) * TOP, TOP), TOP), :]
    top = (total[0:TOP] / weight).astype(BF16)
    for group in range(top_ref.shape[0] // owners):
        first = group % 2 * (TOP // 2)
        part = jnp.broadcast_to(top[first : first + TOP // 2][None, None], (owners, 1, TOP // 2, LANES))
        top_ref[group * owners : (group + 1) * owners] = part
    store = pltpu.make_async_copy(top_ref, send_hbm.at[:, pl.ds(CAP // 8, 1)], sem)
    store.start()
    store.wait()


def unpack_kernel(back_ref, returned_ref, residual_hbm, level_hbm, residual_ref, level_ref, sems):
    groups, owners, rows, lanes = returned_ref.shape
    core = lax.axis_index("dp") % 2
    stores = []
    for pair in range(groups // 2):
        for side in range(2):
            top = returned_ref[2 * pair + side, :, CAP:rows, :].astype(F32)
            level_ref[:, 0, :, lane_slice(2 * pair + side)] = top
        right = jnp.concatenate(
            [
                returned_ref[2 * pair + side, :, 0:CAP, :].reshape(owners * CAP, lanes)
                for side in range(2)
            ],
            axis=1,
        )
        at = lane_slice(pair, 2 * lanes)
        residual_ref[:, at] = dot(back_ref[...], right).astype(BF16)
        stores.append(pltpu.make_async_copy(residual_ref.at[:, at], residual_hbm.at[:, at], sems.at[pair]))
        stores[-1].start()
    stores.append(pltpu.make_async_copy(level_ref, level_hbm.at[:, pl.ds(core, 1)], sems.at[groups // 2]))
    stores[-1].start()
    for store in stores:
        store.wait()


def other_kernel(parts_ref, level_in, level_hbm, level_ref, sem):
    core = lax.axis_index("dp") % 2
    for group in range(parts_ref.shape[0]):
        level_ref[:, 0, :, lane_slice(group)] = parts_ref[group].astype(F32)
    store = pltpu.make_async_copy(level_ref, level_hbm.at[:, pl.ds(1 - core, 1)], sem)
    store.start()
    store.wait()


def shape(dims, kind):
    return jax.ShapeDtypeStruct(dims, kind)


def in_hbm(value):
    return pltpu.with_memory_space_constraint(value, pltpu.HBM)


def swap(value, axes):
    return lax.all_to_all(value, axes, split_axis=0, concat_axis=0, tiled=True)


def on_device(points, assign, parent_one, parent_two, old_level_one):
    count, width = points.shape
    owners = lax.axis_size("cent")
    groups = lax.axis_size("dp")
    devices = owners * groups
    block, lanes = old_level_one.shape
    slots = owners * CAP
    rows = CAP + EXTRA
    total_dims = (LOW, (HIGHS + 1) * LANES)
    answer_dims = (devices, (CAP + TOP // 2) // 8, 8, lanes)
    work = 2 * LOW * block * (HIGHS + 1) * LANES

    labels = assign.reshape(1, count)
    send = call(
        pack_kernel,
        pltpu.HBM((groups, owners, rows, lanes), BF16),
        [HBM, HBM],
        HBM,
        FULL,
        [
            pltpu.VMEM((1, count), I32),
            pltpu.VMEM((count, width), BF16),
            pltpu.VMEM((groups, owners, rows, lanes), BF16),
            pltpu.SemaphoreType.DMA((1 + groups // 2 + groups,)),
        ],
        flops=2 * slots * count * width,
    )(labels, points)
    slab = swap(send.reshape(devices, rows, lanes), BOTH)

    start, back = call(
        parent_kernel,
        (pltpu.HBM(total_dims, F32), shape((count, slots), BF16)),
        [VMEM, VMEM, VMEM],
        (HBM, VMEM),
        FULL,
        [
            pltpu.VMEM((64, LANES), F32),
            pltpu.VMEM((LOW, block), BF16),
            pltpu.VMEM((block, LANES), I32),
            pltpu.VMEM(total_dims, F32),
            pltpu.SemaphoreType.DMA(()),
        ],
        flops=work,
    )(parent_one.reshape(block // LANES, LANES), old_level_one, labels)
    grid = parent_one.reshape(64, 64).T
    table = jnp.concatenate([lax.shift_right_logical(grid, 6), grid & 63], axis=0) + 1
    table = jnp.pad(table, ((0, 0), (0, 64))).astype(BF16)

    share, slab_kept = call(
        upper_kernel,
        (pltpu.HBM((owners, 35, 8, lanes), BF16), pltpu.HBM((devices, rows, lanes), BF16)),
        [VMEM, VMEM, VMEM, HBM],
        (HBM, HBM),
        UPPER,
        [
            pltpu.VMEM((64, LANES), F32),
            pltpu.VMEM((64, LANES), F32),
            pltpu.VMEM(total_dims, F32),
            pltpu.VMEM((LOW, 2048), BF16),
            pltpu.VMEM((2048, LANES), I32),
            pltpu.VMEM(total_dims, F32),
            pltpu.VMEM((owners, 35, 8, lanes), BF16),
            pltpu.VMEM((HIGHS * LOW, 2 * LANES), BF16),
            pltpu.VMEM((256, HIGHS * LOW), BF16),
            pltpu.VMEM((owners, 8, lanes), F32),
            pltpu.SMEM((groups,), I32),
            pltpu.SemaphoreType.DMA((3 + HIGHS,)),
        ],
        flops=work,
    )(slab, table, parent_two.reshape(-1, LANES), in_hbm(start))
    shares = swap(share, "cent")

    level_one, answer = call(
        level_kernel,
        (shape((block, lanes), F32), shape(answer_dims, BF16)),
        [HBM, HBM],
        (HBM, HBM),
        LEVEL,
        [
            pltpu.VMEM((devices, rows, lanes), BF16),
            pltpu.VMEM((64, LANES), F32),
            pltpu.VMEM(total_dims, F32),
            pltpu.VMEM((LOW, HIGHS * LANES), BF16),
            pltpu.VMEM((LOW, 2048), BF16),
            pltpu.VMEM((2048, LANES), I32),
            pltpu.VMEM((block, lanes), BF16),
            pltpu.VMEM((block, lanes), F32),
            pltpu.VMEM((devices, CAP // 8, 8, lanes), BF16),
            pltpu.SMEM((groups,), I32),
            pltpu.SemaphoreType.DMA(()),
            pltpu.SemaphoreType.DMA(()),
            pltpu.SemaphoreType.DMA((HIGHS,)),
            pltpu.SemaphoreType.DMA((4,)),
            pltpu.SemaphoreType.DMA((groups,)),
        ],
        flops=2 * work,
    )(in_hbm(slab_kept), in_hbm(old_level_one))

    shares = shares.reshape(owners, -1, lanes)
    answer = call(
        top_kernel,
        shape(answer_dims, BF16),
        [VMEM, HBM],
        HBM,
        SMALL,
        [
            pltpu.VMEM((LANES, LANES), F32),
            pltpu.VMEM((devices, 1, TOP // 2, lanes), BF16),
            pltpu.SemaphoreType.DMA(()),
        ],
        alias={1: 0},
    )(shares, answer)
    level_two = call(middle_kernel, shape((256, lanes), F32), [VMEM], VMEM, SMALL, flops=work)(shares)
    returned = swap(answer, BOTH)
    returned, level_two = lax.optimization_barrier((returned, level_two))
    half = returned[:, CAP // 8]
    half = lax.ppermute(half, "dp", [(group, group ^ 1) for group in range(groups)])
    top_dims = (owners, 2, TOP // 2, width)
    residual, level_three = call(
        unpack_kernel,
        (shape((count, width), BF16), shape(top_dims, F32)),
        [VMEM, VMEM],
        (HBM, HBM),
        SMALL,
        [
            pltpu.VMEM((count, width), BF16),
            pltpu.VMEM((owners, 1, TOP // 2, width), F32),
            pltpu.SemaphoreType.DMA((1 + groups // 2,)),
        ],
        flops=2 * slots * count * width,
    )(back, returned.reshape(groups, owners, CAP + TOP // 2, lanes))
    level_three = call(
        other_kernel,
        shape(top_dims, F32),
        [VMEM, HBM],
        HBM,
        SMALL,
        [pltpu.VMEM((owners, 1, TOP // 2, width), F32), pltpu.SemaphoreType.DMA(())],
        alias={1: 0},
    )(half.reshape(groups, owners, TOP // 2, lanes), level_three)
    level_three = level_three.reshape(owners * TOP, width)
    return (level_one, level_two, level_three, residual)


def solution(mesh):
    in_specs = (P(("dp", "cent"), None), P(("dp", "cent")), P("cent"), P(), P("cent", "dp"))
    out_specs = (P("cent", "dp"), P("cent", "dp"), P(), P(("dp", "cent"), None))
    return jax.shard_map(
        on_device, mesh=mesh, in_specs=in_specs, out_specs=out_specs, check_vma=False
    )
```

```python
import jax
import jax.numpy as jnp
from jax import lax
from jax.experimental import pallas as pl
from jax.experimental.pallas import tpu as pltpu
from jax.sharding import PartitionSpec as P

F32 = jnp.float32
BF16 = jnp.bfloat16
I32 = jnp.int32
LANES = 128
LOW = 512
HIGHS = 8
CAP = 32
HALF = 16
EXTRA = 8
TOP = 16
BOTH = ("dp", "cent")


def iota(shape, axis):
    return lax.broadcasted_iota(I32, shape, axis)


def dot(left, right):
    return jnp.dot(left, right, preferred_element_type=F32)


def dot_nt(left, right):
    return lax.dot_general(left, right, (((1,), (1,)), ((), ())), preferred_element_type=F32)


def lane_slice(at, width=LANES):
    return slice(at * width, (at + 1) * width)


HBM = pl.BlockSpec(memory_space=pltpu.HBM)
VMEM = pl.BlockSpec(memory_space=pltpu.VMEM)


FULL = 62_900_000
UPPER = 48_000_000
LEVEL = 48_000_000
SMALL = 16_000_000


def call(body, out_shape, ins, outs, vmem, scratch=(), flops=0, size=4 << 20, alias=None):
    return pl.pallas_call(
        body,
        out_shape=out_shape,
        in_specs=ins,
        out_specs=outs,
        scratch_shapes=list(scratch),
        input_output_aliases=alias or {},
        compiler_params=pltpu.CompilerParams(vmem_limit_bytes=vmem),
        cost_estimate=pl.CostEstimate(flops=flops, bytes_accessed=size, transcendentals=0),
    )


def owner_slots(label, owners):
    count = label.shape[1]
    owner = lax.shift_right_logical(label, 12)
    mine = jnp.where(iota((owners, count), 0) == owner, 1.0, 0.0)
    before = jnp.where(iota((count, count), 0) <= iota((count, count), 1), 1.0, 0.0).astype(BF16)
    place = jnp.sum(dot(mine.astype(BF16), before) * mine, axis=0, keepdims=True).astype(I32) - 1
    return mine, place, owner * CAP + place


def slot_table(slot, slots):
    return jnp.where(iota((slots, slot.shape[1]), 0) == slot, 1.0, 0.0).astype(BF16)


def pack_kernel(assign_hbm, points_hbm, send_hbm, assign_ref, points_ref, send_ref, sems):
    owners = send_ref.shape[1]
    parts = send_ref.shape[0]
    load = pltpu.make_async_copy(assign_hbm, assign_ref, sems.at[0])
    load.start()
    loads = []
    for pair in range(parts // 2):
        at = lane_slice(pair, 2 * LANES)
        loads.append(
            pltpu.make_async_copy(points_hbm.at[:, at], points_ref.at[:, at], sems.at[1 + pair])
        )
        loads[-1].start()
    load.wait()
    label = assign_ref[...]
    mine, place, slot = owner_slots(label, owners)
    local = label & 4095
    table = slot_table(slot, owners * CAP)
    shift = (lax.axis_index("cent") % 8) * HALF
    line = iota((LANES, points_ref.shape[0]), 0)
    row = iota((owners, EXTRA, LANES), 1)
    digits = [(lax.shift_right_logical(local, 6) + 1).astype(F32), ((local & 63) + 1).astype(F32)]
    digits = [(mine * digit).astype(BF16) for digit in digits]
    extra = jnp.zeros((owners, EXTRA, LANES), F32)
    for half in range(2):
        first = half * HALF
        inside = (place >= first) & (place < first + HALF)
        lane = jnp.where(inside, place - first + shift, -1)
        lane_table = jnp.where(line == lane, 1.0, 0.0).astype(BF16)
        for kind in range(2):
            found = dot_nt(digits[kind], lane_table)
            extra = jnp.where(row == 2 * kind + half, found[:, None, :], extra)
    extra = extra.astype(BF16)
    stores = []
    for part in range(parts):
        if part % 2 == 0:
            loads[part // 2].wait()
            both = dot(table, points_ref[:, lane_slice(part // 2, 2 * LANES)]).astype(BF16)
        rows = both[:, lane_slice(part % 2)]
        send_ref[part, :, 0:CAP, :] = rows.reshape(owners, CAP, LANES)
        send_ref[part, :, CAP : CAP + EXTRA, :] = extra
        stores.append(
            pltpu.make_async_copy(send_ref.at[part], send_hbm.at[part], sems.at[1 + parts // 2 + part])
        )
        stores[-1].start()
    for store in stores:
        store.wait()


def slot_digits(slab_ref, digits_ref):
    rows = slab_ref[:, CAP : CAP + EXTRA, :].astype(F32).reshape(-1, LANES).astype(BF16)
    shape = (64, rows.shape[0])
    column, line = iota(shape, 1), iota(shape, 0)
    pick = (lax.shift_right_logical(column, 6) == (line & 15)) & (
        (column & 7) == lax.shift_right_logical(line, 4)
    )
    digits_ref[...] = dot(jnp.where(pick, 1.0, 0.0).astype(BF16), rows)


def across_lanes(digits_ref, at, count):
    found = []
    for part in range(count):
        high, low = digits_ref[pl.ds(at + part, 1), :], digits_ref[pl.ds(at + part + 32, 1), :]
        found.append((high * 64.0 + low).astype(I32) - 65)
    return found


def down_rows(digits_ref, at, count):
    same = iota((LANES, LANES), 0) == iota((LANES, LANES), 1)
    parts = []
    for part in range(count):
        high, low = digits_ref[pl.ds(at + part, 1), :], digits_ref[pl.ds(at + part + 32, 1), :]
        parts.append(
            jnp.concatenate([jnp.where(same, high, 0.0), jnp.where(same, low, 0.0)], axis=1)
        )
    left = jnp.concatenate(parts, axis=0).astype(BF16)
    right = jnp.where(iota((2 * LANES, LANES), 0) < LANES, 64.0, 1.0).astype(BF16)
    return dot(left, right).astype(I32) - 65


def low_table(labels):
    line = iota((LOW, LANES), 0)
    return jnp.concatenate(
        [jnp.where(line == (label & (LOW - 1)), 1.0, 0.0).astype(BF16) for label in labels], axis=1
    )


def masked(rows, high, which):
    return jnp.where(high == which, rows, 0.0).astype(BF16)


def counting(high):
    lane = iota(high.shape, 1)
    return jnp.where((high == (lane & 7)) & (lane < 16), 1.0, 0.0).astype(BF16)


def segments(total_ref, left_ref, high_ref, rows_of, digits_ref, steps):
    for step in range(steps):
        left_ref[:, lane_slice(step, 512)] = low_table(across_lanes(digits_ref, 4 * step, 4))
        high_ref[lane_slice(step, 512), :] = lax.shift_right_arithmetic(
            down_rows(digits_ref, 4 * step, 4), 9
        )
    left = left_ref[:, 0 : steps * 512]
    for pair in range(HIGHS // 2):
        right = []
        for step in range(steps):
            high, rows = high_ref[lane_slice(step, 512), :], rows_of(step)
            right.append(
                jnp.concatenate([masked(rows, high, 2 * pair + side) for side in range(2)], axis=1)
            )
        total_ref[:, lane_slice(pair, 2 * LANES)] = dot(left, jnp.concatenate(right, axis=0))
    total_ref[:, HIGHS * LANES :] = dot(left, counting(high_ref[0 : steps * 512, :]))


def add_segments(total_ref, digits_ref, at, rows):
    left = low_table(across_lanes(digits_ref, at, 2))
    high = lax.shift_right_arithmetic(down_rows(digits_ref, at, 2), 9)
    for pair in range(HIGHS // 2):
        right = jnp.concatenate([masked(rows, high, 2 * pair + side) for side in range(2)], axis=1)
        total_ref[:, lane_slice(pair, 2 * LANES)] += dot(left, right)
    total_ref[:, HIGHS * LANES :] += dot(left, counting(high))


def lower_rows(slab_ref, step):
    return slab_ref[lane_slice(step, 32), 0:HALF, :].reshape(512, LANES).astype(F32)


def upper_rows(slab_ref, group):
    return slab_ref[pl.ds(group * 16, 16), HALF:CAP, :].reshape(256, LANES).astype(F32)


def mark_live(digits_ref, live_ref):
    for group in range(live_ref.shape[0]):
        most = jnp.max(digits_ref[16 + 2 * group : 18 + 2 * group, :])
        live_ref[group] = jnp.where(most > 0.0, 1, 0)


def parent_kernel(
    parent_ref, old_ref, assign_ref, total_hbm, back_ref, digits_ref, left_ref, high_ref, total_ref, sem
):
    count, slots = back_ref.shape
    unused, unused, slot = owner_slots(assign_ref[...], slots // CAP)
    same = jnp.where(iota((count, count), 0) == iota((count, count), 1), 1.0, 0.0).astype(BF16)
    back_ref[...] = dot_nt(same, slot_table(slot, slots)).astype(BF16)
    parent = parent_ref[...]
    digits_ref[0:32, :] = (lax.shift_right_logical(parent, 6) + 1).astype(F32)
    digits_ref[32:64, :] = ((parent & 63) + 1).astype(F32)
    segments(
        total_ref,
        left_ref,
        high_ref,
        lambda step: old_ref[lane_slice(step, 512), :].astype(F32),
        digits_ref,
        old_ref.shape[0] // 512,
    )
    store = pltpu.make_async_copy(total_ref, total_hbm, sem)
    store.start()
    store.wait()


def find_parents(digits_ref, parents_ref, table_ref, at, count):
    line = iota((LANES, LANES), 0)
    rows = [(digits_ref[pl.ds(at + n, 1), :], digits_ref[pl.ds(at + n + 32, 1), :]) for n in range(count)]
    left = [jnp.where(line == high.astype(I32) - 1, 1.0, 0.0).astype(BF16) for high, _ in rows]
    found = dot(table_ref[...], jnp.concatenate(left, axis=1))
    for n in range(count):
        chosen = jnp.where((line & 63) == rows[n][1].astype(I32) - 1, found[:, lane_slice(n)], 0.0)
        parents_ref[pl.ds(at + n, 1), :] = jnp.sum(chosen[0:64], axis=0, keepdims=True)
        parents_ref[pl.ds(at + n + 32, 1), :] = jnp.sum(chosen[64:128], axis=0, keepdims=True)


def upper_kernel(
    slab_ref, table_ref, top_ref, start_hbm, send_hbm, slab_hbm,
    digits_ref, parents_ref, total_ref, left_ref, high_ref, start_ref, send_ref, right_ref, tail_ref, live_ref,
    sems,
):
    load = pltpu.make_async_copy(start_hbm, start_ref, sems.at[0])
    load.start()
    keep = pltpu.make_async_copy(slab_ref, slab_hbm, sems.at[2 + HIGHS])
    keep.start()
    slot_digits(slab_ref, digits_ref)
    mark_live(digits_ref, live_ref)
    for step in range(4):
        find_parents(digits_ref, parents_ref, table_ref, 4 * step, 4)
    segments(total_ref, left_ref, high_ref, lambda step: lower_rows(slab_ref, step), parents_ref, 4)

    def more(group, carry):
        @pl.when(live_ref[group] > 0)
        def _():
            find_parents(digits_ref, parents_ref, table_ref, 16 + 2 * group, 2)
            add_segments(total_ref, parents_ref, 16 + 2 * group, upper_rows(slab_ref, group))

        return carry

    lax.fori_loop(0, slab_ref.shape[0] // 16, more, 0)
    load.wait()
    at = slice(HIGHS * LANES, (HIGHS + 1) * LANES)
    weights = total_ref[:, at] + start_ref[:, at]
    coarse = weights.astype(BF16).astype(F32)
    lane = iota((LOW, LANES), 1)
    split = jnp.where(lane < HIGHS, coarse, weights - coarse)
    diagonal = jnp.where(iota((16, LANES), 0) == iota((16, LANES), 1), 1.0, 0.0).astype(BF16)
    across = dot_nt(diagonal, split.astype(BF16))
    tops = []
    stores = [keep]
    for high in range(HIGHS):
        mass = (total_ref[:, lane_slice(high)] + start_ref[:, lane_slice(high)]).astype(BF16)
        for half in range(2):
            send_ref[2 * high + half, 0:32] = mass[half * 256 : (half + 1) * 256].reshape(32, 8, LANES)
        part = (pl.ds(2 * high, 2), pl.ds(0, 32))
        stores.append(pltpu.make_async_copy(send_ref.at[part], send_hbm.at[part], sems.at[1 + high]))
        stores[-1].start()
        right_ref[lane_slice(high, LOW), 0:LANES] = mass
        right_ref[lane_slice(high, LOW), LANES:] = jnp.where((lane & 7) == high, split, 0.0).astype(BF16)
        for part in range(4):
            hit = iota((256, LANES), 0) == top_ref[high * 4 + part : high * 4 + part + 1, :]
            tops.append(jnp.where(hit, 1.0, 0.0).astype(BF16))
    for half in range(2):
        for kind in range(2):
            lines = slice(kind * HIGHS, (kind + 1) * HIGHS)
            for side in range(2):
                tail_ref[pl.ds(side, HIGHS, 2), 2 * kind + half, :] = across[lines, lane_slice(2 * side + half)]
    tops = dot(jnp.concatenate(tops, axis=1), right_ref[...])
    owners = send_ref.shape[0]
    send_ref[:, 32:34] = tops[:, :LANES].astype(BF16).reshape(owners, 2, 8, LANES)
    first = jnp.where(iota((8, LANES), 1) < 16, 1.0, 0.0).astype(BF16)
    heavy = tops[:, LANES:]
    heavy_coarse = heavy.astype(BF16)
    heavy_fine = (heavy - heavy_coarse.astype(F32)).astype(BF16)
    top_weight = (dot_nt(first, heavy_coarse) + dot_nt(first, heavy_fine))[0:1]
    top_coarse = top_weight.astype(BF16).astype(F32)
    for kind, value in enumerate((top_coarse, top_weight - top_coarse)):
        for half in range(2):
            tail_ref[:, 4 + 2 * kind + half, :] = jnp.broadcast_to(value[:, lane_slice(half)], (owners, LANES))
    send_ref[:, 34:35] = tail_ref[...].astype(BF16)[:, None]
    part = (slice(None), pl.ds(32, 3))
    stores.append(pltpu.make_async_copy(send_ref.at[part], send_hbm.at[part], sems.at[1 + HIGHS]))
    stores[-1].start()
    for store in stores:
        store.wait()


def level_kernel(
    slab_hbm, old_hbm, level_hbm, residual_hbm,
    slab_ref, digits_ref, total_ref, table_ref, left_ref, high_ref, old_ref, level_ref, residual_ref, live_ref,
    load_sem, slab_sem, level_sems, low_sems, up_sems,
):
    fetch = pltpu.make_async_copy(slab_hbm, slab_ref, slab_sem)
    fetch.start()
    load = pltpu.make_async_copy(old_hbm, old_ref, load_sem)
    load.start()
    fetch.wait()
    slot_digits(slab_ref, digits_ref)
    mark_live(digits_ref, live_ref)
    segments(total_ref, left_ref, high_ref, lambda step: lower_rows(slab_ref, step), digits_ref, 4)
    groups = slab_ref.shape[0] // 16

    def more(group, carry):
        @pl.when(live_ref[group] > 0)
        def _():
            add_segments(total_ref, digits_ref, 16 + 2 * group, upper_rows(slab_ref, group))

        return carry

    lax.fori_loop(0, groups, more, 0)
    load.wait()
    inverse = 1.0 / (total_ref[:, HIGHS * LANES :] + 1.0)
    stores = []
    for high in range(HIGHS):
        lines = lane_slice(high, LOW)
        mass = total_ref[:, lane_slice(high)] + old_ref[lines, :].astype(F32)
        level = mass * jnp.broadcast_to(inverse[:, high : high + 1], mass.shape)
        level_ref[lines, :] = level
        table_ref[:, lane_slice(high)] = level.astype(BF16)
        stores.append(
            pltpu.make_async_copy(level_ref.at[lines], level_hbm.at[lines], level_sems.at[high])
        )
        stores[-1].start()

    def subtract(at, count, rows):
        label = down_rows(digits_ref, at, count)
        low = label & (LOW - 1)
        high = lax.shift_right_arithmetic(label, 9)
        lane = iota(label.shape, 1)
        left = jnp.concatenate(
            [
                jnp.where(low == lane + part * LANES, 1.0, 0.0).astype(BF16)
                for part in range(LOW // LANES)
            ],
            axis=1,
        )
        for pair in range(HIGHS // 2):
            found = dot(left, table_ref[:, lane_slice(pair, 2 * LANES)])
            for side in range(2):
                rows -= jnp.where(high == 2 * pair + side, found[:, lane_slice(side)], 0.0)
        return rows.astype(BF16)

    for step in range(4):
        sources = lane_slice(step, 32)
        residual_ref[sources, 0 : HALF // 8] = subtract(
            4 * step, 4, lower_rows(slab_ref, step)
        ).reshape(32, HALF // 8, 8, LANES)
        part = (sources, slice(0, HALF // 8))
        stores.append(
            pltpu.make_async_copy(residual_ref.at[part], residual_hbm.at[part], low_sems.at[step])
        )
        stores[-1].start()

    def upper_copy(group):
        part = (pl.ds(group * 16, 16), pl.ds(HALF // 8, HALF // 8))
        return pltpu.make_async_copy(residual_ref.at[part], residual_hbm.at[part], up_sems.at[group])

    def finish(group, carry):
        sources = pl.ds(group * 16, 16)
        @pl.when(live_ref[group] > 0)
        def _():
            residual_ref[sources, HALF // 8 : CAP // 8] = subtract(
                16 + 2 * group, 2, upper_rows(slab_ref, group)
            ).reshape(16, HALF // 8, 8, LANES)

        @pl.when(live_ref[group] == 0)
        def _():
            empty = slab_ref[sources, HALF:CAP, :]
            residual_ref[sources, HALF // 8 : CAP // 8] = empty.reshape(16, HALF // 8, 8, LANES)

        upper_copy(group).start()
        return carry

    lax.fori_loop(0, groups, finish, 0)
    for store in stores:
        store.wait()

    def settle(group, carry):
        upper_copy(group).wait()
        return carry

    lax.fori_loop(0, groups, settle, 0)


def finish_kernel(parts_ref, send_in, level_hbm, send_hbm, column_ref, top_ref, level_ref, sem, level_sem):
    total = parts_ref[0].astype(F32)
    for source in range(1, parts_ref.shape[0]):
        total += parts_ref[source].astype(F32)
    tail = total[272:280].T
    me = lax.axis_index("cent")
    owners = parts_ref.shape[0]
    chosen = jnp.where(me < 8, tail[:, 4:5] + tail[:, 6:7], tail[:, 5:6] + tail[:, 7:8])
    column_ref[...] = jnp.broadcast_to(chosen, (LANES, LANES))
    weight = column_ref[pl.ds(pl.multiple_of((me % 8) * TOP, TOP), TOP), :]
    top = (total[256:272] / weight).astype(BF16)
    for group in range(top_ref.shape[0] // owners):
        first = group % 2 * (TOP // 2)
        part = jnp.broadcast_to(top[first : first + TOP // 2][None, None], (owners, 1, TOP // 2, LANES))
        top_ref[group * owners : (group + 1) * owners] = part
    store = pltpu.make_async_copy(top_ref, send_hbm.at[:, pl.ds(CAP // 8, 1)], sem)
    store.start()
    for half in range(2):
        weight = tail[:, half : half + 1] + tail[:, half + 2 : half + 3]
        lines = slice(half * LANES, (half + 1) * LANES)
        level_ref[lines, :] = total[lines] / jnp.broadcast_to(weight, (LANES, LANES))
    level_store = pltpu.make_async_copy(level_ref, level_hbm, level_sem)
    level_store.start()
    store.wait()
    level_store.wait()


def unpack_kernel(back_ref, returned_ref, residual_hbm, level_hbm, residual_ref, level_ref, sems):
    groups, owners, rows, lanes = returned_ref.shape
    core = lax.axis_index("dp") % 2
    for group in range(groups):
        level_ref[:, 0, :, lane_slice(group)] = returned_ref[group, :, CAP:rows, :].astype(F32)
    stores = [pltpu.make_async_copy(level_ref, level_hbm.at[:, pl.ds(core, 1)], sems.at[groups // 2])]
    stores[-1].start()
    for pair in range(groups // 2):
        right = jnp.concatenate(
            [
                returned_ref[2 * pair + side, :, 0:CAP, :].reshape(owners * CAP, lanes)
                for side in range(2)
            ],
            axis=1,
        )
        at = lane_slice(pair, 2 * lanes)
        residual_ref[:, at] = dot(back_ref[...], right).astype(BF16)
        stores.append(pltpu.make_async_copy(residual_ref.at[:, at], residual_hbm.at[:, at], sems.at[pair]))
        stores[-1].start()
    for store in stores:
        store.wait()


def other_kernel(parts_ref, level_in, level_hbm, level_ref, sem):
    core = lax.axis_index("dp") % 2
    for group in range(parts_ref.shape[0]):
        level_ref[:, 0, :, lane_slice(group)] = parts_ref[group].astype(F32)
    store = pltpu.make_async_copy(level_ref, level_hbm.at[:, pl.ds(1 - core, 1)], sem)
    store.start()
    store.wait()


def shape(dims, kind):
    return jax.ShapeDtypeStruct(dims, kind)


def in_hbm(value):
    return pltpu.with_memory_space_constraint(value, pltpu.HBM)


def swap(value, axes):
    return lax.all_to_all(value, axes, split_axis=0, concat_axis=0, tiled=True)


def on_device(points, assign, parent_one, parent_two, old_level_one):
    count, width = points.shape
    owners = lax.axis_size("cent")
    groups = lax.axis_size("dp")
    devices = owners * groups
    block, lanes = old_level_one.shape
    slots = owners * CAP
    rows = CAP + EXTRA
    total_dims = (LOW, (HIGHS + 1) * LANES)
    answer_dims = (devices, (CAP + TOP // 2) // 8, 8, lanes)
    work = 2 * LOW * block * (HIGHS + 1) * LANES

    labels = assign.reshape(1, count)
    send = call(
        pack_kernel,
        pltpu.HBM((groups, owners, rows, lanes), BF16),
        [HBM, HBM],
        HBM,
        FULL,
        [
            pltpu.VMEM((1, count), I32),
            pltpu.VMEM((count, width), BF16),
            pltpu.VMEM((groups, owners, rows, lanes), BF16),
            pltpu.SemaphoreType.DMA((1 + groups // 2 + groups,)),
        ],
        flops=2 * slots * count * width,
    )(labels, points)
    slab = swap(send.reshape(devices, rows, lanes), BOTH)

    start, back = call(
        parent_kernel,
        (pltpu.HBM(total_dims, F32), shape((count, slots), BF16)),
        [VMEM, VMEM, VMEM],
        (HBM, VMEM),
        FULL,
        [
            pltpu.VMEM((64, LANES), F32),
            pltpu.VMEM((LOW, block), BF16),
            pltpu.VMEM((block, LANES), I32),
            pltpu.VMEM(total_dims, F32),
            pltpu.SemaphoreType.DMA(()),
        ],
        flops=work,
    )(parent_one.reshape(block // LANES, LANES), old_level_one, labels)
    grid = parent_one.reshape(64, 64).T
    table = jnp.concatenate([lax.shift_right_logical(grid, 6), grid & 63], axis=0) + 1
    table = jnp.pad(table, ((0, 0), (0, 64))).astype(BF16)

    share, slab_kept = call(
        upper_kernel,
        (pltpu.HBM((owners, 35, 8, lanes), BF16), pltpu.HBM((devices, rows, lanes), BF16)),
        [VMEM, VMEM, VMEM, HBM],
        (HBM, HBM),
        UPPER,
        [
            pltpu.VMEM((64, LANES), F32),
            pltpu.VMEM((64, LANES), F32),
            pltpu.VMEM(total_dims, F32),
            pltpu.VMEM((LOW, 2048), BF16),
            pltpu.VMEM((2048, LANES), I32),
            pltpu.VMEM(total_dims, F32),
            pltpu.VMEM((owners, 35, 8, lanes), BF16),
            pltpu.VMEM((HIGHS * LOW, 2 * LANES), BF16),
            pltpu.VMEM((owners, 8, lanes), F32),
            pltpu.SMEM((groups,), I32),
            pltpu.SemaphoreType.DMA((3 + HIGHS,)),
        ],
        flops=work,
    )(slab, table, parent_two.reshape(-1, LANES), in_hbm(start))
    shares = swap(share, "cent")

    level_one, answer = call(
        level_kernel,
        (shape((block, lanes), F32), shape(answer_dims, BF16)),
        [HBM, HBM],
        (HBM, HBM),
        LEVEL,
        [
            pltpu.VMEM((devices, rows, lanes), BF16),
            pltpu.VMEM((64, LANES), F32),
            pltpu.VMEM(total_dims, F32),
            pltpu.VMEM((LOW, HIGHS * LANES), BF16),
            pltpu.VMEM((LOW, 2048), BF16),
            pltpu.VMEM((2048, LANES), I32),
            pltpu.VMEM((block, lanes), BF16),
            pltpu.VMEM((block, lanes), F32),
            pltpu.VMEM((devices, CAP // 8, 8, lanes), BF16),
            pltpu.SMEM((groups,), I32),
            pltpu.SemaphoreType.DMA(()),
            pltpu.SemaphoreType.DMA(()),
            pltpu.SemaphoreType.DMA((HIGHS,)),
            pltpu.SemaphoreType.DMA((4,)),
            pltpu.SemaphoreType.DMA((groups,)),
        ],
        flops=2 * work,
    )(in_hbm(slab_kept), in_hbm(old_level_one))

    level_two, answer = call(
        finish_kernel,
        (shape((256, lanes), F32), shape(answer_dims, BF16)),
        [VMEM, HBM],
        (HBM, HBM),
        SMALL,
        [
            pltpu.VMEM((LANES, LANES), F32),
            pltpu.VMEM((devices, 1, TOP // 2, lanes), BF16),
            pltpu.VMEM((256, lanes), F32),
            pltpu.SemaphoreType.DMA(()),
            pltpu.SemaphoreType.DMA(()),
        ],
        alias={1: 1},
    )(shares.reshape(owners, -1, lanes), answer)
    returned = swap(answer, BOTH)
    half = returned[:, CAP // 8]
    half = lax.ppermute(half, "dp", [(group, group ^ 1) for group in range(groups)])
    top_dims = (owners, 2, TOP // 2, width)
    residual, level_three = call(
        unpack_kernel,
        (shape((count, width), BF16), shape(top_dims, F32)),
        [VMEM, VMEM],
        (HBM, HBM),
        SMALL,
        [
            pltpu.VMEM((count, width), BF16),
            pltpu.VMEM((owners, 1, TOP // 2, width), F32),
            pltpu.SemaphoreType.DMA((1 + groups // 2,)),
        ],
        flops=2 * slots * count * width,
    )(back, returned.reshape(groups, owners, CAP + TOP // 2, lanes))
    level_three = call(
        other_kernel,
        shape(top_dims, F32),
        [VMEM, HBM],
        HBM,
        SMALL,
        [pltpu.VMEM((owners, 1, TOP // 2, width), F32), pltpu.SemaphoreType.DMA(())],
        alias={1: 0},
    )(half.reshape(groups, owners, TOP // 2, lanes), level_three)
    level_three = level_three.reshape(owners * TOP, width)
    return (level_one, level_two, level_three, residual)


def solution(mesh):
    in_specs = (P(("dp", "cent"), None), P(("dp", "cent")), P("cent"), P(), P("cent", "dp"))
    out_specs = (P("cent", "dp"), P("cent", "dp"), P(), P(("dp", "cent"), None))
    return jax.shard_map(
        on_device, mesh=mesh, in_specs=in_specs, out_specs=out_specs, check_vma=False
    )
```

```python
import jax
import jax.numpy as jnp
from jax import lax
from jax.experimental import pallas as pl
from jax.experimental.pallas import tpu as pltpu
from jax.sharding import PartitionSpec as P

F32 = jnp.float32
BF16 = jnp.bfloat16
I32 = jnp.int32
LANES = 128
LOW = 512
HIGHS = 8
CAP = 32
HALF = 16
EXTRA = 8
TOP = 16
BOTH = ("dp", "cent")


def iota(shape, axis):
    return lax.broadcasted_iota(I32, shape, axis)


def dot(left, right):
    return jnp.dot(left, right, preferred_element_type=F32)


def dot_nt(left, right):
    return lax.dot_general(left, right, (((1,), (1,)), ((), ())), preferred_element_type=F32)


def lane_slice(at, width=LANES):
    return slice(at * width, (at + 1) * width)


HBM = pl.BlockSpec(memory_space=pltpu.HBM)
VMEM = pl.BlockSpec(memory_space=pltpu.VMEM)


FULL = 62_900_000
UPPER = 48_000_000
LEVEL = 48_000_000
SMALL = 16_000_000


def call(body, out_shape, ins, outs, vmem, scratch=(), flops=0, size=4 << 20, alias=None):
    return pl.pallas_call(
        body,
        out_shape=out_shape,
        in_specs=ins,
        out_specs=outs,
        scratch_shapes=list(scratch),
        input_output_aliases=alias or {},
        compiler_params=pltpu.CompilerParams(vmem_limit_bytes=vmem),
        cost_estimate=pl.CostEstimate(flops=flops, bytes_accessed=size, transcendentals=0),
    )


def owner_slots(label, owners):
    count = label.shape[1]
    owner = lax.shift_right_logical(label, 12)
    mine = jnp.where(iota((owners, count), 0) == owner, 1.0, 0.0)
    before = jnp.where(iota((count, count), 0) <= iota((count, count), 1), 1.0, 0.0).astype(BF16)
    place = jnp.sum(dot(mine.astype(BF16), before) * mine, axis=0, keepdims=True).astype(I32) - 1
    return mine, place, owner * CAP + place


def slot_table(slot, slots):
    return jnp.where(iota((slots, slot.shape[1]), 0) == slot, 1.0, 0.0).astype(BF16)


def pack_kernel(assign_hbm, points_hbm, send_hbm, assign_ref, points_ref, send_ref, sems):
    owners = send_ref.shape[1]
    parts = send_ref.shape[0]
    load = pltpu.make_async_copy(assign_hbm, assign_ref, sems.at[0])
    load.start()
    loads = []
    for pair in range(parts // 2):
        at = lane_slice(pair, 2 * LANES)
        loads.append(
            pltpu.make_async_copy(points_hbm.at[:, at], points_ref.at[:, at], sems.at[1 + pair])
        )
        loads[-1].start()
    load.wait()
    label = assign_ref[...]
    mine, place, slot = owner_slots(label, owners)
    local = label & 4095
    table = slot_table(slot, owners * CAP)
    shift = (lax.axis_index("cent") % 8) * HALF
    line = iota((LANES, points_ref.shape[0]), 0)
    row = iota((owners, EXTRA, LANES), 1)
    digits = [(lax.shift_right_logical(local, 6) + 1).astype(F32), ((local & 63) + 1).astype(F32)]
    digits = [(mine * digit).astype(BF16) for digit in digits]
    extra = jnp.zeros((owners, EXTRA, LANES), F32)
    for half in range(2):
        first = half * HALF
        inside = (place >= first) & (place < first + HALF)
        lane = jnp.where(inside, place - first + shift, -1)
        lane_table = jnp.where(line == lane, 1.0, 0.0).astype(BF16)
        for kind in range(2):
            found = dot_nt(digits[kind], lane_table)
            extra = jnp.where(row == 2 * kind + half, found[:, None, :], extra)
    extra = extra.astype(BF16)
    stores = []
    for part in range(parts):
        if part % 2 == 0:
            loads[part // 2].wait()
            both = dot(table, points_ref[:, lane_slice(part // 2, 2 * LANES)]).astype(BF16)
        rows = both[:, lane_slice(part % 2)]
        send_ref[part, :, 0:CAP, :] = rows.reshape(owners, CAP, LANES)
        send_ref[part, :, CAP : CAP + EXTRA, :] = extra
        stores.append(
            pltpu.make_async_copy(send_ref.at[part], send_hbm.at[part], sems.at[1 + parts // 2 + part])
        )
        stores[-1].start()
    for store in stores:
        store.wait()


def slot_digits(slab_ref, digits_ref):
    rows = slab_ref[:, CAP : CAP + EXTRA, :].astype(F32).reshape(-1, LANES).astype(BF16)
    shape = (64, rows.shape[0])
    column, line = iota(shape, 1), iota(shape, 0)
    pick = (lax.shift_right_logical(column, 6) == (line & 15)) & (
        (column & 7) == lax.shift_right_logical(line, 4)
    )
    digits_ref[...] = dot(jnp.where(pick, 1.0, 0.0).astype(BF16), rows)


def label_rows(digits_ref, at, count):
    return [
        (digits_ref[pl.ds(at + part, 1), :], digits_ref[pl.ds(at + part + 32, 1), :])
        for part in range(count)
    ]


def across_lanes(pairs):
    return [(high * 64.0 + low).astype(I32) - 65 for high, low in pairs]


def down_rows(pairs):
    same = iota((LANES, LANES), 0) == iota((LANES, LANES), 1)
    parts = [
        jnp.concatenate([jnp.where(same, high, 0.0), jnp.where(same, low, 0.0)], axis=1)
        for high, low in pairs
    ]
    left = jnp.concatenate(parts, axis=0).astype(BF16)
    right = jnp.where(iota((2 * LANES, LANES), 0) < LANES, 64.0, 1.0).astype(BF16)
    return dot(left, right).astype(I32) - 65


def low_table(labels):
    line = iota((LOW, LANES), 0)
    return jnp.concatenate(
        [jnp.where(line == (label & (LOW - 1)), 1.0, 0.0).astype(BF16) for label in labels], axis=1
    )


def masked(rows, high, which):
    return jnp.where(high == which, rows, 0.0).astype(BF16)


def counting(high):
    lane = iota(high.shape, 1)
    return jnp.where((high == (lane & 7)) & (lane < 16), 1.0, 0.0).astype(BF16)


def segments(total_ref, left_ref, high_ref, rows_of, digits_ref, steps):
    for step in range(steps):
        pairs = label_rows(digits_ref, 4 * step, 4)
        left_ref[:, lane_slice(step, 512)] = low_table(across_lanes(pairs))
        high_ref[lane_slice(step, 512), :] = lax.shift_right_arithmetic(down_rows(pairs), 9)
    left = left_ref[:, 0 : steps * 512]
    for pair in range(HIGHS // 2):
        right = []
        for step in range(steps):
            high, rows = high_ref[lane_slice(step, 512), :], rows_of(step)
            right.append(
                jnp.concatenate([masked(rows, high, 2 * pair + side) for side in range(2)], axis=1)
            )
        total_ref[:, lane_slice(pair, 2 * LANES)] = dot(left, jnp.concatenate(right, axis=0))
    total_ref[:, HIGHS * LANES :] = dot(left, counting(high_ref[0 : steps * 512, :]))


def add_segments(total_ref, pairs, rows):
    left = low_table(across_lanes(pairs))
    high = lax.shift_right_arithmetic(down_rows(pairs), 9)
    for pair in range(HIGHS // 2):
        right = jnp.concatenate([masked(rows, high, 2 * pair + side) for side in range(2)], axis=1)
        total_ref[:, lane_slice(pair, 2 * LANES)] += dot(left, right)
    total_ref[:, HIGHS * LANES :] += dot(left, counting(high))


def lower_rows(slab_ref, step):
    return slab_ref[lane_slice(step, 32), 0:HALF, :].reshape(512, LANES).astype(F32)


def upper_rows(slab_ref, group):
    return slab_ref[pl.ds(group * 16, 16), HALF:CAP, :].reshape(256, LANES).astype(F32)


def mark_live(digits_ref, live_ref, order_ref):
    groups = live_ref.shape[0]
    count, dead = 0, 0
    for group in range(groups):
        live = jnp.where(jnp.max(digits_ref[16 + 2 * group : 18 + 2 * group, :]) > 0.0, 1, 0)
        live_ref[group] = live
        order_ref[count] = group
        count = count + live
        dead = jnp.where(live > 0, dead, group)
    order_ref[count] = dead
    return lax.shift_right_logical(count + 1, 1)


def parent_kernel(
    parent_ref, old_ref, assign_ref, total_hbm, back_ref, digits_ref, left_ref, high_ref, total_ref, sem
):
    count, slots = back_ref.shape
    unused, unused, slot = owner_slots(assign_ref[...], slots // CAP)
    same = jnp.where(iota((count, count), 0) == iota((count, count), 1), 1.0, 0.0).astype(BF16)
    back_ref[...] = dot_nt(same, slot_table(slot, slots)).astype(BF16)
    parent = parent_ref[...]
    digits_ref[0:32, :] = (lax.shift_right_logical(parent, 6) + 1).astype(F32)
    digits_ref[32:64, :] = ((parent & 63) + 1).astype(F32)
    segments(
        total_ref,
        left_ref,
        high_ref,
        lambda step: old_ref[lane_slice(step, 512), :].astype(F32),
        digits_ref,
        old_ref.shape[0] // 512,
    )
    store = pltpu.make_async_copy(total_ref, total_hbm, sem)
    store.start()
    store.wait()


def find_parents(rows, table_ref):
    line = iota((LANES, LANES), 0)
    left = [jnp.where(line == high.astype(I32) - 1, 1.0, 0.0).astype(BF16) for high, _ in rows]
    found = dot(table_ref[...], jnp.concatenate(left, axis=1))
    parents = []
    for n, (_, low) in enumerate(rows):
        chosen = jnp.where((line & 63) == low.astype(I32) - 1, found[:, lane_slice(n)], 0.0)
        parents.append(
            (
                jnp.sum(chosen[0:64], axis=0, keepdims=True),
                jnp.sum(chosen[64:128], axis=0, keepdims=True),
            )
        )
    return parents


def two_groups(slab_ref, digits_ref, order_ref, pair):
    groups = [order_ref[2 * pair + side] for side in range(2)]
    labels = [row for group in groups for row in label_rows(digits_ref, 16 + 2 * group, 2)]
    return labels, jnp.concatenate([upper_rows(slab_ref, group) for group in groups], axis=0)


def upper_kernel(
    slab_ref, table_ref, top_ref, start_hbm, send_hbm, slab_hbm,
    digits_ref, parents_ref, total_ref, left_ref, high_ref, start_ref, send_ref, right_ref, tail_ref,
    live_ref, order_ref,
    sems,
):
    load = pltpu.make_async_copy(start_hbm, start_ref, sems.at[0])
    load.start()
    keep = pltpu.make_async_copy(slab_ref, slab_hbm, sems.at[2 + HIGHS])
    keep.start()
    slot_digits(slab_ref, digits_ref)
    pairs_live = mark_live(digits_ref, live_ref, order_ref)
    for step in range(4):
        for n, (high, low) in enumerate(find_parents(label_rows(digits_ref, 4 * step, 4), table_ref)):
            parents_ref[4 * step + n : 4 * step + n + 1, :] = high
            parents_ref[4 * step + n + 32 : 4 * step + n + 33, :] = low
    segments(total_ref, left_ref, high_ref, lambda step: lower_rows(slab_ref, step), parents_ref, 4)

    def more(pair, carry):
        labels, rows = two_groups(slab_ref, digits_ref, order_ref, pair)
        add_segments(total_ref, find_parents(labels, table_ref), rows)
        return carry

    lax.fori_loop(0, pairs_live, more, 0)
    load.wait()
    at = slice(HIGHS * LANES, (HIGHS + 1) * LANES)
    weights = total_ref[:, at] + start_ref[:, at]
    coarse = weights.astype(BF16).astype(F32)
    lane = iota((LOW, LANES), 1)
    split = jnp.where(lane < HIGHS, coarse, weights - coarse)
    diagonal = jnp.where(iota((16, LANES), 0) == iota((16, LANES), 1), 1.0, 0.0).astype(BF16)
    across = dot_nt(diagonal, split.astype(BF16))
    tops = []
    stores = [keep]
    for high in range(HIGHS):
        mass = (total_ref[:, lane_slice(high)] + start_ref[:, lane_slice(high)]).astype(BF16)
        for half in range(2):
            send_ref[2 * high + half, 0:32] = mass[half * 256 : (half + 1) * 256].reshape(32, 8, LANES)
        part = (pl.ds(2 * high, 2), pl.ds(0, 32))
        stores.append(pltpu.make_async_copy(send_ref.at[part], send_hbm.at[part], sems.at[1 + high]))
        stores[-1].start()
        right_ref[lane_slice(high, LOW), 0:LANES] = mass
        right_ref[lane_slice(high, LOW), LANES:] = jnp.where((lane & 7) == high, split, 0.0).astype(BF16)
        for part in range(4):
            hit = iota((256, LANES), 0) == top_ref[high * 4 + part : high * 4 + part + 1, :]
            tops.append(jnp.where(hit, 1.0, 0.0).astype(BF16))
    for half in range(2):
        for kind in range(2):
            lines = slice(kind * HIGHS, (kind + 1) * HIGHS)
            for side in range(2):
                tail_ref[pl.ds(side, HIGHS, 2), 2 * kind + half, :] = across[lines, lane_slice(2 * side + half)]
    tops = dot(jnp.concatenate(tops, axis=1), right_ref[...])
    owners = send_ref.shape[0]
    send_ref[:, 32:34] = tops[:, :LANES].astype(BF16).reshape(owners, 2, 8, LANES)
    first = jnp.where(iota((8, LANES), 1) < 16, 1.0, 0.0).astype(BF16)
    heavy = tops[:, LANES:]
    heavy_coarse = heavy.astype(BF16)
    heavy_fine = (heavy - heavy_coarse.astype(F32)).astype(BF16)
    top_weight = (dot_nt(first, heavy_coarse) + dot_nt(first, heavy_fine))[0:1]
    top_coarse = top_weight.astype(BF16).astype(F32)
    for kind, value in enumerate((top_coarse, top_weight - top_coarse)):
        for half in range(2):
            tail_ref[:, 4 + 2 * kind + half, :] = jnp.broadcast_to(value[:, lane_slice(half)], (owners, LANES))
    send_ref[:, 34:35] = tail_ref[...].astype(BF16)[:, None]
    part = (slice(None), pl.ds(32, 3))
    stores.append(pltpu.make_async_copy(send_ref.at[part], send_hbm.at[part], sems.at[1 + HIGHS]))
    stores[-1].start()
    for store in stores:
        store.wait()


def level_kernel(
    slab_hbm, old_hbm, level_hbm, residual_hbm,
    slab_ref, digits_ref, total_ref, table_ref, left_ref, high_ref, old_ref, level_ref, residual_ref, live_ref, order_ref,
    load_sem, slab_sem, level_sems, low_sems, up_sems,
):
    fetch = pltpu.make_async_copy(slab_hbm, slab_ref, slab_sem)
    fetch.start()
    load = pltpu.make_async_copy(old_hbm, old_ref, load_sem)
    load.start()
    fetch.wait()
    slot_digits(slab_ref, digits_ref)
    pairs_live = mark_live(digits_ref, live_ref, order_ref)
    segments(total_ref, left_ref, high_ref, lambda step: lower_rows(slab_ref, step), digits_ref, 4)
    groups = slab_ref.shape[0] // 16

    def more(pair, carry):
        labels, rows = two_groups(slab_ref, digits_ref, order_ref, pair)
        add_segments(total_ref, labels, rows)
        return carry

    lax.fori_loop(0, pairs_live, more, 0)
    load.wait()
    inverse = 1.0 / (total_ref[:, HIGHS * LANES :] + 1.0)
    stores = []
    for high in range(HIGHS):
        lines = lane_slice(high, LOW)
        mass = total_ref[:, lane_slice(high)] + old_ref[lines, :].astype(F32)
        level = mass * jnp.broadcast_to(inverse[:, high : high + 1], mass.shape)
        level_ref[lines, :] = level
        table_ref[:, lane_slice(high)] = level.astype(BF16)
        stores.append(
            pltpu.make_async_copy(level_ref.at[lines], level_hbm.at[lines], level_sems.at[high])
        )
        stores[-1].start()

    def subtract(at, count, rows):
        label = down_rows(label_rows(digits_ref, at, count))
        low = label & (LOW - 1)
        high = lax.shift_right_arithmetic(label, 9)
        lane = iota(label.shape, 1)
        left = jnp.concatenate(
            [
                jnp.where(low == lane + part * LANES, 1.0, 0.0).astype(BF16)
                for part in range(LOW // LANES)
            ],
            axis=1,
        )
        for pair in range(HIGHS // 2):
            found = dot(left, table_ref[:, lane_slice(pair, 2 * LANES)])
            for side in range(2):
                rows -= jnp.where(high == 2 * pair + side, found[:, lane_slice(side)], 0.0)
        return rows.astype(BF16)

    for step in range(4):
        sources = lane_slice(step, 32)
        residual_ref[sources, 0 : HALF // 8] = subtract(
            4 * step, 4, lower_rows(slab_ref, step)
        ).reshape(32, HALF // 8, 8, LANES)
        part = (sources, slice(0, HALF // 8))
        stores.append(
            pltpu.make_async_copy(residual_ref.at[part], residual_hbm.at[part], low_sems.at[step])
        )
        stores[-1].start()

    def upper_copy(group):
        part = (pl.ds(group * 16, 16), pl.ds(HALF // 8, HALF // 8))
        return pltpu.make_async_copy(residual_ref.at[part], residual_hbm.at[part], up_sems.at[group])

    def finish(group, carry):
        sources = pl.ds(group * 16, 16)
        @pl.when(live_ref[group] > 0)
        def _():
            residual_ref[sources, HALF // 8 : CAP // 8] = subtract(
                16 + 2 * group, 2, upper_rows(slab_ref, group)
            ).reshape(16, HALF // 8, 8, LANES)

        @pl.when(live_ref[group] == 0)
        def _():
            empty = slab_ref[sources, HALF:CAP, :]
            residual_ref[sources, HALF // 8 : CAP // 8] = empty.reshape(16, HALF // 8, 8, LANES)

        upper_copy(group).start()
        return carry

    lax.fori_loop(0, groups, finish, 0)
    for store in stores:
        store.wait()

    def settle(group, carry):
        upper_copy(group).wait()
        return carry

    lax.fori_loop(0, groups, settle, 0)


def finish_kernel(parts_ref, send_in, level_hbm, send_hbm, column_ref, top_ref, level_ref, sem, level_sem):
    total = parts_ref[0].astype(F32)
    for source in range(1, parts_ref.shape[0]):
        total += parts_ref[source].astype(F32)
    tail = total[272:280].T
    me = lax.axis_index("cent")
    owners = parts_ref.shape[0]
    chosen = jnp.where(me < 8, tail[:, 4:5] + tail[:, 6:7], tail[:, 5:6] + tail[:, 7:8])
    column_ref[...] = jnp.broadcast_to(chosen, (LANES, LANES))
    weight = column_ref[pl.ds(pl.multiple_of((me % 8) * TOP, TOP), TOP), :]
    top = (total[256:272] / weight).astype(BF16)
    for group in range(top_ref.shape[0] // owners):
        first = group % 2 * (TOP // 2)
        part = jnp.broadcast_to(top[first : first + TOP // 2][None, None], (owners, 1, TOP // 2, LANES))
        top_ref[group * owners : (group + 1) * owners] = part
    store = pltpu.make_async_copy(top_ref, send_hbm.at[:, pl.ds(CAP // 8, 1)], sem)
    store.start()
    for half in range(2):
        weight = tail[:, half : half + 1] + tail[:, half + 2 : half + 3]
        lines = slice(half * LANES, (half + 1) * LANES)
        level_ref[lines, :] = total[lines] / jnp.broadcast_to(weight, (LANES, LANES))
    level_store = pltpu.make_async_copy(level_ref, level_hbm, level_sem)
    level_store.start()
    store.wait()
    level_store.wait()


def unpack_kernel(back_ref, returned_ref, residual_hbm, level_hbm, residual_ref, level_ref, sems):
    groups, owners, rows, lanes = returned_ref.shape
    core = lax.axis_index("dp") % 2
    for group in range(groups):
        level_ref[:, 0, :, lane_slice(group)] = returned_ref[group, :, CAP:rows, :].astype(F32)
    stores = [pltpu.make_async_copy(level_ref, level_hbm.at[:, pl.ds(core, 1)], sems.at[groups // 2])]
    stores[-1].start()
    for pair in range(groups // 2):
        right = jnp.concatenate(
            [
                returned_ref[2 * pair + side, :, 0:CAP, :].reshape(owners * CAP, lanes)
                for side in range(2)
            ],
            axis=1,
        )
        at = lane_slice(pair, 2 * lanes)
        residual_ref[:, at] = dot(back_ref[...], right).astype(BF16)
        stores.append(pltpu.make_async_copy(residual_ref.at[:, at], residual_hbm.at[:, at], sems.at[pair]))
        stores[-1].start()
    for store in stores:
        store.wait()


def other_kernel(parts_ref, level_in, level_hbm, level_ref, sem):
    core = lax.axis_index("dp") % 2
    for group in range(parts_ref.shape[0]):
        level_ref[:, 0, :, lane_slice(group)] = parts_ref[group].astype(F32)
    store = pltpu.make_async_copy(level_ref, level_hbm.at[:, pl.ds(1 - core, 1)], sem)
    store.start()
    store.wait()


def shape(dims, kind):
    return jax.ShapeDtypeStruct(dims, kind)


def in_hbm(value):
    return pltpu.with_memory_space_constraint(value, pltpu.HBM)


def swap(value, axes):
    return lax.all_to_all(value, axes, split_axis=0, concat_axis=0, tiled=True)


def on_device(points, assign, parent_one, parent_two, old_level_one):
    count, width = points.shape
    owners = lax.axis_size("cent")
    groups = lax.axis_size("dp")
    devices = owners * groups
    block, lanes = old_level_one.shape
    slots = owners * CAP
    rows = CAP + EXTRA
    total_dims = (LOW, (HIGHS + 1) * LANES)
    answer_dims = (devices, (CAP + TOP // 2) // 8, 8, lanes)
    work = 2 * LOW * block * (HIGHS + 1) * LANES

    labels = assign.reshape(1, count)
    send = call(
        pack_kernel,
        pltpu.HBM((groups, owners, rows, lanes), BF16),
        [HBM, HBM],
        HBM,
        FULL,
        [
            pltpu.VMEM((1, count), I32),
            pltpu.VMEM((count, width), BF16),
            pltpu.VMEM((groups, owners, rows, lanes), BF16),
            pltpu.SemaphoreType.DMA((1 + groups // 2 + groups,)),
        ],
        flops=2 * slots * count * width,
    )(labels, points)
    slab = swap(send.reshape(devices, rows, lanes), BOTH)

    start, back = call(
        parent_kernel,
        (pltpu.HBM(total_dims, F32), shape((count, slots), BF16)),
        [VMEM, VMEM, VMEM],
        (HBM, VMEM),
        FULL,
        [
            pltpu.VMEM((64, LANES), F32),
            pltpu.VMEM((LOW, block), BF16),
            pltpu.VMEM((block, LANES), I32),
            pltpu.VMEM(total_dims, F32),
            pltpu.SemaphoreType.DMA(()),
        ],
        flops=work,
    )(parent_one.reshape(block // LANES, LANES), old_level_one, labels)
    grid = parent_one.reshape(64, 64).T
    table = jnp.concatenate([lax.shift_right_logical(grid, 6), grid & 63], axis=0) + 1
    table = jnp.pad(table, ((0, 0), (0, 64))).astype(BF16)

    share, slab_kept = call(
        upper_kernel,
        (pltpu.HBM((owners, 35, 8, lanes), BF16), pltpu.HBM((devices, rows, lanes), BF16)),
        [VMEM, VMEM, VMEM, HBM],
        (HBM, HBM),
        UPPER,
        [
            pltpu.VMEM((64, LANES), F32),
            pltpu.VMEM((64, LANES), F32),
            pltpu.VMEM(total_dims, F32),
            pltpu.VMEM((LOW, 2048), BF16),
            pltpu.VMEM((2048, LANES), I32),
            pltpu.VMEM(total_dims, F32),
            pltpu.VMEM((owners, 35, 8, lanes), BF16),
            pltpu.VMEM((HIGHS * LOW, 2 * LANES), BF16),
            pltpu.VMEM((owners, 8, lanes), F32),
            pltpu.SMEM((groups,), I32),
            pltpu.SMEM((groups + 1,), I32),
            pltpu.SemaphoreType.DMA((3 + HIGHS,)),
        ],
        flops=work,
    )(slab, table, parent_two.reshape(-1, LANES), in_hbm(start))
    shares = swap(share, "cent")

    level_one, answer = call(
        level_kernel,
        (shape((block, lanes), F32), shape(answer_dims, BF16)),
        [HBM, HBM],
        (HBM, HBM),
        LEVEL,
        [
            pltpu.VMEM((devices, rows, lanes), BF16),
            pltpu.VMEM((64, LANES), F32),
            pltpu.VMEM(total_dims, F32),
            pltpu.VMEM((LOW, HIGHS * LANES), BF16),
            pltpu.VMEM((LOW, 2048), BF16),
            pltpu.VMEM((2048, LANES), I32),
            pltpu.VMEM((block, lanes), BF16),
            pltpu.VMEM((block, lanes), F32),
            pltpu.VMEM((devices, CAP // 8, 8, lanes), BF16),
            pltpu.SMEM((groups,), I32),
            pltpu.SMEM((groups + 1,), I32),
            pltpu.SemaphoreType.DMA(()),
            pltpu.SemaphoreType.DMA(()),
            pltpu.SemaphoreType.DMA((HIGHS,)),
            pltpu.SemaphoreType.DMA((4,)),
            pltpu.SemaphoreType.DMA((groups,)),
        ],
        flops=2 * work,
    )(in_hbm(slab_kept), in_hbm(old_level_one))

    level_two, answer = call(
        finish_kernel,
        (shape((256, lanes), F32), shape(answer_dims, BF16)),
        [VMEM, HBM],
        (HBM, HBM),
        SMALL,
        [
            pltpu.VMEM((LANES, LANES), F32),
            pltpu.VMEM((devices, 1, TOP // 2, lanes), BF16),
            pltpu.VMEM((256, lanes), F32),
            pltpu.SemaphoreType.DMA(()),
            pltpu.SemaphoreType.DMA(()),
        ],
        alias={1: 1},
    )(shares.reshape(owners, -1, lanes), answer)
    returned = swap(answer, BOTH)
    half = returned[:, CAP // 8]
    half = lax.ppermute(half, "dp", [(group, group ^ 1) for group in range(groups)])
    top_dims = (owners, 2, TOP // 2, width)
    residual, level_three = call(
        unpack_kernel,
        (shape((count, width), BF16), shape(top_dims, F32)),
        [VMEM, VMEM],
        (HBM, HBM),
        SMALL,
        [
            pltpu.VMEM((count, width), BF16),
            pltpu.VMEM((owners, 1, TOP // 2, width), F32),
            pltpu.SemaphoreType.DMA((1 + groups // 2,)),
        ],
        flops=2 * slots * count * width,
    )(back, returned.reshape(groups, owners, CAP + TOP // 2, lanes))
    level_three = call(
        other_kernel,
        shape(top_dims, F32),
        [VMEM, HBM],
        HBM,
        SMALL,
        [pltpu.VMEM((owners, 1, TOP // 2, width), F32), pltpu.SemaphoreType.DMA(())],
        alias={1: 0},
    )(half.reshape(groups, owners, TOP // 2, lanes), level_three)
    level_three = level_three.reshape(owners * TOP, width)
    return (level_one, level_two, level_three, residual)


def solution(mesh):
    in_specs = (P(("dp", "cent"), None), P(("dp", "cent")), P("cent"), P(), P("cent", "dp"))
    out_specs = (P("cent", "dp"), P("cent", "dp"), P(), P(("dp", "cent"), None))
    return jax.shard_map(
        on_device, mesh=mesh, in_specs=in_specs, out_specs=out_specs, check_vma=False
    )
```
